512 devices in a mesh: gx: 16 (over z, y_lo), gy: 32 (over x, y_hi, core).
Axes of the slice: x: 4, y: 8 (y_hi: 4, y_lo: 2; y = y_hi * 2 + y_lo), z: 8, core: 2. Of those that a mesh axis runs over, the one named last changes fastest.
Arguments:
- forcing_late: bfloat16 [4, 137, 512, 512], P(None, None, 'gx', 'gy'), may hold values from -6 to 6
- forcing_early: bfloat16 [4, 137, 512, 512], P(None, None, 'gx', 'gy'), may hold values from -6 to 6
- stencil_coef: float32 [4, 512, 512], P(None, 'gx', 'gy'), may hold values from 0.05 to 0.25
- jacobian: bfloat16 [16, 512, 4, 137, 137], P('gx', 'gy'), may hold values from -0.5 to 0.5
- cloudy_cols: int32 [16, 32, 48], P('gx', 'gy'), may hold values from 0 to 511, as said below
- cloudy_count: int32 [16, 32], P('gx', 'gy'), may hold values from 0 to 48, as said below
- owner_rank: int32 [16, 32, 48], P('gx', 'gy'), may hold values from 0 to 31, as said below
- owner_slot: int32 [16, 32, 48], P('gx', 'gy'), may hold values from 0 to 15, as said below
Outputs:
- adjoint_state: float32 [4, 137, 512, 512], P(None, None, 'gx', 'gy')
The draws below stay inside these ranges and needn't reach their ends.
Inputs may be any that keep to these rules, and one draw needn't show every extreme that they name: `cloudy_count`: entries beyond a domain's count are to be ignored; the cloudy_cols of a domain are all distinct. Over one longitude row of domains the counts sum to 16 * 32, and one domain has exactly 48. `cloudy_cols`: distinct within a domain. `owner_rank`: within one longitude row of domains each owner receives exactly 16 live cloudy columns; one domain sends at most 2 of them to one owner, and some domain sends exactly 2 to some owner in every row. `owner_slot`: within one longitude row of domains the live columns that go to one owner take its slots 0 to 15, each once.
All inputs are finite; a program needn't handle non-finite values.
Results may differ from the reference program's by a relative error of at most 0.0008.
Values may be sent and summed in bfloat16 or wider, within the bound.
No kernel may reach another device: no remote copies, remote signals or barrier semaphores. Data moves between devices by JAX's collectives and lax.ppermute only.
A program may use at most 64 MiB of HBM per device.

```python
import math
import jax
import jax.numpy as jnp
from jax import lax

FIELDS = 4
LEVELS = 137
CX = 32
CY = 16
OWN = 16
SRC_CAP = 48
SLOTS = 512
NX = 512
NY = 512
N_GX = 16
N_GY = 32


def routing(key):
    heavy_key = jax.random.fold_in(key, 101)
    weight_key = jax.random.fold_in(key, 102)
    heavy = jax.random.randint(heavy_key, (N_GX, 1), 0, N_GY).astype(jnp.int32)
    weights = jax.random.randint(weight_key, (N_GX, N_GY), 2, 5).astype(jnp.int32)
    domains = jnp.arange(N_GY, dtype=jnp.int32)[None, :]
    weights = jnp.where(domains == heavy, 0, weights)
    running = jnp.cumsum(weights, axis=1).astype(jnp.int32)
    remaining = N_GY * OWN - SRC_CAP
    bounds = remaining * running // running[:, -1:]
    previous = jnp.concatenate([jnp.zeros((N_GX, 1), jnp.int32), bounds[:, :-1]], axis=1)
    loads = (bounds - previous + jnp.where(domains == heavy, SRC_CAP, 0)).astype(jnp.int32)
    starts = (jnp.cumsum(loads, axis=1) - loads).astype(jnp.int32)
    entries = jnp.arange(SRC_CAP, dtype=jnp.int32)[None, None, :]
    positions = starts[:, :, None] + entries
    usable = entries < loads[:, :, None]
    owners = jnp.where(usable, positions % N_GY, 0).astype(jnp.int32)
    slots = jnp.where(usable, positions // N_GY, 0).astype(jnp.int32)
    return (loads, owners, slots)


def draw_cloudy_count(key, part):
    loads, owners, slots = routing(key)
    return loads


def draw_owner_rank(key, part):
    loads, owners, slots = routing(key)
    return owners


def draw_owner_slot(key, part):
    loads, owners, slots = routing(key)
    return slots


def draw_cloudy_cols(key, part):
    key = jax.random.fold_in(key, 4)
    domain_keys = jax.random.split(key, N_GX * N_GY)
    chosen = jax.vmap(lambda single: jax.random.permutation(single, CX * CY)[:SRC_CAP])(domain_keys)
    return chosen.reshape(N_GX, N_GY, SRC_CAP).astype(jnp.int32)


def levels(rng, shape, cuts, low, top_value):
    gain, own = 1.0, jax.random.fold_in(rng, 6)
    for dim, blocks in cuts:
        steps = jnp.exp(jax.random.uniform(jax.random.fold_in(own, dim), (blocks,), jnp.float32, low / len(cuts), top_value / len(cuts)))
        gain = gain * jnp.repeat(steps, shape[dim] // blocks).reshape([-1 if axis == dim else 1 for axis in range(len(shape))])
    return gain


def bell_draw(key, dims, scale, reach, shards=(), held_as=jnp.bfloat16):
    drawn = scale * jax.random.normal(key, dims, jnp.float32)
    if shards:
        drawn = drawn * levels(key, dims, shards, -0.22, 0.18)
    return jnp.clip(drawn, -reach, reach).astype(held_as)


def setup_inputs(seed: int = 0) -> dict:
    arg_keys = jax.random.split(jax.random.key(seed), 9)
    return {
        "forcing_late": bell_draw(arg_keys[0], (FIELDS, LEVELS, NX, NY), 1.0, 6.0, ((2, 16), (3, 32))),
        "forcing_early": bell_draw(arg_keys[1], (FIELDS, LEVELS, NX, NY), 1.0, 6.0, ((2, 16), (3, 32))),
        "stencil_coef": jnp.clip(jnp.exp(math.log(0.25) - 1.609438 * jax.random.uniform(arg_keys[2], (4, NX, NY), jnp.float32) ** levels(arg_keys[2], (4, NX, NY), ((1, 16), (2, 32)), -0.2, 0.2)), 0.05, 0.25),
        "jacobian": bell_draw(arg_keys[3], (N_GX, SLOTS, FIELDS, LEVELS, LEVELS), LEVELS ** -0.5, 0.5, ((0, 16), (1, 32))),
        "cloudy_cols": draw_cloudy_cols(jax.random.fold_in(arg_keys[8], 71), 0),
        "cloudy_count": draw_cloudy_count(jax.random.fold_in(arg_keys[8], 71), 0),
        "owner_rank": draw_owner_rank(jax.random.fold_in(arg_keys[8], 71), 0),
        "owner_slot": draw_owner_slot(jax.random.fold_in(arg_keys[8], 71), 0),
    }


def stencil(field, stencil_coef):
    before_lon = jnp.roll(field, 1, axis=2)
    after_lon = jnp.roll(field, -1, axis=2)
    padded = jnp.pad(field, ((0, 0), (0, 0), (0, 0), (1, 1)))
    return (field + stencil_coef[0] * before_lon + stencil_coef[1] * after_lon
            + stencil_coef[2] * padded[:, :, :, :-2] + stencil_coef[3] * padded[:, :, :, 2:])


def physics(field, jacobian, cloudy_cols, cloudy_count, owner_rank, owner_slot):
    capacity = cloudy_cols.shape[2]
    lon_index = jnp.arange(N_GX, dtype=jnp.int32)[:, None, None]
    lat_index = jnp.arange(N_GY, dtype=jnp.int32)[None, :, None]
    rows_lon = (lon_index * CX + cloudy_cols // CY).astype(jnp.int32)
    rows_lat = (lat_index * CY + cloudy_cols % CY).astype(jnp.int32)
    usable = jnp.arange(capacity, dtype=jnp.int32)[None, None, :] < cloudy_count[:, :, None]
    picked = field[:, :, rows_lon, rows_lat].astype(jnp.bfloat16)
    target = jnp.where(usable, owner_rank * OWN + owner_slot, OWN * N_GY).astype(jnp.int32)
    lon_full = jnp.broadcast_to(lon_index, target.shape).astype(jnp.int32)
    placed = jnp.zeros((N_GX, OWN * N_GY, field.shape[0], field.shape[1]), jnp.bfloat16)
    placed = placed.at[lon_full, target].set(jnp.transpose(picked, (2, 3, 4, 0, 1)), mode="drop")

    def apply_row(pieces):
        matrices, values = pieces
        return jnp.einsum("sfij,sfi->sfj", matrices.astype(jnp.float32), values.astype(jnp.float32),
                          precision=lax.Precision.HIGHEST)

    increments = lax.map(apply_row, (jacobian, placed))
    fetched = increments[lon_full, jnp.minimum(target, OWN * N_GY - 1)]
    fetched = jnp.where(usable[:, :, :, None, None], fetched, 0.0)
    return field.at[:, :, rows_lon, rows_lat].add(jnp.transpose(fetched, (3, 4, 0, 1, 2)))


def reference(forcing_late, forcing_early, stencil_coef, jacobian, cloudy_cols, cloudy_count, owner_rank, owner_slot):
    adjoint = forcing_late.astype(jnp.float32)
    adjoint = stencil(physics(adjoint, jacobian, cloudy_cols, cloudy_count, owner_rank, owner_slot), stencil_coef)
    adjoint = adjoint + forcing_early.astype(jnp.float32)
    adjoint = stencil(physics(adjoint, jacobian, cloudy_cols, cloudy_count, owner_rank, owner_slot), stencil_coef)
    return adjoint
```

```python
import functools

import jax
import jax.numpy as jnp
from jax import lax
from jax.experimental import pallas as pl
from jax.experimental.pallas import tpu as pltpu
from jax.sharding import PartitionSpec as P

BF16 = jnp.bfloat16
F32 = jnp.float32
VMEM = pltpu.VMEM
SMEM = pltpu.SMEM
PAIR = 2


def call(kernel, out_shape, in_spaces, out_spaces, scratch=(), flops=1000, bytes_accessed=1000000):
    return pl.pallas_call(
        kernel,
        out_shape=out_shape,
        in_specs=[pl.BlockSpec(memory_space=space) for space in in_spaces],
        out_specs=[pl.BlockSpec(memory_space=space) for space in out_spaces],
        scratch_shapes=scratch,
        compiler_params=pltpu.CompilerParams(vmem_limit_bytes=40 * 1024 * 1024),
        cost_estimate=pl.CostEstimate(flops=flops, bytes_accessed=bytes_accessed, transcendentals=0),
    )


def entry_loop(count_ref, body):
    def step(e, carry):
        body(e)
        return carry

    lax.fori_loop(0, count_ref[0], step, 0)


def pack_first(cols, count, owner, slot, late, outbox, target, wide, rows, used):
    fields, span_lon, span_lat, levels = late.shape
    for f in range(fields):
        wide[f, :, :, :levels] = late[f].astype(F32)
    lane = lax.broadcasted_iota(jnp.int32, (1, levels + 1), 1)
    rows[...] = jnp.zeros(rows.shape, F32)
    for o in range(rows.shape[0] // (PAIR * fields)):
        used[o] = 0
    for e in range(target.shape[0]):
        target[e] = 0

    def body(e):
        o = owner[e]
        rank = used[o]
        used[o] = rank + 1
        t = o * PAIR + rank
        target[e] = t
        lon = cols[e] // span_lat
        lat = cols[e] % span_lat
        code = slot[e] * fields
        for f in range(fields):
            column = wide[f, lon, pl.ds(lat, 1), :]
            rows[pl.ds(t * fields + f, 1), :] = jnp.where(lane == levels, (code + f + 1).astype(F32), column)

    entry_loop(count, body)
    outbox[...] = rows[...].astype(BF16)


def place_kernel(received, placed, chosen_out):
    levels = placed.shape[1]
    values = received[...].astype(F32)
    codes = values[:, levels:]
    wanted = (lax.broadcasted_iota(jnp.int32, (values.shape[0], placed.shape[0]), 1) + 1).astype(F32)
    chosen = (codes == wanted).astype(BF16)
    chosen_out[...] = chosen
    placed[...] = lax.dot_general(
        chosen, values[:, :levels].astype(BF16), (((0,), (0,)), ((), ())), preferred_element_type=F32
    ).astype(BF16)


def place_again_kernel(received, chosen, placed):
    placed[...] = lax.dot_general(
        chosen[...], received[...], (((0,), (0,)), ((), ())), preferred_element_type=F32
    ).astype(BF16)


def split_dot(chosen, value):
    high = value.astype(BF16)
    rest = value - high.astype(F32)
    middle = rest.astype(BF16)
    low = (rest - middle.astype(F32)).astype(BF16)
    dot = functools.partial(jnp.dot, preferred_element_type=F32)
    return dot(chosen, high) + dot(chosen, middle) + dot(chosen, low)


def answer_kernel(result, chosen, answer):
    answer[...] = split_dot(chosen[...], result[...])


def add_increments(cols, count, target, returned, field):
    fields, span_lon, span_lat, levels = field.shape

    def body(e):
        t = target[e]
        lon = cols[e] // span_lat
        lat = cols[e] % span_lat
        for f in range(fields):
            here = (f, lon, pl.ds(lat, 1), slice(None))
            field[here] = field[here] + returned[pl.ds(t * fields + f, 1), :]

    entry_loop(count, body)


def store_edges(field, lon_low, lon_high, lat_low, lat_high):
    fields, span_lon, span_lat, levels = field.shape
    for f in range(fields):
        lon_low[f] = field[f, 0].astype(BF16)
        lon_high[f] = field[f, span_lon - 1].astype(BF16)
        lat_low[f] = jnp.concatenate([field[f, p, :1, :] for p in range(span_lon)], axis=0).astype(BF16)
        lat_high[f] = jnp.concatenate(
            [field[f, p, span_lat - 1 :, :] for p in range(span_lon)], axis=0
        ).astype(BF16)


def add_first(cols, count, target, late, returned, field, lon_low, lon_high, lat_low, lat_high):
    for f in range(field.shape[0]):
        field[f] = late[f].astype(F32)
    add_increments(cols, count, target, returned, field)
    store_edges(field, lon_low, lon_high, lat_low, lat_high)


def add_second(cols, count, target, base, returned, field, lon_low, lon_high, lat_low, lat_high):
    field[...] = base[...]
    add_increments(cols, count, target, returned, field)
    store_edges(field, lon_low, lon_high, lat_low, lat_high)


def stencil_into(field, coef, from_before, from_after, from_low, from_high, extra, out):
    fields, span_lon, span_lat, levels = field.shape
    row = lax.broadcasted_iota(jnp.int32, (span_lat, levels), 0)
    low_rows = [from_low[f].astype(F32) for f in range(fields)]
    high_rows = [from_high[f].astype(F32) for f in range(fields)]
    for p in range(span_lon):
        weight = [jnp.broadcast_to(coef[k, :, p : p + 1], (span_lat, levels)) for k in range(4)]
        for f in range(fields):
            here = field[f, p]
            before = field[f, p - 1] if p > 0 else from_before[f].astype(F32)
            after = field[f, p + 1] if p < span_lon - 1 else from_after[f].astype(F32)
            low = jnp.where(row == 0, low_rows[f][p : p + 1], pltpu.roll(here, 1, 0))
            high = jnp.where(row == span_lat - 1, high_rows[f][p : p + 1], pltpu.roll(here, span_lat - 1, 0))
            total = here + weight[0] * before + weight[1] * after + weight[2] * low + weight[3] * high
            if extra is not None:
                total = total + extra[f, p].astype(F32)
            out[f, p] = total


def step_first(cols, count, target, field, coef, from_before, from_after, from_low, from_high, early, out, outbox, rows):
    fields, span_lon, span_lat, levels = field.shape
    stencil_into(field, coef, from_before, from_after, from_low, from_high, early, out)
    rows[...] = jnp.zeros(rows.shape, F32)

    def body(e):
        t = target[e]
        lon = cols[e] // span_lat
        lat = cols[e] % span_lat
        for f in range(fields):
            rows[pl.ds(t * fields + f, 1), :] = out[f, lon, pl.ds(lat, 1), :]

    entry_loop(count, body)
    outbox[...] = rows[...].astype(BF16)


def step_second(field, coef, from_before, from_after, from_low, from_high, out):
    stencil_into(field, coef, from_before, from_after, from_low, from_high, None, out)


def exchange(rows, groups):
    width = rows.shape[1]
    moved = lax.all_to_all(
        rows.reshape(groups, rows.shape[0] // groups, width), "gy", split_axis=0, concat_axis=0, tiled=True
    )
    return moved.reshape(rows.shape)


def halos(lon_low, lon_high, lat_low, lat_high):
    lon = lax.axis_size("gx")
    lat = lax.axis_size("gy")
    up = [(i, (i + 1) % lon) for i in range(lon)]
    down = [(target, source) for source, target in up]
    north = [(i, i + 1) for i in range(lat - 1)]
    south = [(target, source) for source, target in north]
    from_before = lax.ppermute(lon_high, "gx", up)
    from_after = lax.ppermute(lon_low, "gx", down)
    from_low = lax.ppermute(lat_high, "gy", north)
    from_high = lax.ppermute(lat_low, "gy", south)
    return from_before, from_after, from_low, from_high


def on_device(late, early, stencil_coef, jacobian, cloudy_cols, cloudy_count, owner_rank, owner_slot):
    fields, levels, span_lon, span_lat = late.shape
    groups = lax.axis_size("gy")
    own_slots = jacobian.shape[1]
    capacity = cloudy_cols.shape[2]
    late = late.transpose(0, 2, 3, 1)
    early = early.transpose(0, 2, 3, 1)
    coef = stencil_coef.transpose(0, 2, 1)
    cols = cloudy_cols.reshape(capacity)
    count = cloudy_count.reshape(1)
    owner = owner_rank.reshape(capacity)
    slot = owner_slot.reshape(capacity)
    matrices = jacobian[0]
    shape = jax.ShapeDtypeStruct
    inbox_rows = groups * PAIR * fields
    grid = (fields, span_lon, span_lat, levels)

    outbox, target = call(
        pack_first,
        [shape((inbox_rows, levels + 1), BF16), shape((capacity,), jnp.int32)],
        [SMEM] * 4 + [VMEM],
        [VMEM, SMEM],
        [VMEM(grid[:3] + (levels + 1,), F32), VMEM((inbox_rows, levels + 1), F32), SMEM((groups,), jnp.int32)],
    )(cols, count, owner, slot, late)
    received = exchange(outbox, groups)
    placed, chosen = call(
        place_kernel,
        [shape((own_slots * fields, levels), BF16), shape((inbox_rows, own_slots * fields), BF16)],
        [VMEM],
        [VMEM] * 2,
    )(received)

    def apply(placed):
        result = jnp.einsum(
            "sfij,sfi->sfj",
            matrices,
            placed.reshape(own_slots, fields, levels),
            preferred_element_type=F32,
        ).reshape(own_slots * fields, levels)
        (answer,) = call(answer_kernel, [shape((inbox_rows, levels), F32)], [VMEM] * 2, [VMEM])(result, chosen)
        return exchange(answer, groups)

    edge_shapes = [shape((fields, span_lat, levels), BF16)] * 2 + [shape((fields, span_lon, levels), BF16)] * 2
    returned = apply(placed)
    field, *edges = call(add_first, [shape(grid, F32)] + edge_shapes, [SMEM] * 3 + [VMEM] * 2, [VMEM] * 5)(
        cols, count, target, late, returned
    )
    adjoint, outbox = call(
        step_first,
        [shape(grid, F32), shape((inbox_rows, levels), BF16)],
        [SMEM] * 3 + [VMEM] * 7,
        [VMEM] * 2,
        [VMEM((inbox_rows, levels), F32)],
    )(cols, count, target, field, coef, *halos(*edges), early)
    received = exchange(outbox, groups)
    (placed,) = call(place_again_kernel, [shape((own_slots * fields, levels), BF16)], [VMEM] * 2, [VMEM])(
        received, chosen
    )
    returned = apply(placed)
    field, *edges = call(add_second, [shape(grid, F32)] + edge_shapes, [SMEM] * 3 + [VMEM] * 2, [VMEM] * 5)(
        cols, count, target, adjoint, returned
    )
    (final,) = call(step_second, [shape(grid, F32)], [VMEM] * 6, [VMEM])(field, coef, *halos(*edges))
    return final.transpose(0, 3, 1, 2)


def solution(mesh):
    return jax.shard_map(
        on_device,
        mesh=mesh,
        in_specs=(
            P(None, None, "gx", "gy"),
            P(None, None, "gx", "gy"),
            P(None, "gx", "gy"),
            P("gx", "gy", None, None, None),
            P("gx", "gy", None),
            P("gx", "gy"),
            P("gx", "gy", None),
            P("gx", "gy", None),
        ),
        out_specs=P(None, None, "gx", "gy"),
        check_vma=False,
    )
```

```python
import functools

import jax
import jax.numpy as jnp
from jax import lax
from jax.experimental import pallas as pl
from jax.experimental.pallas import tpu as pltpu
from jax.sharding import PartitionSpec as P

BF16 = jnp.bfloat16
F32 = jnp.float32
VMEM = pltpu.VMEM
SMEM = pltpu.SMEM
HBM = pltpu.HBM
PAIR = 2
LANES = 128


def call(kernel, out_shape, in_spaces, out_spaces, scratch=(), aliases=None, flops=1000, touched=1000000, vmem=40):
    return pl.pallas_call(
        kernel,
        out_shape=out_shape,
        in_specs=[pl.BlockSpec(memory_space=space) for space in in_spaces],
        out_specs=[pl.BlockSpec(memory_space=space) for space in out_spaces],
        scratch_shapes=scratch,
        input_output_aliases=aliases or {},
        compiler_params=pltpu.CompilerParams(vmem_limit_bytes=vmem * 1024 * 1024),
        cost_estimate=pl.CostEstimate(flops=flops, bytes_accessed=touched, transcendentals=0),
    )


def entry_loop(count, body):
    def step(e, carry):
        body(e)
        return carry

    lax.fori_loop(0, count, step, 0)


def unpack_field(packed, field, f):
    field[f, 0] = packed[f, :, :LANES].astype(F32)
    field[f, 1, :, : packed.shape[2] - LANES] = packed[f, :, LANES:].astype(F32)


def pack_first(
    cols_hbm, count_hbm, owner_hbm, slot_hbm, late_hbm, outbox, plan, cols, count, owner, slot, late, field, rows, used, sems
):
    fields = field.shape[0]
    levels = late.shape[2]
    capacity = cols.shape[2]
    owners = used.shape[0]
    tail = levels - LANES
    end = lax.broadcasted_iota(jnp.int32, (1, LANES), 1)
    small = [(cols_hbm, cols), (count_hbm, count), (owner_hbm, owner), (slot_hbm, slot)]
    copies = [pltpu.make_async_copy(source, target, sems.at[i]) for i, (source, target) in enumerate(small)]
    copies += [pltpu.make_async_copy(late_hbm.at[f], late.at[f], sems.at[len(small) + f]) for f in range(fields)]
    for copy in copies:
        copy.start()
    rows[...] = jnp.zeros(rows.shape, F32)
    for o in range(owners):
        used[o] = 0
    for e in range(2 * capacity + 1):
        plan[e] = 0
    for f in range(fields):
        copies[len(small) + f].wait()
        unpack_field(late, field, f)
    for copy in copies[: len(small)]:
        copy.wait()
    live = count[0, 0]
    plan[0] = live

    def body(e):
        o = owner[0, 0, e]
        column = cols[0, 0, e]
        rank = used[o]
        used[o] = rank + 1
        plan[1 + e] = column
        plan[1 + capacity + e] = rank * (fields * owners) + o
        first = (o * PAIR + rank) * fields
        code = slot[0, 0, e] * fields
        for f in range(fields):
            mark = (code + (f + 1)).astype(F32)
            rows[0, pl.ds(first + f, 1), :] = field[f, 0, pl.ds(column, 1), :]
            rows[1, pl.ds(first + f, 1), :] = jnp.where(end == tail, mark, field[f, 1, pl.ds(column, 1), :])

    entry_loop(live, body)
    outbox[:, :LANES] = rows[0].astype(BF16)
    outbox[:, LANES:] = rows[1, :, : tail + 1].astype(BF16)


def place_first(received, placed, chosen_out, answering, wide):
    levels = placed.shape[1]
    values = received[...].astype(F32)
    codes = values[:, levels:]
    wanted = (lax.broadcasted_iota(jnp.int32, (values.shape[0], placed.shape[0]), 1) + 1).astype(F32)
    wide[...] = (codes == wanted).astype(F32)
    chosen = wide[...].astype(BF16)
    chosen_out[...] = chosen
    placed[...] = lax.dot_general(
        chosen, values[:, :levels].astype(BF16), (((0,), (0,)), ((), ())), preferred_element_type=F32
    ).astype(BF16)
    per_owner = 8
    owners = values.shape[0] // per_owner
    for r in range(per_owner):
        answering[r * owners : (r + 1) * owners, :] = wide[pl.ds(r, owners, stride=per_owner), :].astype(BF16)


def place_second(received, chosen, placed):
    placed[...] = lax.dot_general(
        chosen[...], received[...], (((0,), (0,)), ((), ())), preferred_element_type=F32
    ).astype(BF16)


def split_dot(chosen, value):
    high = value.astype(BF16)
    rest = value - high.astype(F32)
    middle = rest.astype(BF16)
    low = (rest - middle.astype(F32)).astype(BF16)
    dot = functools.partial(jnp.dot, preferred_element_type=F32)
    return dot(chosen, high) + dot(chosen, middle) + dot(chosen, low)


def answer_kernel(result, answering, answer, wide):
    owners = answer.shape[0]
    levels = result.shape[1]
    tail = levels - LANES
    per_owner = answering.shape[0] // owners
    wide[...] = jnp.zeros(wide.shape, F32)
    wide[:, :levels] = result[...]
    rows = split_dot(answering[...], wide[...])
    tails = jnp.zeros((owners, LANES), F32)
    for r in range(per_owner):
        block = rows[r * owners : (r + 1) * owners]
        answer[:, r * LANES : (r + 1) * LANES] = block[:, :LANES]
        end = block[:, LANES:]
        tails = tails + (pltpu.roll(end, tail * r, 1) if r else end)
    answer[:, per_owner * LANES :] = tails


def add_first(plan, returned, late, field, *rest, levels):
    for f in range(field.shape[0]):
        unpack_field(late, field, f)
    add_increments(plan, returned, field, field, *rest, levels=levels)


def add_increments(plan, returned, base, field, lon_low, lon_high, lat_low, lat_high, inbox, *, levels):
    fields, halves, columns_all, lanes = field.shape
    owners = returned.shape[0]
    per_owner = inbox.shape[1] // owners
    capacity = (plan.shape[0] - 1) // 2
    tail = levels - LANES
    tails = returned[:, per_owner * LANES :]
    for r in range(per_owner):
        inbox[0, r * owners : (r + 1) * owners] = returned[:, r * LANES : (r + 1) * LANES]
        inbox[1, r * owners : (r + 1) * owners] = pltpu.roll(tails, LANES - tail * r, 1) if r else tails

    def body(e):
        column = plan[1 + e]
        row = plan[1 + capacity + e]
        for f in range(fields):
            for h in range(halves):
                here = (f, h, pl.ds(column, 1), slice(None))
                field[here] = base[here] + inbox[h, pl.ds(row + f * owners, 1), :]

    entry_loop(plan[0], body)
    span_lat = lon_low.shape[2]
    span_lon = lat_low.shape[2]
    for f in range(fields):
        for h in range(halves):
            lon_low[f, h] = field[f, h, :span_lat].astype(BF16)
            lon_high[f, h] = field[f, h, columns_all - span_lat :].astype(BF16)
            lat_low[f, h] = field[f, h, pl.ds(0, span_lon, stride=span_lat), :].astype(BF16)
            lat_high[f, h] = field[f, h, pl.ds(span_lat - 1, span_lon, stride=span_lat), :].astype(BF16)


def inner_stencil(field, coef, extra, out):
    fields, halves, columns_all, lanes = field.shape
    span_lat, span_lon = coef.shape[1:]
    row = lax.broadcasted_iota(jnp.int32, (span_lat, 1), 0)
    for p in range(span_lon):
        weight = [coef[k, :, p : p + 1] for k in range(4)]
        weight[2] = jnp.where(row == 0, 0.0, weight[2])
        weight[3] = jnp.where(row == span_lat - 1, 0.0, weight[3])
        weight = [jnp.broadcast_to(w, (span_lat, lanes)) for w in weight]
        at = slice(p * span_lat, (p + 1) * span_lat)
        for f in range(fields):
            for h in range(halves):
                here = field[f, h, at]
                total = here + weight[2] * pltpu.roll(here, 1, 0) + weight[3] * pltpu.roll(here, span_lat - 1, 0)
                if p > 0:
                    total = total + weight[0] * field[f, h, (p - 1) * span_lat : p * span_lat]
                if p < span_lon - 1:
                    total = total + weight[1] * field[f, h, (p + 1) * span_lat : (p + 2) * span_lat]
                if extra is None:
                    out[f, h, at] = total
                elif h == 0:
                    out[f, h, at] = total + extra[f, at, :lanes].astype(F32)
                else:
                    tail = extra.shape[2] - lanes
                    out[f, h, at, :tail] = total[:, :tail] + extra[f, at, lanes:].astype(F32)


def inner_first(field, coef, early, out):
    inner_stencil(field, coef, early, out)


def inner_last(field, coef, out):
    inner_stencil(field, coef, None, out)


def edge_weights(coef):
    span_lat, span_lon = coef.shape[1:]
    same = lax.broadcasted_iota(jnp.int32, (span_lon, span_lon), 0) == lax.broadcasted_iota(
        jnp.int32, (span_lon, span_lon), 1
    )

    def upright(line):
        return jnp.sum(jnp.where(same, jnp.broadcast_to(line, (span_lon, span_lon)), 0.0), axis=1, keepdims=True)

    return (
        coef[0, :, :1],
        coef[1, :, span_lon - 1 :],
        upright(coef[2, :1, :]),
        upright(coef[3, span_lat - 1 :, :]),
    )


def add_edges(f, h, weights, from_before, from_after, from_low, from_high, out):
    columns_all = out.shape[2]
    span_lat = from_before.shape[2]
    span_lon = from_low.shape[2]
    first = (f, h, slice(0, span_lat))
    last = (f, h, slice(columns_all - span_lat, columns_all))
    low = (f, h, pl.ds(0, span_lon, stride=span_lat), slice(None))
    high = (f, h, pl.ds(span_lat - 1, span_lon, stride=span_lat), slice(None))
    for at, weight, edge in zip((first, last, low, high), weights, (from_before, from_after, from_low, from_high)):
        out[at] = out[at] + weight * edge[f, h].astype(F32)


def edges_first(plan, inner, coef, from_before, from_after, from_low, from_high, out, outbox, rows):
    fields, halves, columns_all, lanes = out.shape
    capacity = (plan.shape[0] - 1) // 2
    owners = rows.shape[1] // (PAIR * fields)
    tail = outbox.shape[1] - lanes
    weights = edge_weights(coef)
    rows[...] = jnp.zeros(rows.shape, F32)
    for f in range(fields):
        for h in range(halves):
            add_edges(f, h, weights, from_before, from_after, from_low, from_high, out)

    def body(e):
        column = plan[1 + e]
        row = plan[1 + capacity + e]
        rank = row // (fields * owners)
        first = ((row - rank * (fields * owners)) * PAIR + rank) * fields
        for f in range(fields):
            for h in range(halves):
                rows[h, pl.ds(first + f, 1), :] = out[f, h, pl.ds(column, 1), :]

    entry_loop(plan[0], body)
    outbox[:, :lanes] = rows[0].astype(BF16)
    outbox[:, lanes:] = rows[1, :, :tail].astype(BF16)


def edges_last(inner, coef, from_before, from_after, from_low, from_high, out_hbm, both, out, sems):
    fields, halves, columns_all, lanes = inner.shape
    tail = out.shape[2] - lanes
    weights = edge_weights(coef)
    copies = []
    for f in range(fields):
        for h in range(halves):
            both[f, h] = inner[f, h]
            add_edges(f, h, weights, from_before, from_after, from_low, from_high, both)
        out[f, :, :lanes] = both[f, 0]
        out[f, :, lanes:] = both[f, 1, :, :tail]
        copies.append(pltpu.make_async_copy(out.at[f], out_hbm.at[f], sems.at[f]))
        copies[f].start()
    for copy in copies:
        copy.wait()


def exchange(rows, groups):
    width = rows.shape[0] // groups
    moved = lax.all_to_all(
        rows.reshape(groups, width, rows.shape[1]), "gy", split_axis=0, concat_axis=0, tiled=True
    )
    return moved.reshape(rows.shape)


def halos(lon_low, lon_high, lat_low, lat_high):
    lon = lax.axis_size("gx")
    lat = lax.axis_size("gy")
    up = [(i, (i + 1) % lon) for i in range(lon)]
    down = [(target, source) for source, target in up]
    north = [(i, i + 1) for i in range(lat - 1)]
    south = [(target, source) for source, target in north]
    from_low = lax.ppermute(lat_high, "gy", north)
    from_high = lax.ppermute(lat_low, "gy", south)
    from_before = lax.ppermute(lon_high, "gx", up)
    from_after = lax.ppermute(lon_low, "gx", down)
    return from_before, from_after, from_low, from_high


def on_device(late, early, stencil_coef, jacobian, cloudy_cols, cloudy_count, owner_rank, owner_slot):
    fields, levels, span_lon, span_lat = late.shape
    groups = lax.axis_size("gy")
    own_slots = jacobian.shape[1]
    capacity = cloudy_cols.shape[2]
    columns_all = span_lon * span_lat
    late = late.transpose(0, 2, 3, 1).reshape(fields, columns_all, levels)
    early = early.transpose(0, 2, 3, 1).reshape(fields, columns_all, levels)
    coef = stencil_coef.transpose(0, 2, 1)
    matrices = jacobian[0]
    shape = jax.ShapeDtypeStruct
    per_owner = PAIR * fields
    inbox_rows = groups * per_owner
    grid = (fields, columns_all, levels)
    halves = (fields, 2, columns_all, LANES)
    plan_shape = shape((2 * capacity + 1,), jnp.int32)

    outbox, plan = call(
        pack_first,
        [shape((inbox_rows, levels + 1), BF16), plan_shape],
        [HBM] * 5,
        [VMEM, SMEM],
        [
            SMEM(cloudy_cols.shape, jnp.int32),
            SMEM(cloudy_count.shape, jnp.int32),
            SMEM(owner_rank.shape, jnp.int32),
            SMEM(owner_slot.shape, jnp.int32),
            VMEM(grid, BF16),
            VMEM(halves, F32),
            VMEM((2, inbox_rows, LANES), F32),
            SMEM((groups,), jnp.int32),
            pltpu.SemaphoreType.DMA((4 + fields,)),
        ],
        vmem=57,
    )(cloudy_cols, cloudy_count, owner_rank, owner_slot, late)
    received = exchange(outbox, groups)
    chosen_shape = shape((inbox_rows, own_slots * fields), BF16)
    placed_shape = shape((own_slots * fields, levels), BF16)
    placed, chosen, answering = call(
        place_first,
        [placed_shape, chosen_shape, chosen_shape],
        [VMEM],
        [VMEM] * 3,
        [VMEM(chosen_shape.shape, F32)],
    )(received)

    def apply(placed):
        result = jnp.einsum(
            "sfij,sfi->sfj",
            matrices,
            placed.reshape(own_slots, fields, levels),
            preferred_element_type=F32,
        ).reshape(own_slots * fields, levels)
        (answer,) = call(
            answer_kernel,
            [shape((groups, (per_owner + 1) * LANES), F32)],
            [VMEM] * 2,
            [VMEM],
            [VMEM((own_slots * fields, 2 * LANES), F32)],
        )(result, answering)
        return exchange(answer, groups)

    edge_shapes = [shape((fields, 2, span, LANES), BF16) for span in (span_lat, span_lat, span_lon, span_lon)]

    def add(kernel, returned, base, aliases):
        return call(
            functools.partial(kernel, levels=levels),
            [shape(halves, F32)] + edge_shapes,
            [SMEM] + [VMEM] * 2,
            [VMEM] * 5,
            [VMEM((2, inbox_rows, LANES), F32)],
            aliases,
        )(plan, returned, base)

    field, *edges = add(add_first, apply(placed), late, {})
    neighbours = halos(*edges)
    (inner,) = call(inner_first, [shape(halves, F32)], [VMEM] * 3, [VMEM], touched=6000000)(field, coef, early)
    adjoint, outbox = call(
        edges_first,
        [shape(halves, F32), shape((inbox_rows, levels), BF16)],
        [SMEM] + [VMEM] * 6,
        [VMEM] * 2,
        [VMEM((2, inbox_rows, LANES), F32)],
        {1: 0},
    )(plan, inner, coef, *neighbours)
    received = exchange(outbox, groups)
    (placed,) = call(place_second, [placed_shape], [VMEM] * 2, [VMEM])(received, chosen)
    field, *edges = add(add_increments, apply(placed), adjoint, {2: 0})
    neighbours = halos(*edges)
    (inner,) = call(inner_last, [shape(halves, F32)], [VMEM] * 2, [VMEM], touched=6000000)(field, coef)
    (final,) = call(
        edges_last,
        [shape(grid, F32)],
        [VMEM] * 6,
        [HBM],
        [VMEM(halves, F32), VMEM(grid, F32), pltpu.SemaphoreType.DMA((fields,))],
    )(inner, coef, *neighbours)
    return final.reshape(fields, span_lon, span_lat, levels).transpose(0, 3, 1, 2)


def solution(mesh):
    return jax.shard_map(
        on_device,
        mesh=mesh,
        in_specs=(
            P(None, None, "gx", "gy"),
            P(None, None, "gx", "gy"),
            P(None, "gx", "gy"),
            P("gx", "gy", None, None, None),
            P("gx", "gy", None),
            P("gx", "gy"),
            P("gx", "gy", None),
            P("gx", "gy", None),
        ),
        out_specs=P(None, None, "gx", "gy"),
        check_vma=False,
    )
```

```python
import functools

import jax
import jax.numpy as jnp
from jax import lax
from jax.experimental import pallas as pl
from jax.experimental.pallas import tpu as pltpu
from jax.sharding import PartitionSpec as P

BF16 = jnp.bfloat16
F32 = jnp.float32
VMEM = pltpu.VMEM
SMEM = pltpu.SMEM
HBM = pltpu.HBM
PAIR = 2
LANES = 128
GROUP = 4


def call(kernel, out_shape, in_spaces, out_spaces, scratch=(), aliases=None, flops=1000, touched=1000000, vmem=40):
    return pl.pallas_call(
        kernel,
        out_shape=out_shape,
        in_specs=[pl.BlockSpec(memory_space=space) for space in in_spaces],
        out_specs=[pl.BlockSpec(memory_space=space) for space in out_spaces],
        scratch_shapes=scratch,
        input_output_aliases=aliases or {},
        compiler_params=pltpu.CompilerParams(vmem_limit_bytes=vmem * 1024 * 1024),
        cost_estimate=pl.CostEstimate(flops=flops, bytes_accessed=touched, transcendentals=0),
    )


def entry_groups(plan, body):
    capacity = (plan.shape[0] - 1) // 2

    def step(g, carry):
        first = g * GROUP
        body([(plan[1 + first + i], plan[1 + capacity + first + i]) for i in range(GROUP)])
        return carry

    lax.fori_loop(0, (plan[0] + (GROUP - 1)) // GROUP, step, 0)


def unpack_field(packed, field, f):
    field[f, 0] = packed[f, :, :LANES].astype(F32)
    field[f, 1, :, : packed.shape[2] - LANES] = packed[f, :, LANES:].astype(F32)


def pack_first(
    cols_hbm, count_hbm, owner_hbm, slot_hbm, late_hbm, outbox, plan, cols, count, owner, slot, late, field, rows, used, sems
):
    fields = field.shape[0]
    levels = late.shape[2]
    capacity = cols.shape[2]
    owners = used.shape[0]
    tail = levels - LANES
    end = lax.broadcasted_iota(jnp.int32, (1, LANES), 1)
    small = [(cols_hbm, cols), (count_hbm, count), (owner_hbm, owner), (slot_hbm, slot)]
    copies = [pltpu.make_async_copy(source, target, sems.at[i]) for i, (source, target) in enumerate(small)]
    copies += [pltpu.make_async_copy(late_hbm.at[f], late.at[f], sems.at[len(small) + f]) for f in range(fields)]
    for copy in copies:
        copy.start()
    for o in range(owners):
        used[o] = 0
    for copy in copies[: len(small)]:
        copy.wait()
    live = count[0, 0]
    plan[0] = live

    def route(e, carry):
        o = owner[0, 0, e]
        rank = used[o]
        used[o] = rank + 1
        plan[1 + e] = cols[0, 0, e]
        plan[1 + capacity + e] = rank * (fields * owners) + o
        return carry

    lax.fori_loop(0, live, route, 0)
    whole = (live // GROUP) * GROUP

    def repeat(e, carry):
        for part in (1, 1 + capacity):
            plan[part + e] = plan[part + whole]
        slot[0, 0, e] = slot[0, 0, whole]
        return carry

    lax.fori_loop(live, ((live + (GROUP - 1)) // GROUP) * GROUP, repeat, 0)
    rows[...] = jnp.zeros(rows.shape, F32)
    for f in range(fields):
        copies[len(small) + f].wait()
        unpack_field(late, field, f)

    def gather(g, carry):
        first = g * GROUP
        found = []
        for i in range(GROUP):
            column = plan[1 + first + i]
            row = outbox_row(plan[1 + capacity + first + i], owners, fields)
            code = slot[0, 0, first + i] * fields
            for f in range(fields):
                mark = (code + (f + 1)).astype(F32)
                found.append((0, row + f, field[f, 0, pl.ds(column, 1), :]))
                found.append((1, row + f, jnp.where(end == tail, mark, field[f, 1, pl.ds(column, 1), :])))
        for h, row, value in found:
            rows[h, pl.ds(row, 1), :] = value
        return carry

    lax.fori_loop(0, (live + (GROUP - 1)) // GROUP, gather, 0)
    outbox[:, :LANES] = rows[0].astype(BF16)
    outbox[:, LANES:] = rows[1, :, : tail + 1].astype(BF16)


def outbox_row(row, owners, fields):
    rank = row // (fields * owners)
    return ((row - rank * (fields * owners)) * PAIR + rank) * fields


def split_dot(chosen, value):
    high = value.astype(BF16)
    rest = value - high.astype(F32)
    middle = rest.astype(BF16)
    low = (rest - middle.astype(F32)).astype(BF16)
    dot = functools.partial(jnp.dot, preferred_element_type=F32)
    return dot(chosen, high) + dot(chosen, middle) + dot(chosen, low)


def fetch(matrices_hbm, matrices, sems):
    copies = [
        pltpu.make_async_copy(matrices_hbm.at[s], matrices.at[s], sems.at[s]) for s in range(matrices.shape[0])
    ]
    for copy in copies:
        copy.start()
    return copies


def products(chosen, values, answering, matrices, copies, answer, spread, result):
    own_slots, levels, fields, _ = matrices.shape
    depth = levels * fields
    placed = lax.dot_general(chosen, values, (((0,), (0,)), ((), ())), preferred_element_type=F32).astype(BF16)
    iota = functools.partial(lax.broadcasted_iota, jnp.int32)
    widen = (iota((levels, depth), 1) // fields == iota((levels, depth), 0)).astype(F32).astype(BF16)
    wide = jnp.dot(placed, widen, preferred_element_type=F32)
    own = iota(spread.shape, 1) % fields == iota(spread.shape, 0) % fields
    spread[...] = jnp.where(own, wide, 0.0)
    result[...] = jnp.zeros(result.shape, F32)
    for s in range(own_slots):
        at = slice(s * fields, (s + 1) * fields)
        copies[s].wait()
        result[at, :levels] = jnp.dot(
            spread[at].astype(BF16), matrices[s].reshape(depth, levels), preferred_element_type=F32
        )
    owners = answer.shape[0]
    tail = levels - LANES
    per_owner = answering.shape[0] // owners
    rows = split_dot(answering, result[...])
    tails = jnp.zeros((owners, LANES), F32)
    for r in range(per_owner):
        block = rows[r * owners : (r + 1) * owners]
        answer[:, r * LANES : (r + 1) * LANES] = block[:, :LANES]
        end = block[:, LANES:]
        tails = tails + (pltpu.roll(end, tail * r, 1) if r else end)
    answer[:, per_owner * LANES :] = tails


def physics_first(received, matrices_hbm, answer, chosen_out, answering_out, spread, result, matrices, sems, choice):
    copies = fetch(matrices_hbm, matrices, sems)
    levels = matrices.shape[1]
    owners = answer.shape[0]
    per_owner = received.shape[0] // owners
    values = received[...].astype(F32)
    codes = values[:, levels:]
    wanted = (lax.broadcasted_iota(jnp.int32, choice.shape, 1) + 1).astype(F32)
    choice[...] = (codes == wanted).astype(F32)
    chosen = choice[...].astype(BF16)
    answering = jnp.concatenate(
        [choice[pl.ds(r, owners, stride=per_owner), :] for r in range(per_owner)], axis=0
    ).astype(BF16)
    chosen_out[...] = chosen
    answering_out[...] = answering
    products(chosen, values[:, :levels].astype(BF16), answering, matrices, copies, answer, spread, result)


def physics_second(received, matrices_hbm, chosen, answering, answer, spread, result, matrices, sems):
    copies = fetch(matrices_hbm, matrices, sems)
    products(chosen[...], received[...], answering[...], matrices, copies, answer, spread, result)


def add_first(plan, returned, late, field, *rest, levels):
    for f in range(field.shape[0]):
        unpack_field(late, field, f)
    add_increments(plan, returned, field, field, *rest, levels=levels)


def add_increments(plan, returned, base, field, lon_low, lon_high, lat_low, lat_high, inbox, *, levels):
    fields, halves, columns_all, lanes = field.shape
    owners = returned.shape[0]
    per_owner = inbox.shape[1] // owners
    tail = levels - LANES
    tails = returned[:, per_owner * LANES :]
    for r in range(per_owner):
        inbox[0, r * owners : (r + 1) * owners] = returned[:, r * LANES : (r + 1) * LANES]
        inbox[1, r * owners : (r + 1) * owners] = pltpu.roll(tails, LANES - tail * r, 1) if r else tails

    def body(entries):
        found = []
        for column, row in entries:
            for f in range(fields):
                for h in range(halves):
                    here = (f, h, pl.ds(column, 1), slice(None))
                    found.append((here, base[here] + inbox[h, pl.ds(row + f * owners, 1), :]))
        for here, value in found:
            field[here] = value

    entry_groups(plan, body)
    span_lat = lon_low.shape[2]
    span_lon = lat_low.shape[2]
    for f in range(fields):
        for h in range(halves):
            lon_low[f, h] = field[f, h, :span_lat].astype(BF16)
            lon_high[f, h] = field[f, h, columns_all - span_lat :].astype(BF16)
            lat_low[f, h] = field[f, h, pl.ds(0, span_lon, stride=span_lat), :].astype(BF16)
            lat_high[f, h] = field[f, h, pl.ds(span_lat - 1, span_lon, stride=span_lat), :].astype(BF16)


def inner_stencil(field, coef, extra, out):
    fields, halves, columns_all, lanes = field.shape
    span_lat, span_lon = coef.shape[1:]
    row = lax.broadcasted_iota(jnp.int32, (span_lat, 1), 0)
    for p in range(span_lon):
        weight = [coef[k, :, p : p + 1] for k in range(4)]
        weight[2] = jnp.where(row == 0, 0.0, weight[2])
        weight[3] = jnp.where(row == span_lat - 1, 0.0, weight[3])
        weight = [jnp.broadcast_to(w, (span_lat, lanes)) for w in weight]
        at = slice(p * span_lat, (p + 1) * span_lat)
        for f in range(fields):
            for h in range(halves):
                here = field[f, h, at]
                total = here + weight[2] * pltpu.roll(here, 1, 0) + weight[3] * pltpu.roll(here, span_lat - 1, 0)
                if p > 0:
                    total = total + weight[0] * field[f, h, (p - 1) * span_lat : p * span_lat]
                if p < span_lon - 1:
                    total = total + weight[1] * field[f, h, (p + 1) * span_lat : (p + 2) * span_lat]
                if extra is None:
                    out[f, h, at] = total
                elif h == 0:
                    out[f, h, at] = total + extra[f, at, :lanes].astype(F32)
                else:
                    tail = extra.shape[2] - lanes
                    out[f, h, at, :tail] = total[:, :tail] + extra[f, at, lanes:].astype(F32)


def inner_first(field, coef, early, out):
    inner_stencil(field, coef, early, out)


def inner_last(field, coef, out):
    inner_stencil(field, coef, None, out)


def edge_weights(coef):
    span_lat, span_lon = coef.shape[1:]
    same = lax.broadcasted_iota(jnp.int32, (span_lon, span_lon), 0) == lax.broadcasted_iota(
        jnp.int32, (span_lon, span_lon), 1
    )

    def upright(line):
        return jnp.sum(jnp.where(same, jnp.broadcast_to(line, (span_lon, span_lon)), 0.0), axis=1, keepdims=True)

    return (
        coef[0, :, :1],
        coef[1, :, span_lon - 1 :],
        upright(coef[2, :1, :]),
        upright(coef[3, span_lat - 1 :, :]),
    )


def add_edges(f, h, weights, from_before, from_after, from_low, from_high, out):
    columns_all = out.shape[2]
    span_lat = from_before.shape[2]
    span_lon = from_low.shape[2]
    first = (f, h, slice(0, span_lat))
    last = (f, h, slice(columns_all - span_lat, columns_all))
    low = (f, h, pl.ds(0, span_lon, stride=span_lat), slice(None))
    high = (f, h, pl.ds(span_lat - 1, span_lon, stride=span_lat), slice(None))
    for at, weight, edge in zip((first, last, low, high), weights, (from_before, from_after, from_low, from_high)):
        out[at] = out[at] + weight * edge[f, h].astype(F32)


def edges_first(plan, inner, coef, from_before, from_after, from_low, from_high, out, outbox, rows):
    fields, halves, columns_all, lanes = out.shape
    owners = rows.shape[1] // (PAIR * fields)
    tail = outbox.shape[1] - lanes
    weights = edge_weights(coef)
    rows[...] = jnp.zeros(rows.shape, F32)
    for f in range(fields):
        for h in range(halves):
            add_edges(f, h, weights, from_before, from_after, from_low, from_high, out)

    def body(entries):
        found = []
        for column, row in entries:
            first = outbox_row(row, owners, fields)
            for f in range(fields):
                for h in range(halves):
                    found.append((h, first + f, out[f, h, pl.ds(column, 1), :]))
        for h, row, value in found:
            rows[h, pl.ds(row, 1), :] = value

    entry_groups(plan, body)
    outbox[:, :lanes] = rows[0].astype(BF16)
    outbox[:, lanes:] = rows[1, :, :tail].astype(BF16)


def edges_last(inner, coef, from_before, from_after, from_low, from_high, out_hbm, both, out, sems):
    fields, halves, columns_all, lanes = inner.shape
    tail = out.shape[2] - lanes
    weights = edge_weights(coef)
    copies = []
    for f in range(fields):
        for h in range(halves):
            both[f, h] = inner[f, h]
            add_edges(f, h, weights, from_before, from_after, from_low, from_high, both)
        out[f, :, :lanes] = both[f, 0]
        out[f, :, lanes:] = both[f, 1, :, :tail]
        copies.append(pltpu.make_async_copy(out.at[f], out_hbm.at[f], sems.at[f]))
        copies[f].start()
    for copy in copies:
        copy.wait()


def exchange(rows, groups):
    width = rows.shape[0] // groups
    moved = lax.all_to_all(
        rows.reshape(groups, width, rows.shape[1]), "gy", split_axis=0, concat_axis=0, tiled=True
    )
    return moved.reshape(rows.shape)


def halos(lon_low, lon_high, lat_low, lat_high):
    lon = lax.axis_size("gx")
    lat = lax.axis_size("gy")
    up = [(i, (i + 1) % lon) for i in range(lon)]
    down = [(target, source) for source, target in up]
    north = [(i, i + 1) for i in range(lat - 1)]
    south = [(target, source) for source, target in north]
    from_low = lax.ppermute(lat_high, "gy", north)
    from_high = lax.ppermute(lat_low, "gy", south)
    from_before = lax.ppermute(lon_high, "gx", up)
    from_after = lax.ppermute(lon_low, "gx", down)
    return from_before, from_after, from_low, from_high


def on_device(late, early, stencil_coef, jacobian, cloudy_cols, cloudy_count, owner_rank, owner_slot):
    fields, levels, span_lon, span_lat = late.shape
    groups = lax.axis_size("gy")
    own_slots = jacobian.shape[1]
    capacity = cloudy_cols.shape[2]
    columns_all = span_lon * span_lat
    late = late.transpose(0, 2, 3, 1).reshape(fields, columns_all, levels)
    early = early.transpose(0, 2, 3, 1).reshape(fields, columns_all, levels)
    coef = stencil_coef.transpose(0, 2, 1)
    matrices = jacobian[0].transpose(0, 2, 1, 3)
    shape = jax.ShapeDtypeStruct
    per_owner = PAIR * fields
    inbox_rows = groups * per_owner
    grid = (fields, columns_all, levels)
    halves = (fields, 2, columns_all, LANES)
    plan_shape = shape((2 * capacity + 1,), jnp.int32)

    outbox, plan = call(
        pack_first,
        [shape((inbox_rows, levels + 1), BF16), plan_shape],
        [HBM] * 5,
        [VMEM, SMEM],
        [
            SMEM(cloudy_cols.shape, jnp.int32),
            SMEM(cloudy_count.shape, jnp.int32),
            SMEM(owner_rank.shape, jnp.int32),
            SMEM(owner_slot.shape, jnp.int32),
            VMEM(grid, BF16),
            VMEM(halves, F32),
            VMEM((2, inbox_rows, LANES), F32),
            SMEM((groups,), jnp.int32),
            pltpu.SemaphoreType.DMA((4 + fields,)),
        ],
        vmem=57,
    )(cloudy_cols, cloudy_count, owner_rank, owner_slot, late)
    received = exchange(outbox, groups)
    chosen_shape = shape((inbox_rows, own_slots * fields), BF16)
    answer_shape = shape((groups, (per_owner + 1) * LANES), F32)
    spaces = [
        VMEM((own_slots * fields, levels * fields), F32),
        VMEM((own_slots * fields, 2 * LANES), F32),
        VMEM(matrices.shape, BF16),
        pltpu.SemaphoreType.DMA((own_slots,)),
    ]
    answer, chosen, answering = call(
        physics_first,
        [answer_shape, chosen_shape, chosen_shape],
        [VMEM, HBM],
        [VMEM] * 3,
        spaces + [VMEM(chosen_shape.shape, F32)],
        vmem=50,
    )(received, matrices)
    returned = exchange(answer, groups)

    edge_shapes = [shape((fields, 2, span, LANES), BF16) for span in (span_lat, span_lat, span_lon, span_lon)]

    def add(kernel, returned, base, aliases):
        return call(
            functools.partial(kernel, levels=levels),
            [shape(halves, F32)] + edge_shapes,
            [SMEM] + [VMEM] * 2,
            [VMEM] * 5,
            [VMEM((2, inbox_rows, LANES), F32)],
            aliases,
        )(plan, returned, base)

    field, *edges = add(add_first, returned, late, {})
    neighbours = halos(*edges)
    (inner,) = call(inner_first, [shape(halves, F32)], [VMEM] * 3, [VMEM], touched=6000000)(field, coef, early)
    adjoint, outbox = call(
        edges_first,
        [shape(halves, F32), shape((inbox_rows, levels), BF16)],
        [SMEM] + [VMEM] * 6,
        [VMEM] * 2,
        [VMEM((2, inbox_rows, LANES), F32)],
        {1: 0},
    )(plan, inner, coef, *neighbours)
    received = exchange(outbox, groups)
    (answer,) = call(physics_second, [answer_shape], [VMEM, HBM] + [VMEM] * 2, [VMEM], spaces, vmem=50)(
        received, matrices, chosen, answering
    )
    returned = exchange(answer, groups)
    field, *edges = add(add_increments, returned, adjoint, {2: 0})
    neighbours = halos(*edges)
    (inner,) = call(inner_last, [shape(halves, F32)], [VMEM] * 2, [VMEM], touched=6000000)(field, coef)
    (final,) = call(
        edges_last,
        [shape(grid, F32)],
        [VMEM] * 6,
        [HBM],
        [VMEM(halves, F32), VMEM(grid, F32), pltpu.SemaphoreType.DMA((fields,))],
    )(inner, coef, *neighbours)
    return final.reshape(fields, span_lon, span_lat, levels).transpose(0, 3, 1, 2)


def solution(mesh):
    return jax.shard_map(
        on_device,
        mesh=mesh,
        in_specs=(
            P(None, None, "gx", "gy"),
            P(None, None, "gx", "gy"),
            P(None, "gx", "gy"),
            P("gx", "gy", None, None, None),
            P("gx", "gy", None),
            P("gx", "gy"),
            P("gx", "gy", None),
            P("gx", "gy", None),
        ),
        out_specs=P(None, None, "gx", "gy"),
        check_vma=False,
    )
```

```python
import functools

import jax
import jax.numpy as jnp
from jax import lax
from jax.experimental import pallas as pl
from jax.experimental.pallas import tpu as pltpu
from jax.sharding import PartitionSpec as P

BF16 = jnp.bfloat16
F32 = jnp.float32
VMEM = pltpu.VMEM
SMEM = pltpu.SMEM
HBM = pltpu.HBM
PAIR = 2
LANES = 128
GROUP = 4
AHEAD = 4


def call(kernel, out_shape, in_spaces, out_spaces, scratch=(), aliases=None, flops=1000, touched=1000000, vmem=40):
    return pl.pallas_call(
        kernel,
        out_shape=out_shape,
        in_specs=[pl.BlockSpec(memory_space=space) for space in in_spaces],
        out_specs=[pl.BlockSpec(memory_space=space) for space in out_spaces],
        scratch_shapes=scratch,
        input_output_aliases=aliases or {},
        compiler_params=pltpu.CompilerParams(vmem_limit_bytes=vmem * 1024 * 1024),
        cost_estimate=pl.CostEstimate(flops=flops, bytes_accessed=touched, transcendentals=0),
    )


def entry_groups(plan, body):
    capacity = (plan.shape[0] - 1) // 2

    def step(g, carry):
        first = g * GROUP
        body([(plan[1 + first + i], plan[1 + capacity + first + i]) for i in range(GROUP)])
        return carry

    lax.fori_loop(0, (plan[0] + (GROUP - 1)) // GROUP, step, 0)


def unpack_field(packed, field, f):
    field[f, 0] = packed[f, :, :LANES].astype(F32)
    field[f, 1, :, : packed.shape[2] - LANES] = packed[f, :, LANES:].astype(F32)


def pack_first(
    cols_hbm, count_hbm, owner_hbm, slot_hbm, late_hbm, outbox, plan, cols, count, owner, slot, late, field, rows, used, sems
):
    fields = field.shape[0]
    levels = late.shape[2]
    capacity = cols.shape[2]
    owners = used.shape[0]
    tail = levels - LANES
    end = lax.broadcasted_iota(jnp.int32, (1, LANES), 1)
    small = [(cols_hbm, cols), (count_hbm, count), (owner_hbm, owner), (slot_hbm, slot)]
    copies = [pltpu.make_async_copy(source, target, sems.at[i]) for i, (source, target) in enumerate(small)]
    copies += [pltpu.make_async_copy(late_hbm.at[f], late.at[f], sems.at[len(small) + f]) for f in range(fields)]
    for copy in copies:
        copy.start()
    for o in range(owners):
        used[o] = 0
    for copy in copies[: len(small)]:
        copy.wait()
    live = count[0, 0]
    plan[0] = live

    def route(e, carry):
        o = owner[0, 0, e]
        rank = used[o]
        used[o] = rank + 1
        plan[1 + e] = cols[0, 0, e]
        plan[1 + capacity + e] = rank * (fields * owners) + o
        return carry

    lax.fori_loop(0, live, route, 0)
    whole = (live // GROUP) * GROUP

    def repeat(e, carry):
        for part in (1, 1 + capacity):
            plan[part + e] = plan[part + whole]
        slot[0, 0, e] = slot[0, 0, whole]
        return carry

    lax.fori_loop(live, ((live + (GROUP - 1)) // GROUP) * GROUP, repeat, 0)
    rows[...] = jnp.zeros(rows.shape, F32)
    for f in range(fields):
        copies[len(small) + f].wait()
        unpack_field(late, field, f)

    def gather(g, carry):
        first = g * GROUP
        found = []
        for i in range(GROUP):
            column = plan[1 + first + i]
            row = outbox_row(plan[1 + capacity + first + i], owners, fields)
            code = slot[0, 0, first + i] * fields
            for f in range(fields):
                mark = (code + (f + 1)).astype(F32)
                found.append((0, row + f, field[f, 0, pl.ds(column, 1), :]))
                found.append((1, row + f, jnp.where(end == tail, mark, field[f, 1, pl.ds(column, 1), :])))
        for h, row, value in found:
            rows[h, pl.ds(row, 1), :] = value
        return carry

    lax.fori_loop(0, (live + (GROUP - 1)) // GROUP, gather, 0)
    outbox[:, :LANES] = rows[0].astype(BF16)
    outbox[:, LANES:] = rows[1, :, : tail + 1].astype(BF16)


def outbox_row(row, owners, fields):
    rank = row // (fields * owners)
    return ((row - rank * (fields * owners)) * PAIR + rank) * fields


def split_dot(chosen, value):
    high = value.astype(BF16)
    rest = value - high.astype(F32)
    middle = rest.astype(BF16)
    low = (rest - middle.astype(F32)).astype(BF16)
    dot = functools.partial(jnp.dot, preferred_element_type=F32)
    return dot(chosen, high) + dot(chosen, middle) + dot(chosen, low)


def fetch(matrices_hbm, matrices, sems):
    copies = [
        pltpu.make_async_copy(matrices_hbm.at[s], matrices.at[s], sems.at[s]) for s in range(matrices.shape[0])
    ]
    for copy in copies[:AHEAD]:
        copy.start()
    return copies


def products(chosen, values, answering, matrices, copies, answer, spread, result):
    own_slots, levels, fields, _ = matrices.shape
    depth = levels * fields
    placed = lax.dot_general(chosen, values, (((0,), (0,)), ((), ())), preferred_element_type=F32).astype(BF16)
    iota = functools.partial(lax.broadcasted_iota, jnp.int32)
    widen = (iota((levels, depth), 1) // fields == iota((levels, depth), 0)).astype(F32).astype(BF16)
    wide = jnp.dot(placed, widen, preferred_element_type=F32)
    own = iota(spread.shape, 1) % fields == iota(spread.shape, 0) % fields
    spread[...] = jnp.where(own, wide, 0.0)
    result[...] = jnp.zeros(result.shape, F32)
    for s in range(own_slots):
        at = slice(s * fields, (s + 1) * fields)
        if copies:
            copies[s].wait()
            if s + AHEAD < own_slots:
                copies[s + AHEAD].start()
        result[at, :levels] = jnp.dot(
            spread[at].astype(BF16), matrices[s].reshape(depth, levels), preferred_element_type=F32
        )
    owners = answer.shape[0]
    tail = levels - LANES
    per_owner = answering.shape[0] // owners
    rows = split_dot(answering, result[...])
    tails = jnp.zeros((owners, LANES), F32)
    for r in range(per_owner):
        block = rows[r * owners : (r + 1) * owners]
        answer[:, r * LANES : (r + 1) * LANES] = block[:, :LANES]
        end = block[:, LANES:]
        tails = tails + (pltpu.roll(end, tail * r, 1) if r else end)
    answer[:, per_owner * LANES :] = tails


def physics_first(received, matrices_hbm, answer, chosen_out, answering_out, spread, result, matrices, sems, choice):
    copies = fetch(matrices_hbm, matrices, sems)
    levels = matrices.shape[1]
    owners = answer.shape[0]
    per_owner = received.shape[0] // owners
    values = received[...].astype(F32)
    codes = values[:, levels:]
    wanted = (lax.broadcasted_iota(jnp.int32, choice.shape, 1) + 1).astype(F32)
    choice[...] = (codes == wanted).astype(F32)
    chosen = choice[...].astype(BF16)
    answering = jnp.concatenate(
        [choice[pl.ds(r, owners, stride=per_owner), :] for r in range(per_owner)], axis=0
    ).astype(BF16)
    chosen_out[...] = chosen
    answering_out[...] = answering
    products(chosen, values[:, :levels].astype(BF16), answering, matrices, copies, answer, spread, result)


def physics_second(received, matrices, chosen, answering, answer, spread, result):
    products(chosen[...], received[...], answering[...], matrices, [], answer, spread, result)


def add_first(plan, returned, late, field, *rest, levels):
    for f in range(field.shape[0]):
        unpack_field(late, field, f)
    add_increments(plan, returned, field, field, *rest, levels=levels)


def add_increments(plan, returned, base, field, lon_low, lon_high, lat_low, lat_high, inbox, *, levels):
    fields, halves, columns_all, lanes = field.shape
    owners = returned.shape[0]
    per_owner = inbox.shape[1] // owners
    tail = levels - LANES
    tails = returned[:, per_owner * LANES :]
    for r in range(per_owner):
        inbox[0, r * owners : (r + 1) * owners] = returned[:, r * LANES : (r + 1) * LANES]
        inbox[1, r * owners : (r + 1) * owners] = pltpu.roll(tails, LANES - tail * r, 1) if r else tails

    def body(entries):
        found = []
        for column, row in entries:
            for f in range(fields):
                for h in range(halves):
                    here = (f, h, pl.ds(column, 1), slice(None))
                    found.append((here, base[here] + inbox[h, pl.ds(row + f * owners, 1), :]))
        for here, value in found:
            field[here] = value

    entry_groups(plan, body)
    span_lat = lon_low.shape[2]
    span_lon = lat_low.shape[2]
    for f in range(fields):
        for h in range(halves):
            lon_low[f, h] = field[f, h, :span_lat].astype(BF16)
            lon_high[f, h] = field[f, h, columns_all - span_lat :].astype(BF16)
            lat_low[f, h] = field[f, h, pl.ds(0, span_lon, stride=span_lat), :].astype(BF16)
            lat_high[f, h] = field[f, h, pl.ds(span_lat - 1, span_lon, stride=span_lat), :].astype(BF16)


def inner_stencil(field, coef, extra, out):
    fields, halves, columns_all, lanes = field.shape
    span_lat, span_lon = coef.shape[1:]
    row = lax.broadcasted_iota(jnp.int32, (span_lat, 1), 0)
    for p in range(span_lon):
        weight = [coef[k, :, p : p + 1] for k in range(4)]
        weight[2] = jnp.where(row == 0, 0.0, weight[2])
        weight[3] = jnp.where(row == span_lat - 1, 0.0, weight[3])
        weight = [jnp.broadcast_to(w, (span_lat, lanes)) for w in weight]
        at = slice(p * span_lat, (p + 1) * span_lat)
        for f in range(fields):
            for h in range(halves):
                here = field[f, h, at]
                total = here + weight[2] * pltpu.roll(here, 1, 0) + weight[3] * pltpu.roll(here, span_lat - 1, 0)
                if p > 0:
                    total = total + weight[0] * field[f, h, (p - 1) * span_lat : p * span_lat]
                if p < span_lon - 1:
                    total = total + weight[1] * field[f, h, (p + 1) * span_lat : (p + 2) * span_lat]
                if extra is None:
                    out[f, h, at] = total
                elif h == 0:
                    out[f, h, at] = total + extra[f, at, :lanes].astype(F32)
                else:
                    tail = extra.shape[2] - lanes
                    out[f, h, at, :tail] = total[:, :tail] + extra[f, at, lanes:].astype(F32)


def inner_first(field, coef, early, out):
    inner_stencil(field, coef, early, out)


def inner_last(field, coef, out):
    inner_stencil(field, coef, None, out)


def edge_weights(coef):
    span_lat, span_lon = coef.shape[1:]
    same = lax.broadcasted_iota(jnp.int32, (span_lon, span_lon), 0) == lax.broadcasted_iota(
        jnp.int32, (span_lon, span_lon), 1
    )

    def upright(line):
        return jnp.sum(jnp.where(same, jnp.broadcast_to(line, (span_lon, span_lon)), 0.0), axis=1, keepdims=True)

    return (
        coef[0, :, :1],
        coef[1, :, span_lon - 1 :],
        upright(coef[2, :1, :]),
        upright(coef[3, span_lat - 1 :, :]),
    )


def add_edges(f, h, weights, from_before, from_after, from_low, from_high, out):
    columns_all = out.shape[2]
    span_lat = from_before.shape[2]
    span_lon = from_low.shape[2]
    first = (f, h, slice(0, span_lat))
    last = (f, h, slice(columns_all - span_lat, columns_all))
    low = (f, h, pl.ds(0, span_lon, stride=span_lat), slice(None))
    high = (f, h, pl.ds(span_lat - 1, span_lon, stride=span_lat), slice(None))
    for at, weight, edge in zip((first, last, low, high), weights, (from_before, from_after, from_low, from_high)):
        out[at] = out[at] + weight * edge[f, h].astype(F32)


def edges_first(plan, inner, coef, from_before, from_after, from_low, from_high, out, outbox, rows):
    fields, halves, columns_all, lanes = out.shape
    owners = rows.shape[1] // (PAIR * fields)
    tail = outbox.shape[1] - lanes
    weights = edge_weights(coef)
    rows[...] = jnp.zeros(rows.shape, F32)
    for f in range(fields):
        for h in range(halves):
            add_edges(f, h, weights, from_before, from_after, from_low, from_high, out)

    def body(entries):
        found = []
        for column, row in entries:
            first = outbox_row(row, owners, fields)
            for f in range(fields):
                for h in range(halves):
                    found.append((h, first + f, out[f, h, pl.ds(column, 1), :]))
        for h, row, value in found:
            rows[h, pl.ds(row, 1), :] = value

    entry_groups(plan, body)
    outbox[:, :lanes] = rows[0].astype(BF16)
    outbox[:, lanes:] = rows[1, :, :tail].astype(BF16)


def edges_last(inner, coef, from_before, from_after, from_low, from_high, out_hbm, both, out, sems):
    fields, halves, columns_all, lanes = inner.shape
    tail = out.shape[2] - lanes
    weights = edge_weights(coef)
    copies = []
    for f in range(fields):
        for h in range(halves):
            both[f, h] = inner[f, h]
            add_edges(f, h, weights, from_before, from_after, from_low, from_high, both)
        out[f, :, :lanes] = both[f, 0]
        out[f, :, lanes:] = both[f, 1, :, :tail]
        copies.append(pltpu.make_async_copy(out.at[f], out_hbm.at[f], sems.at[f]))
        copies[f].start()
    for copy in copies:
        copy.wait()


def exchange(rows, groups):
    width = rows.shape[0] // groups
    moved = lax.all_to_all(
        rows.reshape(groups, width, rows.shape[1]), "gy", split_axis=0, concat_axis=0, tiled=True
    )
    return moved.reshape(rows.shape)


def halos(lon_low, lon_high, lat_low, lat_high):
    lon = lax.axis_size("gx")
    lat = lax.axis_size("gy")
    up = [(i, (i + 1) % lon) for i in range(lon)]
    down = [(target, source) for source, target in up]
    north = [(i, i + 1) for i in range(lat - 1)]
    south = [(target, source) for source, target in north]
    from_low = lax.ppermute(lat_high, "gy", north)
    from_high = lax.ppermute(lat_low, "gy", south)
    from_before = lax.ppermute(lon_high, "gx", up)
    from_after = lax.ppermute(lon_low, "gx", down)
    return from_before, from_after, from_low, from_high


def on_device(late, early, stencil_coef, jacobian, cloudy_cols, cloudy_count, owner_rank, owner_slot):
    fields, levels, span_lon, span_lat = late.shape
    groups = lax.axis_size("gy")
    own_slots = jacobian.shape[1]
    capacity = cloudy_cols.shape[2]
    columns_all = span_lon * span_lat
    late = late.transpose(0, 2, 3, 1).reshape(fields, columns_all, levels)
    early = early.transpose(0, 2, 3, 1).reshape(fields, columns_all, levels)
    coef = stencil_coef.transpose(0, 2, 1)
    matrices = jacobian[0].transpose(0, 2, 1, 3)
    shape = jax.ShapeDtypeStruct
    per_owner = PAIR * fields
    inbox_rows = groups * per_owner
    grid = (fields, columns_all, levels)
    halves = (fields, 2, columns_all, LANES)
    plan_shape = shape((2 * capacity + 1,), jnp.int32)

    outbox, plan = call(
        pack_first,
        [shape((inbox_rows, levels + 1), BF16), plan_shape],
        [HBM] * 5,
        [VMEM, SMEM],
        [
            SMEM(cloudy_cols.shape, jnp.int32),
            SMEM(cloudy_count.shape, jnp.int32),
            SMEM(owner_rank.shape, jnp.int32),
            SMEM(owner_slot.shape, jnp.int32),
            VMEM(grid, BF16),
            VMEM(halves, F32),
            VMEM((2, inbox_rows, LANES), F32),
            SMEM((groups,), jnp.int32),
            pltpu.SemaphoreType.DMA((4 + fields,)),
        ],
        vmem=57,
    )(cloudy_cols, cloudy_count, owner_rank, owner_slot, late)
    received = exchange(outbox, groups)
    chosen_shape = shape((inbox_rows, own_slots * fields), BF16)
    answer_shape = shape((groups, (per_owner + 1) * LANES), F32)
    spaces = [
        VMEM((own_slots * fields, levels * fields), F32),
        VMEM((own_slots * fields, 2 * LANES), F32),
    ]
    answer, chosen, answering = call(
        physics_first,
        [answer_shape, chosen_shape, chosen_shape],
        [VMEM, HBM],
        [VMEM] * 3,
        spaces
        + [
            VMEM(matrices.shape, BF16),
            pltpu.SemaphoreType.DMA((own_slots,)),
            VMEM(chosen_shape.shape, F32),
        ],
        vmem=50,
    )(received, matrices)
    returned = exchange(answer, groups)

    edge_shapes = [shape((fields, 2, span, LANES), BF16) for span in (span_lat, span_lat, span_lon, span_lon)]

    def add(kernel, returned, base, aliases):
        return call(
            functools.partial(kernel, levels=levels),
            [shape(halves, F32)] + edge_shapes,
            [SMEM] + [VMEM] * 2,
            [VMEM] * 5,
            [VMEM((2, inbox_rows, LANES), F32)],
            aliases,
        )(plan, returned, base)

    field, *edges = add(add_first, returned, late, {})
    neighbours = halos(*edges)
    (inner,) = call(inner_first, [shape(halves, F32)], [VMEM] * 3, [VMEM], touched=6000000)(field, coef, early)
    adjoint, outbox = call(
        edges_first,
        [shape(halves, F32), shape((inbox_rows, levels), BF16)],
        [SMEM] + [VMEM] * 6,
        [VMEM] * 2,
        [VMEM((2, inbox_rows, LANES), F32)],
        {1: 0},
    )(plan, inner, coef, *neighbours)
    received = exchange(outbox, groups)
    (answer,) = call(physics_second, [answer_shape], [VMEM] * 4, [VMEM], spaces)(
        received, matrices, chosen, answering
    )
    returned = exchange(answer, groups)
    field, *edges = add(add_increments, returned, adjoint, {2: 0})
    neighbours = halos(*edges)
    (inner,) = call(inner_last, [shape(halves, F32)], [VMEM] * 2, [VMEM], touched=6000000)(field, coef)
    (final,) = call(
        edges_last,
        [shape(grid, F32)],
        [VMEM] * 6,
        [HBM],
        [VMEM(halves, F32), VMEM(grid, F32), pltpu.SemaphoreType.DMA((fields,))],
    )(inner, coef, *neighbours)
    return final.reshape(fields, span_lon, span_lat, levels).transpose(0, 3, 1, 2)


def solution(mesh):
    return jax.shard_map(
        on_device,
        mesh=mesh,
        in_specs=(
            P(None, None, "gx", "gy"),
            P(None, None, "gx", "gy"),
            P(None, "gx", "gy"),
            P("gx", "gy", None, None, None),
            P("gx", "gy", None),
            P("gx", "gy"),
            P("gx", "gy", None),
            P("gx", "gy", None),
        ),
        out_specs=P(None, None, "gx", "gy"),
        check_vma=False,
    )
```

```python
import functools

import jax
import jax.numpy as jnp
from jax import lax
from jax.experimental import pallas as pl
from jax.experimental.pallas import tpu as pltpu
from jax.sharding import PartitionSpec as P

BF16 = jnp.bfloat16
F32 = jnp.float32
VMEM = pltpu.VMEM
SMEM = pltpu.SMEM
HBM = pltpu.HBM
PAIR = 2
LANES = 128
GROUP = 4


def call(kernel, out_shape, in_spaces, out_spaces, scratch=(), aliases=None, flops=1000, touched=1000000, vmem=40):
    return pl.pallas_call(
        kernel,
        out_shape=out_shape,
        in_specs=[pl.BlockSpec(memory_space=space) for space in in_spaces],
        out_specs=[pl.BlockSpec(memory_space=space) for space in out_spaces],
        scratch_shapes=scratch,
        input_output_aliases=aliases or {},
        compiler_params=pltpu.CompilerParams(vmem_limit_bytes=vmem * 1024 * 1024),
        cost_estimate=pl.CostEstimate(flops=flops, bytes_accessed=touched, transcendentals=0),
    )


def entry_groups(plan, body):
    capacity = (plan.shape[0] - 1) // 2

    def step(g, carry):
        first = g * GROUP
        body([(plan[1 + first + i], plan[1 + capacity + first + i]) for i in range(GROUP)])
        return carry

    lax.fori_loop(0, (plan[0] + (GROUP - 1)) // GROUP, step, 0)


def unpack_field(packed, field, f):
    field[f, 0] = packed[f, :, :LANES].astype(F32)
    field[f, 1, :, : packed.shape[2] - LANES] = packed[f, :, LANES:].astype(F32)


def pack_first(
    cols_hbm, count_hbm, owner_hbm, slot_hbm, late_hbm, outbox, plan, cols, count, owner, slot, late, field, rows, used, sems
):
    fields = field.shape[0]
    levels = late.shape[2]
    capacity = cols.shape[2]
    owners = used.shape[0]
    tail = levels - LANES
    end = lax.broadcasted_iota(jnp.int32, (1, LANES), 1)
    small = [(cols_hbm, cols), (count_hbm, count), (owner_hbm, owner), (slot_hbm, slot)]
    copies = [pltpu.make_async_copy(source, target, sems.at[i]) for i, (source, target) in enumerate(small)]
    copies += [pltpu.make_async_copy(late_hbm.at[f], late.at[f], sems.at[len(small) + f]) for f in range(fields)]
    for copy in copies:
        copy.start()
    for o in range(owners):
        used[o] = 0
    for copy in copies[: len(small)]:
        copy.wait()
    live = count[0, 0]
    plan[0] = live

    def route(e, carry):
        o = owner[0, 0, e]
        rank = used[o]
        used[o] = rank + 1
        plan[1 + e] = cols[0, 0, e]
        plan[1 + capacity + e] = rank * (fields * owners) + o
        return carry

    lax.fori_loop(0, live, route, 0)
    whole = (live // GROUP) * GROUP

    def repeat(e, carry):
        for part in (1, 1 + capacity):
            plan[part + e] = plan[part + whole]
        slot[0, 0, e] = slot[0, 0, whole]
        return carry

    lax.fori_loop(live, ((live + (GROUP - 1)) // GROUP) * GROUP, repeat, 0)
    rows[...] = jnp.zeros(rows.shape, F32)
    for f in range(fields):
        copies[len(small) + f].wait()
        unpack_field(late, field, f)

    def gather(g, carry):
        first = g * GROUP
        found = []
        for i in range(GROUP):
            column = plan[1 + first + i]
            row = outbox_row(plan[1 + capacity + first + i], owners, fields)
            code = slot[0, 0, first + i] * fields
            for f in range(fields):
                mark = (code + (f + 1)).astype(F32)
                found.append((0, row + f, field[f, 0, pl.ds(column, 1), :]))
                found.append((1, row + f, jnp.where(end == tail, mark, field[f, 1, pl.ds(column, 1), :])))
        for h, row, value in found:
            rows[h, pl.ds(row, 1), :] = value
        return carry

    lax.fori_loop(0, (live + (GROUP - 1)) // GROUP, gather, 0)
    outbox[:, :LANES] = rows[0].astype(BF16)
    outbox[:, LANES:] = rows[1, :, : tail + 1].astype(BF16)


def outbox_row(row, owners, fields):
    rank = row // (fields * owners)
    return ((row - rank * (fields * owners)) * PAIR + rank) * fields


def split_dot(chosen, value):
    high = value.astype(BF16)
    rest = value - high.astype(F32)
    middle = rest.astype(BF16)
    low = (rest - middle.astype(F32)).astype(BF16)
    dot = functools.partial(jnp.dot, preferred_element_type=F32)
    return dot(chosen, high) + dot(chosen, middle) + dot(chosen, low)


def products(chosen, values, answering, matrices, answer, spread, result):
    own_slots, levels, fields, _ = matrices.shape
    depth = levels * fields
    placed = lax.dot_general(chosen, values, (((0,), (0,)), ((), ())), preferred_element_type=F32).astype(BF16)
    iota = functools.partial(lax.broadcasted_iota, jnp.int32)
    widen = (iota((levels, depth), 1) // fields == iota((levels, depth), 0)).astype(F32).astype(BF16)
    wide = jnp.dot(placed, widen, preferred_element_type=F32)
    own = iota(spread.shape, 1) % fields == iota(spread.shape, 0) % fields
    spread[...] = jnp.where(own, wide, 0.0)
    result[...] = jnp.zeros(result.shape, F32)
    for s in range(own_slots):
        at = slice(s * fields, (s + 1) * fields)
        result[at, :levels] = jnp.dot(
            spread[at].astype(BF16), matrices[s].reshape(depth, levels), preferred_element_type=F32
        )
    owners = answer.shape[0]
    tail = levels - LANES
    per_owner = answering.shape[0] // owners
    rows = split_dot(answering, result[...])
    tails = jnp.zeros((owners, LANES), F32)
    for r in range(per_owner):
        block = rows[r * owners : (r + 1) * owners]
        answer[:, r * LANES : (r + 1) * LANES] = block[:, :LANES]
        end = block[:, LANES:]
        tails = tails + (pltpu.roll(end, tail * r, 1) if r else end)
    answer[:, per_owner * LANES :] = tails


def physics_first(received, matrices, answer, chosen_out, answering_out, spread, result, choice):
    levels = matrices.shape[1]
    owners = answer.shape[0]
    per_owner = received.shape[0] // owners
    values = received[...].astype(F32)
    codes = values[:, levels:]
    wanted = (lax.broadcasted_iota(jnp.int32, choice.shape, 1) + 1).astype(F32)
    choice[...] = (codes == wanted).astype(F32)
    chosen = choice[...].astype(BF16)
    answering = jnp.concatenate(
        [choice[pl.ds(r, owners, stride=per_owner), :] for r in range(per_owner)], axis=0
    ).astype(BF16)
    chosen_out[...] = chosen
    answering_out[...] = answering
    products(chosen, values[:, :levels].astype(BF16), answering, matrices, answer, spread, result)


def physics_second(received, matrices, chosen, answering, answer, spread, result):
    products(chosen[...], received[...], answering[...], matrices, answer, spread, result)


def widen(late, field):
    for f in range(field.shape[0]):
        unpack_field(late, field, f)


def add_increments(plan, returned, base, field, lon_even, lon_odd, lat_even, lat_odd, inbox, *, levels):
    fields, halves, columns_all, lanes = field.shape
    owners = returned.shape[0]
    per_owner = inbox.shape[1] // owners
    tail = levels - LANES
    tails = returned[:, per_owner * LANES :]
    for r in range(per_owner):
        inbox[0, r * owners : (r + 1) * owners] = returned[:, r * LANES : (r + 1) * LANES]
        inbox[1, r * owners : (r + 1) * owners] = pltpu.roll(tails, LANES - tail * r, 1) if r else tails

    def body(entries):
        found = []
        for column, row in entries:
            for f in range(fields):
                for h in range(halves):
                    here = (f, h, pl.ds(column, 1), slice(None))
                    found.append((here, base[here] + inbox[h, pl.ds(row + f * owners, 1), :]))
        for here, value in found:
            field[here] = value

    entry_groups(plan, body)
    span_lat = lon_even.shape[2]
    span_lon = lat_even.shape[2]
    lon_up, lat_up = upward()
    for f in range(fields):
        for h in range(halves):
            low = field[f, h, :span_lat].astype(BF16)
            high = field[f, h, columns_all - span_lat :].astype(BF16)
            lon_even[f, h] = jnp.where(lon_up, high, low)
            lon_odd[f, h] = jnp.where(lon_up, low, high)
            low = field[f, h, pl.ds(0, span_lon, stride=span_lat), :].astype(BF16)
            high = field[f, h, pl.ds(span_lat - 1, span_lon, stride=span_lat), :].astype(BF16)
            lat_even[f, h] = jnp.where(lat_up, high, low)
            lat_odd[f, h] = jnp.where(lat_up, low, high)


def upward():
    return lax.axis_index("gx") % 2 == 0, lax.axis_index("gy") % 2 == 0


def inner_stencil(field, coef, extra, out):
    fields, halves, columns_all, lanes = field.shape
    span_lat, span_lon = coef.shape[1:]
    row = lax.broadcasted_iota(jnp.int32, (span_lat, 1), 0)
    for p in range(span_lon):
        weight = [coef[k, :, p : p + 1] for k in range(4)]
        weight[2] = jnp.where(row == 0, 0.0, weight[2])
        weight[3] = jnp.where(row == span_lat - 1, 0.0, weight[3])
        weight = [jnp.broadcast_to(w, (span_lat, lanes)) for w in weight]
        at = slice(p * span_lat, (p + 1) * span_lat)
        for f in range(fields):
            for h in range(halves):
                here = field[f, h, at]
                total = here + weight[2] * pltpu.roll(here, 1, 0) + weight[3] * pltpu.roll(here, span_lat - 1, 0)
                if p > 0:
                    total = total + weight[0] * field[f, h, (p - 1) * span_lat : p * span_lat]
                if p < span_lon - 1:
                    total = total + weight[1] * field[f, h, (p + 1) * span_lat : (p + 2) * span_lat]
                if extra is None:
                    out[f, h, at] = total
                elif h == 0:
                    out[f, h, at] = total + extra[f, at, :lanes].astype(F32)
                else:
                    tail = extra.shape[2] - lanes
                    out[f, h, at, :tail] = total[:, :tail] + extra[f, at, lanes:].astype(F32)


def inner_first(field, coef, early, out):
    inner_stencil(field, coef, early, out)


def inner_last(field, coef, out):
    inner_stencil(field, coef, None, out)


def edge_weights(coef):
    span_lat, span_lon = coef.shape[1:]
    same = lax.broadcasted_iota(jnp.int32, (span_lon, span_lon), 0) == lax.broadcasted_iota(
        jnp.int32, (span_lon, span_lon), 1
    )

    def upright(line):
        return jnp.sum(jnp.where(same, jnp.broadcast_to(line, (span_lon, span_lon)), 0.0), axis=1, keepdims=True)

    return (
        coef[0, :, :1],
        coef[1, :, span_lon - 1 :],
        upright(coef[2, :1, :]),
        upright(coef[3, span_lat - 1 :, :]),
    )


def add_edges(f, h, weights, lon_even, lon_odd, lat_even, lat_odd, out):
    columns_all = out.shape[2]
    span_lat = lon_even.shape[2]
    span_lon = lat_even.shape[2]
    places = (
        (slice(0, span_lat), slice(None)),
        (slice(columns_all - span_lat, columns_all), slice(None)),
        (pl.ds(0, span_lon, stride=span_lat), slice(None)),
        (pl.ds(span_lat - 1, span_lon, stride=span_lat), slice(None)),
    )
    lon_up, lat_up = upward()
    edges = []
    for up, even, odd in ((lon_up, lon_even, lon_odd), (lat_up, lat_even, lat_odd)):
        first, second = even[f, h].astype(F32), odd[f, h].astype(F32)
        edges += [jnp.where(up, second, first), jnp.where(up, first, second)]
    for place, weight, edge in zip(places, weights, edges):
        at = (f, h) + place
        out[at] = out[at] + weight * edge


def edges_first(plan, inner, coef, lon_even, lon_odd, lat_even, lat_odd, out, outbox, rows):
    fields, halves, columns_all, lanes = out.shape
    owners = rows.shape[1] // (PAIR * fields)
    tail = outbox.shape[1] - lanes
    weights = edge_weights(coef)
    rows[...] = jnp.zeros(rows.shape, F32)
    for f in range(fields):
        for h in range(halves):
            add_edges(f, h, weights, lon_even, lon_odd, lat_even, lat_odd, out)

    def body(entries):
        found = []
        for column, row in entries:
            first = outbox_row(row, owners, fields)
            for f in range(fields):
                for h in range(halves):
                    found.append((h, first + f, out[f, h, pl.ds(column, 1), :]))
        for h, row, value in found:
            rows[h, pl.ds(row, 1), :] = value

    entry_groups(plan, body)
    outbox[:, :lanes] = rows[0].astype(BF16)
    outbox[:, lanes:] = rows[1, :, :tail].astype(BF16)


def edges_last(inner, coef, lon_even, lon_odd, lat_even, lat_odd, out_hbm, both, out, sems):
    fields, halves, columns_all, lanes = inner.shape
    tail = out.shape[2] - lanes
    weights = edge_weights(coef)
    copies = []
    for f in range(fields):
        for h in range(halves):
            both[f, h] = inner[f, h]
            add_edges(f, h, weights, lon_even, lon_odd, lat_even, lat_odd, both)
        out[f, :, :lanes] = both[f, 0]
        out[f, :, lanes:] = both[f, 1, :, :tail]
        copies.append(pltpu.make_async_copy(out.at[f], out_hbm.at[f], sems.at[f]))
        copies[f].start()
    for copy in copies:
        copy.wait()


def exchange(rows, groups):
    width = rows.shape[0] // groups
    moved = lax.all_to_all(
        rows.reshape(groups, width, rows.shape[1]), "gy", split_axis=0, concat_axis=0, tiled=True
    )
    return moved.reshape(rows.shape)


def swap(edge, axis, start, periodic):
    count = lax.axis_size(axis)
    pairs = [(i, i + 1) for i in range(start, count - 1, 2)]
    if start and periodic:
        pairs.append((count - 1, 0))
    return lax.ppermute(edge, axis, pairs + [(high, low) for low, high in pairs])


def halos(lon_even, lon_odd, lat_even, lat_odd):
    return (
        swap(lon_even, "gx", 0, True),
        swap(lon_odd, "gx", 1, True),
        swap(lat_even, "gy", 0, False),
        swap(lat_odd, "gy", 1, False),
    )


def on_device(late, early, stencil_coef, jacobian, cloudy_cols, cloudy_count, owner_rank, owner_slot):
    fields, levels, span_lon, span_lat = late.shape
    groups = lax.axis_size("gy")
    own_slots = jacobian.shape[1]
    capacity = cloudy_cols.shape[2]
    columns_all = span_lon * span_lat
    late = late.transpose(0, 2, 3, 1).reshape(fields, columns_all, levels)
    early = early.transpose(0, 2, 3, 1).reshape(fields, columns_all, levels)
    coef = stencil_coef.transpose(0, 2, 1)
    matrices = jacobian[0].transpose(0, 2, 1, 3)
    shape = jax.ShapeDtypeStruct
    per_owner = PAIR * fields
    inbox_rows = groups * per_owner
    grid = (fields, columns_all, levels)
    halves = (fields, 2, columns_all, LANES)
    plan_shape = shape((2 * capacity + 1,), jnp.int32)

    outbox, plan = call(
        pack_first,
        [shape((inbox_rows, levels + 1), BF16), plan_shape],
        [HBM] * 5,
        [VMEM, SMEM],
        [
            SMEM(cloudy_cols.shape, jnp.int32),
            SMEM(cloudy_count.shape, jnp.int32),
            SMEM(owner_rank.shape, jnp.int32),
            SMEM(owner_slot.shape, jnp.int32),
            VMEM(grid, BF16),
            VMEM(halves, F32),
            VMEM((2, inbox_rows, LANES), F32),
            SMEM((groups,), jnp.int32),
            pltpu.SemaphoreType.DMA((4 + fields,)),
        ],
        vmem=57,
    )(cloudy_cols, cloudy_count, owner_rank, owner_slot, late)
    (field,) = call(widen, [shape(halves, F32)], [VMEM], [VMEM], touched=12000000)(late)
    received = exchange(outbox, groups)
    chosen_shape = shape((inbox_rows, own_slots * fields), BF16)
    answer_shape = shape((groups, (per_owner + 1) * LANES), F32)
    spaces = [
        VMEM((own_slots * fields, levels * fields), F32),
        VMEM((own_slots * fields, 2 * LANES), F32),
    ]
    answer, chosen, answering = call(
        physics_first,
        [answer_shape, chosen_shape, chosen_shape],
        [VMEM] * 2,
        [VMEM] * 3,
        spaces
        + [
            VMEM(chosen_shape.shape, F32),
        ],
    )(received, matrices)
    returned = exchange(answer, groups)

    edge_shapes = [shape((fields, 2, span, LANES), BF16) for span in (span_lat, span_lat, span_lon, span_lon)]

    def add(returned, base):
        return call(
            functools.partial(add_increments, levels=levels),
            [shape(halves, F32)] + edge_shapes,
            [SMEM] + [VMEM] * 2,
            [VMEM] * 5,
            [VMEM((2, inbox_rows, LANES), F32)],
            {2: 0},
        )(plan, returned, base)

    field, *edges = add(returned, field)
    neighbours = halos(*edges)
    (inner,) = call(inner_first, [shape(halves, F32)], [VMEM] * 3, [VMEM], touched=6000000)(field, coef, early)
    adjoint, outbox = call(
        edges_first,
        [shape(halves, F32), shape((inbox_rows, levels), BF16)],
        [SMEM] + [VMEM] * 6,
        [VMEM] * 2,
        [VMEM((2, inbox_rows, LANES), F32)],
        {1: 0},
    )(plan, inner, coef, *neighbours)
    received = exchange(outbox, groups)
    (answer,) = call(physics_second, [answer_shape], [VMEM] * 4, [VMEM], spaces)(
        received, matrices, chosen, answering
    )
    returned = exchange(answer, groups)
    field, *edges = add(returned, adjoint)
    neighbours = halos(*edges)
    (inner,) = call(inner_last, [shape(halves, F32)], [VMEM] * 2, [VMEM], touched=6000000)(field, coef)
    (final,) = call(
        edges_last,
        [shape(grid, F32)],
        [VMEM] * 6,
        [HBM],
        [VMEM(halves, F32), VMEM(grid, F32), pltpu.SemaphoreType.DMA((fields,))],
    )(inner, coef, *neighbours)
    return final.reshape(fields, span_lon, span_lat, levels).transpose(0, 3, 1, 2)


def solution(mesh):
    return jax.shard_map(
        on_device,
        mesh=mesh,
        in_specs=(
            P(None, None, "gx", "gy"),
            P(None, None, "gx", "gy"),
            P(None, "gx", "gy"),
            P("gx", "gy", None, None, None),
            P("gx", "gy", None),
            P("gx", "gy"),
            P("gx", "gy", None),
            P("gx", "gy", None),
        ),
        out_specs=P(None, None, "gx", "gy"),
        check_vma=False,
    )
```

```python
import functools

import jax
import jax.numpy as jnp
from jax import lax
from jax.experimental import pallas as pl
from jax.experimental.pallas import tpu as pltpu
from jax.sharding import PartitionSpec as P

BF16 = jnp.bfloat16
F32 = jnp.float32
VMEM = pltpu.VMEM
SMEM = pltpu.SMEM
HBM = pltpu.HBM
PAIR = 2
LANES = 128
GROUP = 4


def call(kernel, out_shape, in_spaces, out_spaces, scratch=(), aliases=None, flops=1000, touched=1000000, vmem=40):
    return pl.pallas_call(
        kernel,
        out_shape=out_shape,
        in_specs=[pl.BlockSpec(memory_space=space) for space in in_spaces],
        out_specs=[pl.BlockSpec(memory_space=space) for space in out_spaces],
        scratch_shapes=scratch,
        input_output_aliases=aliases or {},
        compiler_params=pltpu.CompilerParams(vmem_limit_bytes=vmem * 1024 * 1024),
        cost_estimate=pl.CostEstimate(flops=flops, bytes_accessed=touched, transcendentals=0),
    )


def entry_groups(plan, body):
    capacity = (plan.shape[0] - 1) // 2

    def step(g, carry):
        first = g * GROUP
        body([(plan[1 + first + i], plan[1 + capacity + first + i]) for i in range(GROUP)])
        return carry

    lax.fori_loop(0, (plan[0] + (GROUP - 1)) // GROUP, step, 0)


def unpack_field(packed, field, f):
    field[f, 0] = packed[f, :, :LANES].astype(F32)
    field[f, 1, :, : packed.shape[2] - LANES] = packed[f, :, LANES:].astype(F32)


def tail_lanes(block, start):
    end = block[:, LANES:]
    return pltpu.roll(end, start, 1) if start else end


def pack_first(
    cols_hbm, count_hbm, owner_hbm, slot_hbm, late_hbm, outbox, plan, cols, count, owner, slot, late, pick, codes, wide, used, sems
):
    fields, _, levels = late.shape
    capacity = cols.shape[2]
    owners = used.shape[0]
    tail = levels - LANES
    small = [(cols_hbm, cols), (count_hbm, count), (owner_hbm, owner), (slot_hbm, slot)]
    copies = [pltpu.make_async_copy(source, target, sems.at[i]) for i, (source, target) in enumerate(small)]
    copies += [pltpu.make_async_copy(late_hbm.at[f], late.at[f], sems.at[len(small) + f]) for f in range(fields)]
    for copy in copies:
        copy.start()
    for o in range(owners):
        used[o] = 0
    pick[...] = jnp.zeros(pick.shape, F32)
    codes[...] = jnp.zeros(codes.shape, F32)
    wide[...] = jnp.zeros(wide.shape, F32)
    for copy in copies[: len(small)]:
        copy.wait()
    live = count[0, 0]
    plan[0] = live
    places = lax.broadcasted_iota(jnp.int32, (1, pick.shape[1]), 1)

    def route(e, carry):
        o = owner[0, 0, e]
        rank = used[o]
        used[o] = rank + 1
        column = cols[0, 0, e]
        plan[1 + e] = column
        plan[1 + capacity + e] = rank * (fields * owners) + o
        pick[pl.ds(o * PAIR + rank, 1), :] = (places == column).astype(F32)
        codes[pl.ds(o * PAIR + rank, 1), :] = jnp.full((1, LANES), slot[0, 0, e] + 1, jnp.int32).astype(F32)
        return carry

    lax.fori_loop(0, live, route, 0)
    whole = (live // GROUP) * GROUP

    def repeat(e, carry):
        for part in (1, 1 + capacity):
            plan[part + e] = plan[part + whole]
        return carry

    lax.fori_loop(live, ((live + (GROUP - 1)) // GROUP) * GROUP, repeat, 0)
    chosen = pick[...].astype(BF16)
    rows, lanes = [], lax.broadcasted_iota(jnp.int32, codes.shape, 1)
    tails = jnp.where(lanes == tail * fields, codes[...], 0.0)
    for f in range(fields):
        copies[len(small) + f].wait()
        wide[:, :levels] = jnp.dot(chosen, late[f], preferred_element_type=F32)
        rows.append(wide[:, :LANES])
        tails = tails + tail_lanes(wide[...], tail * f)
    outbox[...] = jnp.concatenate(rows + [tails], axis=1).astype(BF16).reshape(outbox.shape)


def outbox_row(row, owners, fields):
    rank = row // (fields * owners)
    return (row - rank * (fields * owners)) * PAIR + rank


def split_dot(chosen, value):
    high = value.astype(BF16)
    rest = value - high.astype(F32)
    middle = rest.astype(BF16)
    low = (rest - middle.astype(F32)).astype(BF16)
    dot = functools.partial(jnp.dot, preferred_element_type=F32)
    return dot(chosen, high) + dot(chosen, middle) + dot(chosen, low)


def products(chosen, received, matrices, answer, spread, result):
    own_slots, levels, fields, _ = matrices.shape
    owners = received.shape[0]
    depth = levels * fields
    tail = levels - LANES
    iota = functools.partial(lax.broadcasted_iota, jnp.int32)
    values = received[...].reshape(owners * PAIR, received.shape[2]).astype(F32)
    choice = chosen[...].astype(BF16)
    field_of_row = iota((own_slots * fields, levels), 0) % fields
    placed = jnp.zeros((own_slots * fields, levels), F32)
    tails = values[:, fields * LANES :]
    for f in range(fields):
        end = pltpu.roll(tails, LANES - tail * f, 1) if f else tails
        full = jnp.concatenate([values[:, f * LANES : (f + 1) * LANES], end[:, :tail]], axis=1)
        every = lax.dot_general(
            choice, full.astype(BF16), (((0,), (0,)), ((), ())), preferred_element_type=F32
        )
        placed = jnp.where(field_of_row == f, every, placed)
    spreader = (iota((levels, depth), 1) // fields == iota((levels, depth), 0)).astype(F32).astype(BF16)
    own = iota(spread.shape, 1) % fields == iota(spread.shape, 0) % fields
    spread[...] = jnp.where(own, jnp.dot(placed.astype(BF16), spreader, preferred_element_type=F32), 0.0)
    result[...] = jnp.zeros(result.shape, F32)
    for s in range(own_slots):
        at = slice(s * fields, (s + 1) * fields)
        result[at, :levels] = jnp.dot(
            spread[at].astype(BF16), matrices[s].reshape(depth, levels), preferred_element_type=F32
        )
    backward = []
    for k in range(PAIR):
        rows = chosen[pl.ds(k, owners, stride=PAIR), :][:, : own_slots * fields]
        field_of_lane = iota(rows.shape, 1) % fields
        backward += [jnp.where(field_of_lane == f, rows, 0.0) for f in range(fields)]
    rows = split_dot(jnp.concatenate(backward, axis=0).astype(BF16), result[...])
    blocks = [rows[r * owners : (r + 1) * owners] for r in range(PAIR * fields)]
    tails = tail_lanes(blocks[0], 0)
    for r in range(1, PAIR * fields):
        tails = tails + tail_lanes(blocks[r], tail * r)
    answer[...] = jnp.concatenate([block[:, :LANES] for block in blocks] + [tails], axis=1).reshape(answer.shape)


def physics_first(received, matrices, answer, chosen_out, spread, result):
    own_slots, levels, fields, _ = matrices.shape
    owners = received.shape[0]
    code_lane = fields * levels
    codes = received[...].reshape(owners * PAIR, received.shape[2]).astype(F32)[:, code_lane : code_lane + 1]
    wanted = (lax.broadcasted_iota(jnp.int32, chosen_out.shape, 1) // fields + 1).astype(F32)
    chosen_out[...] = (codes == wanted).astype(F32)
    products(chosen_out, received, matrices, answer, spread, result)


def physics_second(received, matrices, chosen, answer, spread, result):
    products(chosen, received, matrices, answer, spread, result)


def add_first(plan, returned, late, field, *rest, levels):
    for f in range(field.shape[0]):
        unpack_field(late, field, f)
    add_increments(plan, returned, field, field, *rest, levels=levels)


def add_increments(plan, returned, base, field, lon_even, lon_odd, lat_even, lat_odd, inbox, *, levels):
    fields, halves, columns_all, lanes = field.shape
    owners = returned.shape[0]
    per_owner = inbox.shape[1] // owners
    tail = levels - LANES
    lines = returned[...].reshape(owners, returned.shape[2])
    tails = lines[:, per_owner * LANES :]
    for r in range(per_owner):
        inbox[0, r * owners : (r + 1) * owners] = lines[:, r * LANES : (r + 1) * LANES]
        inbox[1, r * owners : (r + 1) * owners] = pltpu.roll(tails, LANES - tail * r, 1) if r else tails

    def body(entries):
        found = []
        for column, row in entries:
            for f in range(fields):
                for h in range(halves):
                    here = (f, h, pl.ds(column, 1), slice(None))
                    found.append((here, base[here] + inbox[h, pl.ds(row + f * owners, 1), :]))
        for here, value in found:
            field[here] = value

    entry_groups(plan, body)
    span_lat = lon_even.shape[2]
    span_lon = lat_even.shape[2]
    lon_up, lat_up = upward()
    for f in range(fields):
        for h in range(halves):
            low = field[f, h, :span_lat].astype(BF16)
            high = field[f, h, columns_all - span_lat :].astype(BF16)
            lon_even[f, h] = jnp.where(lon_up, high, low)
            lon_odd[f, h] = jnp.where(lon_up, low, high)
            low = field[f, h, pl.ds(0, span_lon, stride=span_lat), :].astype(BF16)
            high = field[f, h, pl.ds(span_lat - 1, span_lon, stride=span_lat), :].astype(BF16)
            lat_even[f, h] = jnp.where(lat_up, high, low)
            lat_odd[f, h] = jnp.where(lat_up, low, high)


def upward():
    return lax.axis_index("gx") % 2 == 0, lax.axis_index("gy") % 2 == 0


def inner_stencil(field, coef, extra, out):
    fields, halves, columns_all, lanes = field.shape
    span_lat, span_lon = coef.shape[1:]
    row = lax.broadcasted_iota(jnp.int32, (span_lat, 1), 0)
    for p in range(span_lon):
        weight = [coef[k, :, p : p + 1] for k in range(4)]
        weight[2] = jnp.where(row == 0, 0.0, weight[2])
        weight[3] = jnp.where(row == span_lat - 1, 0.0, weight[3])
        weight = [jnp.broadcast_to(w, (span_lat, lanes)) for w in weight]
        at = slice(p * span_lat, (p + 1) * span_lat)
        for f in range(fields):
            for h in range(halves):
                here = field[f, h, at]
                total = here + weight[2] * pltpu.roll(here, 1, 0) + weight[3] * pltpu.roll(here, span_lat - 1, 0)
                if p > 0:
                    total = total + weight[0] * field[f, h, (p - 1) * span_lat : p * span_lat]
                if p < span_lon - 1:
                    total = total + weight[1] * field[f, h, (p + 1) * span_lat : (p + 2) * span_lat]
                if extra is None:
                    out[f, h, at] = total
                elif h == 0:
                    out[f, h, at] = total + extra[f, at, :lanes].astype(F32)
                else:
                    tail = extra.shape[2] - lanes
                    out[f, h, at, :tail] = total[:, :tail] + extra[f, at, lanes:].astype(F32)


def inner_first(field, coef, early, out):
    inner_stencil(field, coef, early, out)


def inner_last(field, coef, out):
    inner_stencil(field, coef, None, out)


def edge_weights(coef):
    span_lat, span_lon = coef.shape[1:]
    same = lax.broadcasted_iota(jnp.int32, (span_lon, span_lon), 0) == lax.broadcasted_iota(
        jnp.int32, (span_lon, span_lon), 1
    )

    def upright(line):
        return jnp.sum(jnp.where(same, jnp.broadcast_to(line, (span_lon, span_lon)), 0.0), axis=1, keepdims=True)

    return (
        coef[0, :, :1],
        coef[1, :, span_lon - 1 :],
        upright(coef[2, :1, :]),
        upright(coef[3, span_lat - 1 :, :]),
    )


def add_edges(f, h, weights, lon_even, lon_odd, lat_even, lat_odd, out):
    columns_all = out.shape[2]
    span_lat = lon_even.shape[2]
    span_lon = lat_even.shape[2]
    places = (
        (slice(0, span_lat), slice(None)),
        (slice(columns_all - span_lat, columns_all), slice(None)),
        (pl.ds(0, span_lon, stride=span_lat), slice(None)),
        (pl.ds(span_lat - 1, span_lon, stride=span_lat), slice(None)),
    )
    lon_up, lat_up = upward()
    edges = []
    for up, even, odd in ((lon_up, lon_even, lon_odd), (lat_up, lat_even, lat_odd)):
        first, second = even[f, h].astype(F32), odd[f, h].astype(F32)
        edges += [jnp.where(up, second, first), jnp.where(up, first, second)]
    for place, weight, edge in zip(places, weights, edges):
        at = (f, h) + place
        out[at] = out[at] + weight * edge


def edges_first(plan, inner, coef, lon_even, lon_odd, lat_even, lat_odd, out, outbox, rows, *, levels):
    fields, halves, columns_all, lanes = out.shape
    owners = outbox.shape[0]
    tail = levels - lanes
    weights = edge_weights(coef)
    rows[...] = jnp.zeros(rows.shape, F32)
    for f in range(fields):
        for h in range(halves):
            add_edges(f, h, weights, lon_even, lon_odd, lat_even, lat_odd, out)

    def body(entries):
        found = []
        for column, row in entries:
            at = outbox_row(row, owners, fields)
            for f in range(fields):
                for h in range(halves):
                    found.append((h, f * (PAIR * owners) + at, out[f, h, pl.ds(column, 1), :]))
        for h, row, value in found:
            rows[h, pl.ds(row, 1), :] = value

    entry_groups(plan, body)
    blocks = [slice(f * PAIR * owners, (f + 1) * PAIR * owners) for f in range(fields)]
    lane = lax.broadcasted_iota(jnp.int32, (PAIR * owners, lanes), 1)
    tails = jnp.zeros((PAIR * owners, lanes), F32)
    for f in range(fields):
        end = jnp.where(lane < tail, rows[1, blocks[f]], 0.0)
        tails = tails + (pltpu.roll(end, tail * f, 1) if f else end)
    packed = jnp.concatenate([rows[0, block] for block in blocks] + [tails], axis=1)
    outbox[...] = packed.astype(BF16).reshape(outbox.shape)


def edges_last(inner, coef, lon_even, lon_odd, lat_even, lat_odd, out_hbm, both, out, sems):
    fields, halves, columns_all, lanes = inner.shape
    tail = out.shape[2] - lanes
    weights = edge_weights(coef)
    copies = []
    for f in range(fields):
        for h in range(halves):
            both[f, h] = inner[f, h]
            add_edges(f, h, weights, lon_even, lon_odd, lat_even, lat_odd, both)
        out[f, :, :lanes] = both[f, 0]
        out[f, :, lanes:] = both[f, 1, :, :tail]
        copies.append(pltpu.make_async_copy(out.at[f], out_hbm.at[f], sems.at[f]))
        copies[f].start()
    for copy in copies:
        copy.wait()


def exchange(lines):
    return lax.all_to_all(lines, "gy", split_axis=0, concat_axis=0, tiled=True)


def swap(edge, axis, start, periodic):
    count = lax.axis_size(axis)
    pairs = [(i, i + 1) for i in range(start, count - 1, 2)]
    if start and periodic:
        pairs.append((count - 1, 0))
    return lax.ppermute(edge, axis, pairs + [(high, low) for low, high in pairs])


def halos(lon_even, lon_odd, lat_even, lat_odd):
    return (
        swap(lon_even, "gx", 0, True),
        swap(lon_odd, "gx", 1, True),
        swap(lat_even, "gy", 0, False),
        swap(lat_odd, "gy", 1, False),
    )


def on_device(late, early, stencil_coef, jacobian, cloudy_cols, cloudy_count, owner_rank, owner_slot):
    fields, levels, span_lon, span_lat = late.shape
    groups = lax.axis_size("gy")
    own_slots = jacobian.shape[1]
    capacity = cloudy_cols.shape[2]
    columns_all = span_lon * span_lat
    late = late.transpose(0, 2, 3, 1).reshape(fields, columns_all, levels)
    early = early.transpose(0, 2, 3, 1).reshape(fields, columns_all, levels)
    coef = stencil_coef.transpose(0, 2, 1)
    matrices = jacobian[0].transpose(0, 2, 1, 3)
    shape = jax.ShapeDtypeStruct
    per_owner = PAIR * fields
    inbox_rows = groups * per_owner
    grid = (fields, columns_all, levels)
    halves = (fields, 2, columns_all, LANES)
    plan_shape = shape((2 * capacity + 1,), jnp.int32)

    outbox_shape = shape((groups, PAIR, (fields + 1) * LANES), BF16)
    outbox, plan = call(
        pack_first,
        [outbox_shape, plan_shape],
        [HBM] * 5,
        [VMEM, SMEM],
        [
            SMEM(cloudy_cols.shape, jnp.int32),
            SMEM(cloudy_count.shape, jnp.int32),
            SMEM(owner_rank.shape, jnp.int32),
            SMEM(owner_slot.shape, jnp.int32),
            VMEM(grid, BF16),
            VMEM((groups * PAIR, columns_all), F32),
            VMEM((groups * PAIR, LANES), F32),
            VMEM((groups * PAIR, 2 * LANES), F32),
            SMEM((groups,), jnp.int32),
            pltpu.SemaphoreType.DMA((4 + fields,)),
        ],
        vmem=57,
    )(cloudy_cols, cloudy_count, owner_rank, owner_slot, late)
    chosen_shape = shape((groups * PAIR, own_slots * fields), F32)
    answer_shape = shape((groups, 1, (per_owner + 1) * LANES), F32)
    spaces = [
        VMEM((own_slots * fields, levels * fields), F32),
        VMEM((own_slots * fields, 2 * LANES), F32),
    ]
    answer, chosen = call(physics_first, [answer_shape, chosen_shape], [VMEM] * 2, [VMEM] * 2, spaces)(
        exchange(outbox), matrices
    )
    returned = exchange(answer)

    edge_shapes = [shape((fields, 2, span, LANES), BF16) for span in (span_lat, span_lat, span_lon, span_lon)]

    def add(kernel, returned, base, aliases):
        return call(
            functools.partial(kernel, levels=levels),
            [shape(halves, F32)] + edge_shapes,
            [SMEM] + [VMEM] * 2,
            [VMEM] * 5,
            [VMEM((2, inbox_rows, LANES), F32)],
            aliases,
        )(plan, returned, base)

    field, *edges = add(add_first, returned, late, {})
    neighbours = halos(*edges)
    (inner,) = call(inner_first, [shape(halves, F32)], [VMEM] * 3, [VMEM], touched=6000000)(field, coef, early)
    adjoint, outbox = call(
        functools.partial(edges_first, levels=levels),
        [shape(halves, F32), outbox_shape],
        [SMEM] + [VMEM] * 6,
        [VMEM] * 2,
        [VMEM((2, inbox_rows, LANES), F32)],
        {1: 0},
    )(plan, inner, coef, *neighbours)
    (answer,) = call(physics_second, [answer_shape], [VMEM] * 3, [VMEM], spaces)(
        exchange(outbox), matrices, chosen
    )
    field, *edges = add(add_increments, exchange(answer), adjoint, {2: 0})
    neighbours = halos(*edges)
    (inner,) = call(inner_last, [shape(halves, F32)], [VMEM] * 2, [VMEM], touched=6000000)(field, coef)
    (final,) = call(
        edges_last,
        [shape(grid, F32)],
        [VMEM] * 6,
        [HBM],
        [VMEM(halves, F32), VMEM(grid, F32), pltpu.SemaphoreType.DMA((fields,))],
    )(inner, coef, *neighbours)
    return final.reshape(fields, span_lon, span_lat, levels).transpose(0, 3, 1, 2)


def solution(mesh):
    return jax.shard_map(
        on_device,
        mesh=mesh,
        in_specs=(
            P(None, None, "gx", "gy"),
            P(None, None, "gx", "gy"),
            P(None, "gx", "gy"),
            P("gx", "gy", None, None, None),
            P("gx", "gy", None),
            P("gx", "gy"),
            P("gx", "gy", None),
            P("gx", "gy", None),
        ),
        out_specs=P(None, None, "gx", "gy"),
        check_vma=False,
    )
```

```python
import functools

import jax
import jax.numpy as jnp
from jax import lax
from jax.experimental import pallas as pl
from jax.experimental.pallas import tpu as pltpu
from jax.sharding import PartitionSpec as P

BF16 = jnp.bfloat16
F32 = jnp.float32
VMEM = pltpu.VMEM
SMEM = pltpu.SMEM
HBM = pltpu.HBM
PAIR = 2
LANES = 128
GROUP = 4


def call(kernel, out_shape, in_spaces, out_spaces, scratch=(), aliases=None, flops=1000, touched=1000000, vmem=40):
    return pl.pallas_call(
        kernel,
        out_shape=out_shape,
        in_specs=[pl.BlockSpec(memory_space=space) for space in in_spaces],
        out_specs=[pl.BlockSpec(memory_space=space) for space in out_spaces],
        scratch_shapes=scratch,
        input_output_aliases=aliases or {},
        compiler_params=pltpu.CompilerParams(vmem_limit_bytes=vmem * 1024 * 1024),
        cost_estimate=pl.CostEstimate(flops=flops, bytes_accessed=touched, transcendentals=0),
    )


def entry_groups(plan, body):
    capacity = (plan.shape[0] - 1) // 2

    def step(g, carry):
        first = g * GROUP
        body([(plan[1 + first + i], plan[1 + capacity + first + i]) for i in range(GROUP)])
        return carry

    lax.fori_loop(0, (plan[0] + (GROUP - 1)) // GROUP, step, 0)


def unpack_field(packed, field, f):
    field[f, 0] = packed[f, :, :LANES].astype(F32)
    field[f, 1, :, : packed.shape[2] - LANES] = packed[f, :, LANES:].astype(F32)


def tail_lanes(block, start):
    end = block[:, LANES:]
    return pltpu.roll(end, start, 1) if start else end


def pack_first(
    cols_hbm, count_hbm, owner_hbm, slot_hbm, late_hbm, outbox, plan, cols, count, owner, slot, late, field, rows, codes, used, sems
):
    fields, _, levels = late.shape
    capacity = cols.shape[2]
    owners = used.shape[0]
    tail = levels - LANES
    small = [(cols_hbm, cols), (count_hbm, count), (owner_hbm, owner), (slot_hbm, slot)]
    copies = [pltpu.make_async_copy(source, target, sems.at[i]) for i, (source, target) in enumerate(small)]
    copies += [pltpu.make_async_copy(late_hbm.at[f], late.at[f], sems.at[len(small) + f]) for f in range(fields)]
    for copy in copies:
        copy.start()
    for o in range(owners):
        used[o] = 0
    rows[...] = jnp.zeros(rows.shape, F32)
    codes[...] = jnp.zeros(codes.shape, F32)
    for copy in copies[: len(small)]:
        copy.wait()
    live = count[0, 0]
    plan[0] = live

    def route(e, carry):
        o = owner[0, 0, e]
        rank = used[o]
        used[o] = rank + 1
        plan[1 + e] = cols[0, 0, e]
        plan[1 + capacity + e] = rank * (fields * owners) + o
        codes[pl.ds(o * PAIR + rank, 1), :] = jnp.full((1, LANES), slot[0, 0, e] + 1, jnp.int32).astype(F32)
        return carry

    lax.fori_loop(0, live, route, 0)
    whole = (live // GROUP) * GROUP

    def repeat(e, carry):
        for part in (1, 1 + capacity):
            plan[part + e] = plan[part + whole]
        return carry

    lax.fori_loop(live, ((live + (GROUP - 1)) // GROUP) * GROUP, repeat, 0)
    for f in range(fields):
        copies[len(small) + f].wait()
        unpack_field(late, field, f)
    gather_columns(plan, field, rows, owners)
    lane = lax.broadcasted_iota(jnp.int32, codes.shape, 1)
    pack_rows(rows, jnp.where(lane == tail * fields, codes[...], 0.0), tail, outbox)


def gather_columns(plan, field, rows, owners):
    fields, halves = field.shape[:2]

    def body(entries):
        found = []
        for column, row in entries:
            at = outbox_row(row, owners, fields)
            for f in range(fields):
                for h in range(halves):
                    found.append((h, f * (PAIR * owners) + at, field[f, h, pl.ds(column, 1), :]))
        for h, row, value in found:
            rows[h, pl.ds(row, 1), :] = value

    entry_groups(plan, body)


def pack_rows(rows, tails, tail, outbox):
    count = outbox.shape[0] * outbox.shape[1]
    blocks = [slice(f * count, (f + 1) * count) for f in range(rows.shape[1] // count)]
    tails = tails + side_by_side([rows[1, block] for block in blocks], tail)
    packed = jnp.concatenate([rows[0, block] for block in blocks] + [tails], axis=1)
    outbox[...] = packed.astype(BF16).reshape(outbox.shape)


def side_by_side(ends, tail):
    lane = lax.broadcasted_iota(jnp.int32, ends[0].shape, 1)
    total = jnp.zeros(ends[0].shape, F32)
    for f, end in enumerate(ends):
        end = jnp.where(lane < tail, end, 0.0)
        total = total + (pltpu.roll(end, tail * f, 1) if f else end)
    return total


def outbox_row(row, owners, fields):
    rank = row // (fields * owners)
    return (row - rank * (fields * owners)) * PAIR + rank


def split_dot(chosen, value):
    high = value.astype(BF16)
    rest = value - high.astype(F32)
    middle = rest.astype(BF16)
    low = (rest - middle.astype(F32)).astype(BF16)
    dot = functools.partial(jnp.dot, preferred_element_type=F32)
    return dot(chosen, high) + dot(chosen, middle) + dot(chosen, low)


def products(chosen, received, matrices, answer, spread, result):
    own_slots, levels, fields, _ = matrices.shape
    owners = received.shape[0]
    depth = levels * fields
    tail = levels - LANES
    iota = functools.partial(lax.broadcasted_iota, jnp.int32)
    values = received[...].reshape(owners * PAIR, received.shape[2]).astype(F32)
    choice = chosen[...].astype(BF16)
    field_of_row = iota((own_slots * fields, levels), 0) % fields
    placed = jnp.zeros((own_slots * fields, levels), F32)
    tails = values[:, fields * LANES :]
    for f in range(fields):
        end = pltpu.roll(tails, LANES - tail * f, 1) if f else tails
        full = jnp.concatenate([values[:, f * LANES : (f + 1) * LANES], end[:, :tail]], axis=1)
        every = lax.dot_general(
            choice, full.astype(BF16), (((0,), (0,)), ((), ())), preferred_element_type=F32
        )
        placed = jnp.where(field_of_row == f, every, placed)
    spreader = (iota((levels, depth), 1) // fields == iota((levels, depth), 0)).astype(F32).astype(BF16)
    own = iota(spread.shape, 1) % fields == iota(spread.shape, 0) % fields
    spread[...] = jnp.where(own, jnp.dot(placed.astype(BF16), spreader, preferred_element_type=F32), 0.0)
    result[...] = jnp.zeros(result.shape, F32)
    for s in range(own_slots):
        at = slice(s * fields, (s + 1) * fields)
        result[at, :levels] = jnp.dot(
            spread[at].astype(BF16), matrices[s].reshape(depth, levels), preferred_element_type=F32
        )
    backward = []
    for k in range(PAIR):
        rows = chosen[pl.ds(k, owners, stride=PAIR), :][:, : own_slots * fields]
        field_of_lane = iota(rows.shape, 1) % fields
        backward += [jnp.where(field_of_lane == f, rows, 0.0) for f in range(fields)]
    rows = split_dot(jnp.concatenate(backward, axis=0).astype(BF16), result[...])
    blocks = [rows[r * owners : (r + 1) * owners] for r in range(PAIR * fields)]
    tails = tail_lanes(blocks[0], 0)
    for r in range(1, PAIR * fields):
        tails = tails + tail_lanes(blocks[r], tail * r)
    answer[...] = jnp.concatenate([block[:, :LANES] for block in blocks] + [tails], axis=1).reshape(answer.shape)


def physics_first(received, matrices, answer, chosen_out, spread, result):
    own_slots, levels, fields, _ = matrices.shape
    owners = received.shape[0]
    code_lane = fields * levels
    codes = received[...].reshape(owners * PAIR, received.shape[2]).astype(F32)[:, code_lane : code_lane + 1]
    wanted = (lax.broadcasted_iota(jnp.int32, chosen_out.shape, 1) // fields + 1).astype(F32)
    chosen_out[...] = (codes == wanted).astype(F32)
    products(chosen_out, received, matrices, answer, spread, result)


def physics_second(received, matrices, chosen, answer, spread, result):
    products(chosen, received, matrices, answer, spread, result)


def add_first(plan, returned, late, field, *rest, levels):
    for f in range(field.shape[0]):
        unpack_field(late, field, f)
    add_increments(plan, returned, field, field, *rest, levels=levels)


def add_increments(plan, returned, base, field, lon_even, lon_odd, lat_even, lat_odd, inbox, *, levels):
    fields, halves, columns_all, lanes = field.shape
    owners = returned.shape[0]
    per_owner = inbox.shape[1] // owners
    tail = levels - LANES
    lines = returned[...].reshape(owners, returned.shape[2])
    tails = lines[:, per_owner * LANES :]
    for r in range(per_owner):
        inbox[0, r * owners : (r + 1) * owners] = lines[:, r * LANES : (r + 1) * LANES]
        inbox[1, r * owners : (r + 1) * owners] = pltpu.roll(tails, LANES - tail * r, 1) if r else tails

    def body(entries):
        found = []
        for column, row in entries:
            for f in range(fields):
                for h in range(halves):
                    here = (f, h, pl.ds(column, 1), slice(None))
                    found.append((here, base[here] + inbox[h, pl.ds(row + f * owners, 1), :]))
        for here, value in found:
            field[here] = value

    entry_groups(plan, body)
    span_lon = lat_even.shape[1]
    span_lat = columns_all // span_lon
    lon_up, lat_up = upward()
    places = edge_places(columns_all, span_lon)
    lon_low, lon_high, lat_low, lat_high = [edge_blocks(field, place, tail) for place in places]
    for up, even, odd, lows, highs in (
        (lon_up, lon_even, lon_odd, lon_low, lon_high),
        (lat_up, lat_even, lat_odd, lat_low, lat_high),
    ):
        for block, (low, high) in enumerate(zip(lows, highs)):
            even[block, : low.shape[0]] = jnp.where(up, high, low).astype(BF16)
            odd[block, : low.shape[0]] = jnp.where(up, low, high).astype(BF16)


def edge_places(columns_all, span_lon):
    span_lat = columns_all // span_lon
    return (
        slice(0, span_lat),
        slice(columns_all - span_lat, columns_all),
        pl.ds(0, span_lon, stride=span_lat),
        pl.ds(span_lat - 1, span_lon, stride=span_lat),
    )


def edge_blocks(field, place, tail):
    fields = field.shape[0]
    return [field[f, 0, place, :] for f in range(fields)] + [
        side_by_side([field[f, 1, place, :] for f in range(fields)], tail)
    ]


def upward():
    return lax.axis_index("gx") % 2 == 0, lax.axis_index("gy") % 2 == 0


def inner_stencil(field, coef, extra, out):
    fields, halves, columns_all, lanes = field.shape
    span_lat, span_lon = coef.shape[1:]
    row = lax.broadcasted_iota(jnp.int32, (span_lat, 1), 0)
    for p in range(span_lon):
        weight = [coef[k, :, p : p + 1] for k in range(4)]
        weight[2] = jnp.where(row == 0, 0.0, weight[2])
        weight[3] = jnp.where(row == span_lat - 1, 0.0, weight[3])
        weight = [jnp.broadcast_to(w, (span_lat, lanes)) for w in weight]
        at = slice(p * span_lat, (p + 1) * span_lat)
        for f in range(fields):
            for h in range(halves):
                here = field[f, h, at]
                total = here + weight[2] * pltpu.roll(here, 1, 0) + weight[3] * pltpu.roll(here, span_lat - 1, 0)
                if p > 0:
                    total = total + weight[0] * field[f, h, (p - 1) * span_lat : p * span_lat]
                if p < span_lon - 1:
                    total = total + weight[1] * field[f, h, (p + 1) * span_lat : (p + 2) * span_lat]
                if extra is None:
                    out[f, h, at] = total
                elif h == 0:
                    out[f, h, at] = total + extra[f, at, :lanes].astype(F32)
                else:
                    tail = extra.shape[2] - lanes
                    out[f, h, at, :tail] = total[:, :tail] + extra[f, at, lanes:].astype(F32)


def inner_first(field, coef, early, out):
    inner_stencil(field, coef, early, out)


def inner_last(field, coef, out):
    inner_stencil(field, coef, None, out)


def edge_weights(coef):
    span_lat, span_lon = coef.shape[1:]
    same = lax.broadcasted_iota(jnp.int32, (span_lon, span_lon), 0) == lax.broadcasted_iota(
        jnp.int32, (span_lon, span_lon), 1
    )

    def upright(line):
        return jnp.sum(jnp.where(same, jnp.broadcast_to(line, (span_lon, span_lon)), 0.0), axis=1, keepdims=True)

    return (
        coef[0, :, :1],
        coef[1, :, span_lon - 1 :],
        upright(coef[2, :1, :]),
        upright(coef[3, span_lat - 1 :, :]),
    )


def add_edges(f, weights, lon_even, lon_odd, lat_even, lat_odd, out, tail):
    fields, _, columns_all, lanes = out.shape
    span_lon = lat_even.shape[1]
    span_lat = columns_all // span_lon
    lon_up, lat_up = upward()
    for h, block in ((0, f), (1, fields)):
        edges = []
        for up, even, odd, count in ((lon_up, lon_even, lon_odd, span_lat), (lat_up, lat_even, lat_odd, span_lon)):
            first, second = even[block, :count].astype(F32), odd[block, :count].astype(F32)
            if h and f:
                first, second = [pltpu.roll(edge, lanes - tail * f, 1) for edge in (first, second)]
            edges += [jnp.where(up, second, first), jnp.where(up, first, second)]
        for place, weight, edge in zip(edge_places(columns_all, span_lon), weights, edges):
            at = (f, h, place, slice(None))
            out[at] = out[at] + weight * edge


def edges_first(plan, inner, coef, lon_odd, lon_even, lat_odd, lat_even, out, outbox, rows, *, levels):
    fields, halves, columns_all, lanes = out.shape
    owners = outbox.shape[0]
    tail = levels - lanes
    weights = edge_weights(coef)
    rows[...] = jnp.zeros(rows.shape, F32)
    for f in range(fields):
        add_edges(f, weights, lon_even, lon_odd, lat_even, lat_odd, out, tail)

    gather_columns(plan, out, rows, owners)
    pack_rows(rows, 0.0, tail, outbox)


def edges_last(inner, coef, lon_odd, lon_even, lat_odd, lat_even, out_hbm, both, out, sems):
    fields, halves, columns_all, lanes = inner.shape
    tail = out.shape[2] - lanes
    weights = edge_weights(coef)
    copies = []
    for f in range(fields):
        both[f] = inner[f]
        add_edges(f, weights, lon_even, lon_odd, lat_even, lat_odd, both, tail)
        out[f, :, :lanes] = both[f, 0]
        out[f, :, lanes:] = both[f, 1, :, :tail]
        copies.append(pltpu.make_async_copy(out.at[f], out_hbm.at[f], sems.at[f]))
        copies[f].start()
    for copy in copies:
        copy.wait()


def exchange(lines):
    return lax.all_to_all(lines, "gy", split_axis=0, concat_axis=0, tiled=True)


def swap(edge, axis, start, periodic):
    count = lax.axis_size(axis)
    pairs = [(i, i + 1) for i in range(start, count - 1, 2)]
    if start and periodic:
        pairs.append((count - 1, 0))
    return lax.ppermute(edge, axis, pairs + [(high, low) for low, high in pairs])


def halos(lon_even, lon_odd, lat_even, lat_odd):
    lon_odd = swap(lon_odd, "gx", 1, True)
    lon_even = swap(lon_even, "gx", 0, True)
    lat_odd = swap(lat_odd, "gy", 1, False)
    lat_even = swap(lat_even, "gy", 0, False)
    return lon_odd, lon_even, lat_odd, lat_even


def on_device(late, early, stencil_coef, jacobian, cloudy_cols, cloudy_count, owner_rank, owner_slot):
    fields, levels, span_lon, span_lat = late.shape
    groups = lax.axis_size("gy")
    own_slots = jacobian.shape[1]
    capacity = cloudy_cols.shape[2]
    columns_all = span_lon * span_lat
    late = late.transpose(0, 2, 3, 1).reshape(fields, columns_all, levels)
    early = early.transpose(0, 2, 3, 1).reshape(fields, columns_all, levels)
    coef = stencil_coef.transpose(0, 2, 1)
    matrices = jacobian[0].transpose(0, 2, 1, 3)
    shape = jax.ShapeDtypeStruct
    per_owner = PAIR * fields
    inbox_rows = groups * per_owner
    grid = (fields, columns_all, levels)
    halves = (fields, 2, columns_all, LANES)
    plan_shape = shape((2 * capacity + 1,), jnp.int32)

    outbox_shape = shape((groups, PAIR, (fields + 1) * LANES), BF16)
    outbox, plan = call(
        pack_first,
        [outbox_shape, plan_shape],
        [HBM] * 5,
        [VMEM, SMEM],
        [
            SMEM(cloudy_cols.shape, jnp.int32),
            SMEM(cloudy_count.shape, jnp.int32),
            SMEM(owner_rank.shape, jnp.int32),
            SMEM(owner_slot.shape, jnp.int32),
            VMEM(grid, BF16),
            VMEM(halves, F32),
            VMEM((2, inbox_rows, LANES), F32),
            VMEM((groups * PAIR, LANES), F32),
            SMEM((groups,), jnp.int32),
            pltpu.SemaphoreType.DMA((4 + fields,)),
        ],
        vmem=57,
    )(cloudy_cols, cloudy_count, owner_rank, owner_slot, late)
    chosen_shape = shape((groups * PAIR, own_slots * fields), F32)
    answer_shape = shape((groups, 1, (per_owner + 1) * LANES), F32)
    spaces = [
        VMEM((own_slots * fields, levels * fields), F32),
        VMEM((own_slots * fields, 2 * LANES), F32),
    ]
    answer, chosen = call(physics_first, [answer_shape, chosen_shape], [VMEM] * 2, [VMEM] * 2, spaces)(
        exchange(outbox), matrices
    )
    returned = exchange(answer)

    edge_shapes = [shape((fields + 1, span_lon, LANES), BF16)] * 4

    def add(kernel, returned, base, aliases):
        return call(
            functools.partial(kernel, levels=levels),
            [shape(halves, F32)] + edge_shapes,
            [SMEM] + [VMEM] * 2,
            [VMEM] * 5,
            [VMEM((2, inbox_rows, LANES), F32)],
            aliases,
        )(plan, returned, base)

    field, *edges = add(add_first, returned, late, {})
    neighbours = halos(*edges)
    (inner,) = call(inner_first, [shape(halves, F32)], [VMEM] * 3, [VMEM], touched=6000000)(field, coef, early)
    adjoint, outbox = call(
        functools.partial(edges_first, levels=levels),
        [shape(halves, F32), outbox_shape],
        [SMEM] + [VMEM] * 6,
        [VMEM] * 2,
        [VMEM((2, inbox_rows, LANES), F32)],
        {1: 0},
    )(plan, inner, coef, *neighbours)
    (answer,) = call(physics_second, [answer_shape], [VMEM] * 3, [VMEM], spaces)(
        exchange(outbox), matrices, chosen
    )
    field, *edges = add(add_increments, exchange(answer), adjoint, {2: 0})
    neighbours = halos(*edges)
    (inner,) = call(inner_last, [shape(halves, F32)], [VMEM] * 2, [VMEM], touched=6000000)(field, coef)
    (final,) = call(
        edges_last,
        [shape(grid, F32)],
        [VMEM] * 6,
        [HBM],
        [VMEM(halves, F32), VMEM(grid, F32), pltpu.SemaphoreType.DMA((fields,))],
    )(inner, coef, *neighbours)
    return final.reshape(fields, span_lon, span_lat, levels).transpose(0, 3, 1, 2)


def solution(mesh):
    return jax.shard_map(
        on_device,
        mesh=mesh,
        in_specs=(
            P(None, None, "gx", "gy"),
            P(None, None, "gx", "gy"),
            P(None, "gx", "gy"),
            P("gx", "gy", None, None, None),
            P("gx", "gy", None),
            P("gx", "gy"),
            P("gx", "gy", None),
            P("gx", "gy", None),
        ),
        out_specs=P(None, None, "gx", "gy"),
        check_vma=False,
    )
```

```python
import functools

import jax
import jax.numpy as jnp
from jax import lax
from jax.experimental import pallas as pl
from jax.experimental.pallas import tpu as pltpu
from jax.sharding import PartitionSpec as P

BF16 = jnp.bfloat16
F32 = jnp.float32
VMEM = pltpu.VMEM
SMEM = pltpu.SMEM
HBM = pltpu.HBM
PAIR = 2
LANES = 128
GROUP = 4


def call(kernel, out_shape, in_spaces, out_spaces, scratch=(), aliases=None, flops=1000, touched=1000000, vmem=40):
    return pl.pallas_call(
        kernel,
        out_shape=out_shape,
        in_specs=[pl.BlockSpec(memory_space=space) for space in in_spaces],
        out_specs=[pl.BlockSpec(memory_space=space) for space in out_spaces],
        scratch_shapes=scratch,
        input_output_aliases=aliases or {},
        compiler_params=pltpu.CompilerParams(vmem_limit_bytes=vmem * 1024 * 1024),
        cost_estimate=pl.CostEstimate(flops=flops, bytes_accessed=touched, transcendentals=0),
    )


def entry_groups(plan, body):
    capacity = (plan.shape[0] - 1) // 2

    def step(g, carry):
        first = g * GROUP
        body([(plan[1 + first + i], plan[1 + capacity + first + i]) for i in range(GROUP)])
        return carry

    lax.fori_loop(0, (plan[0] + (GROUP - 1)) // GROUP, step, 0)


def unpack_field(packed, field, f):
    field[f, 0] = packed[f, :, :LANES].astype(F32)
    field[f, 1, :, : packed.shape[2] - LANES] = packed[f, :, LANES:].astype(F32)


def tail_lanes(block, start):
    end = block[:, LANES:]
    return pltpu.roll(end, start, 1) if start else end


def pack_first(
    cols_hbm, count_hbm, owner_hbm, slot_hbm, late_hbm, outbox, plan, cols, count, owner, slot, late, field, rows, codes, used, sems
):
    fields, _, levels = late.shape
    capacity = cols.shape[2]
    owners = used.shape[0]
    tail = levels - LANES
    small = [(cols_hbm, cols), (count_hbm, count), (owner_hbm, owner), (slot_hbm, slot)]
    copies = [pltpu.make_async_copy(source, target, sems.at[i]) for i, (source, target) in enumerate(small)]
    copies += [pltpu.make_async_copy(late_hbm.at[f], late.at[f], sems.at[len(small) + f]) for f in range(fields)]
    for copy in copies:
        copy.start()
    for o in range(owners):
        used[o] = 0
    rows[...] = jnp.zeros(rows.shape, F32)
    codes[...] = jnp.zeros(codes.shape, F32)
    for copy in copies[: len(small)]:
        copy.wait()
    live = count[0, 0]
    plan[0] = live

    def route(e, carry):
        o = owner[0, 0, e]
        rank = used[o]
        used[o] = rank + 1
        plan[1 + e] = cols[0, 0, e]
        plan[1 + capacity + e] = rank * (fields * owners) + o
        codes[pl.ds(o * PAIR + rank, 1), :] = jnp.full((1, LANES), slot[0, 0, e] + 1, jnp.int32).astype(F32)
        return carry

    lax.fori_loop(0, live, route, 0)
    whole = (live // GROUP) * GROUP

    def repeat(e, carry):
        for part in (1, 1 + capacity):
            plan[part + e] = plan[part + whole]
        return carry

    lax.fori_loop(live, ((live + (GROUP - 1)) // GROUP) * GROUP, repeat, 0)
    for f in range(fields):
        copies[len(small) + f].wait()
        unpack_field(late, field, f)
    gather_columns(plan, field, rows, owners)
    lane = lax.broadcasted_iota(jnp.int32, codes.shape, 1)
    pack_rows(rows, jnp.where(lane == tail * fields, codes[...], 0.0), tail, outbox)


def gather_columns(plan, field, rows, owners):
    fields, halves = field.shape[:2]

    def body(entries):
        found = []
        for column, row in entries:
            at = outbox_row(row, owners, fields)
            for f in range(fields):
                for h in range(halves):
                    found.append((h, f * (PAIR * owners) + at, field[f, h, pl.ds(column, 1), :]))
        for h, row, value in found:
            rows[h, pl.ds(row, 1), :] = value

    entry_groups(plan, body)


def pack_rows(rows, tails, tail, outbox):
    count = outbox.shape[0] * outbox.shape[1]
    blocks = [slice(f * count, (f + 1) * count) for f in range(rows.shape[1] // count)]
    tails = tails + side_by_side([rows[1, block] for block in blocks], tail)
    packed = jnp.concatenate([rows[0, block] for block in blocks] + [tails], axis=1)
    outbox[...] = packed.astype(BF16).reshape(outbox.shape)


def side_by_side(ends, tail):
    lane = lax.broadcasted_iota(jnp.int32, ends[0].shape, 1)
    total = jnp.zeros(ends[0].shape, F32)
    for f, end in enumerate(ends):
        end = jnp.where(lane < tail, end, 0.0)
        total = total + (pltpu.roll(end, tail * f, 1) if f else end)
    return total


def outbox_row(row, owners, fields):
    rank = row // (fields * owners)
    return (row - rank * (fields * owners)) * PAIR + rank


def split_dot(chosen, value):
    high = value.astype(BF16)
    rest = value - high.astype(F32)
    middle = rest.astype(BF16)
    low = (rest - middle.astype(F32)).astype(BF16)
    dot = functools.partial(jnp.dot, preferred_element_type=F32)
    return dot(chosen, high) + dot(chosen, middle) + dot(chosen, low)


def products(chosen, received, matrices, answer, spread, result):
    own_slots, levels, fields, _ = matrices.shape
    owners = received.shape[0]
    depth = levels * fields
    tail = levels - LANES
    iota = functools.partial(lax.broadcasted_iota, jnp.int32)
    values = received[...].reshape(owners * PAIR, received.shape[2]).astype(F32)
    choice = chosen[...].astype(BF16)
    field_of_row = iota((own_slots * fields, levels), 0) % fields
    placed = jnp.zeros((own_slots * fields, levels), F32)
    tails = values[:, fields * LANES :]
    for f in range(fields):
        end = pltpu.roll(tails, LANES - tail * f, 1) if f else tails
        full = jnp.concatenate([values[:, f * LANES : (f + 1) * LANES], end[:, :tail]], axis=1)
        every = lax.dot_general(
            choice, full.astype(BF16), (((0,), (0,)), ((), ())), preferred_element_type=F32
        )
        placed = jnp.where(field_of_row == f, every, placed)
    spreader = (iota((levels, depth), 1) // fields == iota((levels, depth), 0)).astype(F32).astype(BF16)
    own = iota(spread.shape, 1) % fields == iota(spread.shape, 0) % fields
    spread[...] = jnp.where(own, jnp.dot(placed.astype(BF16), spreader, preferred_element_type=F32), 0.0)
    result[...] = jnp.zeros(result.shape, F32)
    for s in range(own_slots):
        at = slice(s * fields, (s + 1) * fields)
        result[at, :levels] = jnp.dot(
            spread[at].astype(BF16), matrices[s].reshape(depth, levels), preferred_element_type=F32
        )
    backward = []
    for k in range(PAIR):
        rows = chosen[pl.ds(k, owners, stride=PAIR), :][:, : own_slots * fields]
        field_of_lane = iota(rows.shape, 1) % fields
        backward += [jnp.where(field_of_lane == f, rows, 0.0) for f in range(fields)]
    rows = split_dot(jnp.concatenate(backward, axis=0).astype(BF16), result[...])
    blocks = [rows[r * owners : (r + 1) * owners] for r in range(PAIR * fields)]
    tails = tail_lanes(blocks[0], 0)
    for r in range(1, PAIR * fields):
        tails = tails + tail_lanes(blocks[r], tail * r)
    answer[...] = jnp.concatenate([block[:, :LANES] for block in blocks] + [tails], axis=1).reshape(answer.shape)


def physics_first(received, matrices, answer, chosen_out, spread, result):
    own_slots, levels, fields, _ = matrices.shape
    owners = received.shape[0]
    code_lane = fields * levels
    codes = received[...].reshape(owners * PAIR, received.shape[2]).astype(F32)[:, code_lane : code_lane + 1]
    wanted = (lax.broadcasted_iota(jnp.int32, chosen_out.shape, 1) // fields + 1).astype(F32)
    chosen_out[...] = (codes == wanted).astype(F32)
    products(chosen_out, received, matrices, answer, spread, result)


def physics_second(received, matrices, chosen, answer, spread, result):
    products(chosen, received, matrices, answer, spread, result)


def add_first(plan, returned, late, field, *rest, levels):
    for f in range(field.shape[0]):
        unpack_field(late, field, f)
    add_increments(plan, returned, field, field, *rest, levels=levels)


def add_increments(plan, returned, base, field, lon_even, lon_odd, lat_even, lat_odd, inbox, *, levels):
    fields, halves, columns_all, lanes = field.shape
    owners = returned.shape[0]
    per_owner = inbox.shape[1] // owners
    tail = levels - LANES
    lines = returned[...].reshape(owners, returned.shape[2])
    tails = lines[:, per_owner * LANES :]
    for r in range(per_owner):
        inbox[0, r * owners : (r + 1) * owners] = lines[:, r * LANES : (r + 1) * LANES]
        inbox[1, r * owners : (r + 1) * owners] = pltpu.roll(tails, LANES - tail * r, 1) if r else tails

    def body(entries):
        found = []
        for column, row in entries:
            for f in range(fields):
                for h in range(halves):
                    here = (f, h, pl.ds(column, 1), slice(None))
                    found.append((here, base[here] + inbox[h, pl.ds(row + f * owners, 1), :]))
        for here, value in found:
            field[here] = value

    entry_groups(plan, body)
    span_lon = lat_even.shape[1]
    span_lat = columns_all // span_lon
    lon_up, lat_up = upward()
    places = edge_places(columns_all, span_lon)
    lon_low, lon_high, lat_low, lat_high = [edge_blocks(field, place, tail) for place in places]
    for up, even, odd, lows, highs in (
        (lon_up, lon_even, lon_odd, lon_low, lon_high),
        (lat_up, lat_even, lat_odd, lat_low, lat_high),
    ):
        for block, (low, high) in enumerate(zip(lows, highs)):
            even[block, : low.shape[0]] = jnp.where(up, high, low).astype(even.dtype)
            odd[block, : low.shape[0]] = jnp.where(up, low, high).astype(odd.dtype)


def edge_places(columns_all, span_lon):
    span_lat = columns_all // span_lon
    return (
        slice(0, span_lat),
        slice(columns_all - span_lat, columns_all),
        pl.ds(0, span_lon, stride=span_lat),
        pl.ds(span_lat - 1, span_lon, stride=span_lat),
    )


def edge_blocks(field, place, tail):
    fields = field.shape[0]
    return [field[f, 0, place, :] for f in range(fields)] + [
        side_by_side([field[f, 1, place, :] for f in range(fields)], tail)
    ]


def upward():
    return lax.axis_index("gx") % 2 == 0, lax.axis_index("gy") % 2 == 0


def inner_stencil(field, coef, extra, out):
    fields, halves, columns_all, lanes = field.shape
    span_lat, span_lon = coef.shape[1:]
    row = lax.broadcasted_iota(jnp.int32, (span_lat, 1), 0)
    for p in range(span_lon):
        weight = [coef[k, :, p : p + 1] for k in range(4)]
        weight[2] = jnp.where(row == 0, 0.0, weight[2])
        weight[3] = jnp.where(row == span_lat - 1, 0.0, weight[3])
        weight = [jnp.broadcast_to(w, (span_lat, lanes)) for w in weight]
        at = slice(p * span_lat, (p + 1) * span_lat)
        for f in range(fields):
            for h in range(halves):
                here = field[f, h, at]
                total = here + weight[2] * pltpu.roll(here, 1, 0) + weight[3] * pltpu.roll(here, span_lat - 1, 0)
                if p > 0:
                    total = total + weight[0] * field[f, h, (p - 1) * span_lat : p * span_lat]
                if p < span_lon - 1:
                    total = total + weight[1] * field[f, h, (p + 1) * span_lat : (p + 2) * span_lat]
                if extra is None:
                    out[f, h, at] = total
                elif h == 0:
                    out[f, h, at] = total + extra[f, at, :lanes].astype(F32)
                else:
                    tail = extra.shape[2] - lanes
                    out[f, h, at, :tail] = total[:, :tail] + extra[f, at, lanes:].astype(F32)


def inner_first(field, coef, early, out):
    inner_stencil(field, coef, early, out)


def inner_last(field, coef, out):
    inner_stencil(field, coef, None, out)


def edge_weights(coef):
    span_lat, span_lon = coef.shape[1:]
    same = lax.broadcasted_iota(jnp.int32, (span_lon, span_lon), 0) == lax.broadcasted_iota(
        jnp.int32, (span_lon, span_lon), 1
    )

    def upright(line):
        return jnp.sum(jnp.where(same, jnp.broadcast_to(line, (span_lon, span_lon)), 0.0), axis=1, keepdims=True)

    return (
        coef[0, :, :1],
        coef[1, :, span_lon - 1 :],
        upright(coef[2, :1, :]),
        upright(coef[3, span_lat - 1 :, :]),
    )


def add_edges(f, weights, lon_even, lon_odd, lat_even, lat_odd, out, tail):
    fields, _, columns_all, lanes = out.shape
    span_lon = lat_even.shape[1]
    span_lat = columns_all // span_lon
    lon_up, lat_up = upward()
    for h, block in ((0, f), (1, fields)):
        edges = []
        for up, even, odd, count in ((lon_up, lon_even, lon_odd, span_lat), (lat_up, lat_even, lat_odd, span_lon)):
            first, second = even[block, :count].astype(F32), odd[block, :count].astype(F32)
            if h and f:
                first, second = [pltpu.roll(edge, lanes - tail * f, 1) for edge in (first, second)]
            edges += [jnp.where(up, second, first), jnp.where(up, first, second)]
        for place, weight, edge in zip(edge_places(columns_all, span_lon), weights, edges):
            at = (f, h, place, slice(None))
            out[at] = out[at] + weight * edge


def edges_first(plan, inner, coef, lon_odd, lon_even, lat_odd, lat_even, out, outbox, rows, *, levels):
    fields, halves, columns_all, lanes = out.shape
    owners = outbox.shape[0]
    tail = levels - lanes
    weights = edge_weights(coef)
    rows[...] = jnp.zeros(rows.shape, F32)
    for f in range(fields):
        add_edges(f, weights, lon_even, lon_odd, lat_even, lat_odd, out, tail)

    gather_columns(plan, out, rows, owners)
    pack_rows(rows, 0.0, tail, outbox)


def edges_last(inner, coef, lon_odd, lon_even, lat_odd, lat_even, out_hbm, both, out, sems):
    fields, halves, columns_all, lanes = inner.shape
    tail = out.shape[2] - lanes
    weights = edge_weights(coef)
    copies = []
    for f in range(fields):
        add_edges(f, weights, lon_even, lon_odd, lat_even, lat_odd, both, tail)
        out[f, :, :lanes] = both[f, 0]
        out[f, :, lanes:] = both[f, 1, :, :tail]
        copies.append(pltpu.make_async_copy(out.at[f], out_hbm.at[f], sems.at[f]))
        copies[f].start()
    for copy in copies:
        copy.wait()


def exchange(lines):
    return lax.all_to_all(lines, "gy", split_axis=0, concat_axis=0, tiled=True)


def swap(edge, axis, start, periodic):
    count = lax.axis_size(axis)
    pairs = [(i, i + 1) for i in range(start, count - 1, 2)]
    if start and periodic:
        pairs.append((count - 1, 0))
    return lax.ppermute(edge, axis, pairs + [(high, low) for low, high in pairs])


def halos(lon_even, lon_odd, lat_even, lat_odd):
    lon_odd = swap(lon_odd, "gx", 1, True)
    lon_even = swap(lon_even, "gx", 0, True)
    lat_odd = swap(lat_odd, "gy", 1, False)
    lat_even = swap(lat_even, "gy", 0, False)
    return lon_odd, lon_even, lat_odd, lat_even


def on_device(late, early, stencil_coef, jacobian, cloudy_cols, cloudy_count, owner_rank, owner_slot):
    fields, levels, span_lon, span_lat = late.shape
    groups = lax.axis_size("gy")
    own_slots = jacobian.shape[1]
    capacity = cloudy_cols.shape[2]
    columns_all = span_lon * span_lat
    late = late.transpose(0, 2, 3, 1).reshape(fields, columns_all, levels)
    early = early.transpose(0, 2, 3, 1).reshape(fields, columns_all, levels)
    coef = stencil_coef.transpose(0, 2, 1)
    matrices = jacobian[0].transpose(0, 2, 1, 3)
    shape = jax.ShapeDtypeStruct
    per_owner = PAIR * fields
    inbox_rows = groups * per_owner
    grid = (fields, columns_all, levels)
    halves = (fields, 2, columns_all, LANES)
    plan_shape = shape((2 * capacity + 1,), jnp.int32)

    outbox_shape = shape((groups, PAIR, (fields + 1) * LANES), BF16)
    outbox, plan = call(
        pack_first,
        [outbox_shape, plan_shape],
        [HBM] * 5,
        [VMEM, SMEM],
        [
            SMEM(cloudy_cols.shape, jnp.int32),
            SMEM(cloudy_count.shape, jnp.int32),
            SMEM(owner_rank.shape, jnp.int32),
            SMEM(owner_slot.shape, jnp.int32),
            VMEM(grid, BF16),
            VMEM(halves, F32),
            VMEM((2, inbox_rows, LANES), F32),
            VMEM((groups * PAIR, LANES), F32),
            SMEM((groups,), jnp.int32),
            pltpu.SemaphoreType.DMA((4 + fields,)),
        ],
        vmem=57,
    )(cloudy_cols, cloudy_count, owner_rank, owner_slot, late)
    chosen_shape = shape((groups * PAIR, own_slots * fields), F32)
    answer_shape = shape((groups, 1, (per_owner + 1) * LANES), F32)
    spaces = [
        VMEM((own_slots * fields, levels * fields), F32),
        VMEM((own_slots * fields, 2 * LANES), F32),
    ]
    answer, chosen = call(physics_first, [answer_shape, chosen_shape], [VMEM] * 2, [VMEM] * 2, spaces)(
        exchange(outbox), matrices
    )
    returned = exchange(answer)

    def add(kernel, returned, base, aliases, edge_type):
        return call(
            functools.partial(kernel, levels=levels),
            [shape(halves, F32)] + [shape((fields + 1, span_lon, LANES), edge_type)] * 4,
            [SMEM] + [VMEM] * 2,
            [VMEM] * 5,
            [VMEM((2, inbox_rows, LANES), F32)],
            aliases,
        )(plan, returned, base)

    field, *edges = add(add_first, returned, late, {}, F32)
    neighbours = halos(*edges)
    (inner,) = call(inner_first, [shape(halves, F32)], [VMEM] * 3, [VMEM], touched=6000000)(field, coef, early)
    adjoint, outbox = call(
        functools.partial(edges_first, levels=levels),
        [shape(halves, F32), outbox_shape],
        [SMEM] + [VMEM] * 6,
        [VMEM] * 2,
        [VMEM((2, inbox_rows, LANES), F32)],
        {1: 0},
    )(plan, inner, coef, *neighbours)
    (answer,) = call(physics_second, [answer_shape], [VMEM] * 3, [VMEM], spaces)(
        exchange(outbox), matrices, chosen
    )
    field, *edges = add(add_increments, exchange(answer), adjoint, {2: 0}, BF16)
    neighbours = halos(*edges)
    (inner,) = call(inner_last, [shape(halves, F32)], [VMEM] * 2, [VMEM], touched=6000000)(field, coef)
    final, _ = call(
        edges_last,
        [shape(grid, F32), shape(halves, F32)],
        [VMEM] * 6,
        [HBM, VMEM],
        [VMEM(grid, F32), pltpu.SemaphoreType.DMA((fields,))],
        {0: 1},
    )(inner, coef, *neighbours)
    return final.reshape(fields, span_lon, span_lat, levels).transpose(0, 3, 1, 2)


def solution(mesh):
    return jax.shard_map(
        on_device,
        mesh=mesh,
        in_specs=(
            P(None, None, "gx", "gy"),
            P(None, None, "gx", "gy"),
            P(None, "gx", "gy"),
            P("gx", "gy", None, None, None),
            P("gx", "gy", None),
            P("gx", "gy"),
            P("gx", "gy", None),
            P("gx", "gy", None),
        ),
        out_specs=P(None, None, "gx", "gy"),
        check_vma=False,
    )
```

```python
import functools

import jax
import jax.numpy as jnp
from jax import lax
from jax.experimental import pallas as pl
from jax.experimental.pallas import tpu as pltpu
from jax.sharding import PartitionSpec as P

BF16 = jnp.bfloat16
F32 = jnp.float32
VMEM = pltpu.VMEM
SMEM = pltpu.SMEM
HBM = pltpu.HBM
PAIR = 2
LANES = 128
GROUP = 4


def call(kernel, out_shape, in_spaces, out_spaces, scratch=(), aliases=None, flops=1000, touched=1000000, vmem=40):
    return pl.pallas_call(
        kernel,
        out_shape=out_shape,
        in_specs=[pl.BlockSpec(memory_space=space) for space in in_spaces],
        out_specs=[pl.BlockSpec(memory_space=space) for space in out_spaces],
        scratch_shapes=scratch,
        input_output_aliases=aliases or {},
        compiler_params=pltpu.CompilerParams(vmem_limit_bytes=vmem * 1024 * 1024),
        cost_estimate=pl.CostEstimate(flops=flops, bytes_accessed=touched, transcendentals=0),
    )


def entry_groups(plan, body):
    capacity = (plan.shape[0] - 1) // 2

    def step(g, carry):
        first = g * GROUP
        body([(plan[1 + first + i], plan[1 + capacity + first + i]) for i in range(GROUP)])
        return carry

    lax.fori_loop(0, (plan[0] + (GROUP - 1)) // GROUP, step, 0)


def unpack_field(packed, field, f):
    field[f, 0] = packed[f, :, :LANES].astype(F32)
    field[f, 1, :, : packed.shape[2] - LANES] = packed[f, :, LANES:].astype(F32)


def tail_lanes(block, start):
    end = block[:, LANES:]
    return pltpu.roll(end, start, 1) if start else end


def pack_first(
    cols_hbm, count_hbm, owner_hbm, slot_hbm, late_hbm, outbox, plan, cols, count, owner, slot, late, field, rows, codes, used, sems
):
    fields, _, levels = late.shape
    capacity = cols.shape[2]
    owners = used.shape[0]
    tail = levels - LANES
    small = [(cols_hbm, cols), (count_hbm, count), (owner_hbm, owner), (slot_hbm, slot)]
    copies = [pltpu.make_async_copy(source, target, sems.at[i]) for i, (source, target) in enumerate(small)]
    copies += [pltpu.make_async_copy(late_hbm.at[f], late.at[f], sems.at[len(small) + f]) for f in range(fields)]
    for copy in copies:
        copy.start()
    for o in range(owners):
        used[o] = 0
    rows[...] = jnp.zeros(rows.shape, F32)
    codes[...] = jnp.zeros(codes.shape, F32)
    for copy in copies[: len(small)]:
        copy.wait()
    live = count[0, 0]
    plan[0] = live

    def route(e, carry):
        o = owner[0, 0, e]
        rank = used[o]
        used[o] = rank + 1
        plan[1 + e] = cols[0, 0, e]
        plan[1 + capacity + e] = rank * (fields * owners) + o
        codes[pl.ds(o * PAIR + rank, 1), :] = jnp.full((1, LANES), slot[0, 0, e] + 1, jnp.int32).astype(F32)
        return carry

    lax.fori_loop(0, live, route, 0)
    whole = (live // GROUP) * GROUP

    def repeat(e, carry):
        for part in (1, 1 + capacity):
            plan[part + e] = plan[part + whole]
        return carry

    lax.fori_loop(live, ((live + (GROUP - 1)) // GROUP) * GROUP, repeat, 0)
    for f in range(fields):
        copies[len(small) + f].wait()
        unpack_field(late, field, f)
    gather_columns(plan, field, rows, owners)
    lane = lax.broadcasted_iota(jnp.int32, codes.shape, 1)
    pack_rows(rows, jnp.where(lane == tail * fields, codes[...], 0.0), tail, outbox)


def gather_columns(plan, field, rows, owners):
    fields, halves = field.shape[:2]

    def body(entries):
        found = []
        for column, row in entries:
            at = outbox_row(row, owners, fields)
            for f in range(fields):
                for h in range(halves):
                    found.append((h, f * (PAIR * owners) + at, field[f, h, pl.ds(column, 1), :]))
        for h, row, value in found:
            rows[h, pl.ds(row, 1), :] = value

    entry_groups(plan, body)


def pack_rows(rows, tails, tail, outbox):
    count = outbox.shape[0] * outbox.shape[1]
    blocks = [slice(f * count, (f + 1) * count) for f in range(rows.shape[1] // count)]
    tails = tails + side_by_side([rows[1, block] for block in blocks], tail)
    packed = jnp.concatenate([rows[0, block] for block in blocks] + [tails], axis=1)
    outbox[...] = packed.astype(BF16).reshape(outbox.shape)


def side_by_side(ends, tail):
    lane = lax.broadcasted_iota(jnp.int32, ends[0].shape, 1)
    total = jnp.zeros(ends[0].shape, F32)
    for f, end in enumerate(ends):
        end = jnp.where(lane < tail, end, 0.0)
        total = total + (pltpu.roll(end, tail * f, 1) if f else end)
    return total


def outbox_row(row, owners, fields):
    rank = row // (fields * owners)
    return (row - rank * (fields * owners)) * PAIR + rank


def split_dot(chosen, value):
    high = value.astype(BF16)
    rest = value - high.astype(F32)
    middle = rest.astype(BF16)
    low = (rest - middle.astype(F32)).astype(BF16)
    dot = functools.partial(jnp.dot, preferred_element_type=F32)
    return dot(chosen, high) + dot(chosen, middle) + dot(chosen, low)


def products(chosen, received, matrices, answer, spread, result):
    own_slots, levels, fields, _ = matrices.shape
    owners = received.shape[0]
    depth = levels * fields
    tail = levels - LANES
    iota = functools.partial(lax.broadcasted_iota, jnp.int32)
    values = received[...].reshape(owners * PAIR, received.shape[2]).astype(F32)
    choice = chosen[...].astype(BF16)
    field_of_row = iota((own_slots * fields, levels), 0) % fields
    placed = jnp.zeros((own_slots * fields, levels), F32)
    tails = values[:, fields * LANES :]
    for f in range(fields):
        end = pltpu.roll(tails, LANES - tail * f, 1) if f else tails
        full = jnp.concatenate([values[:, f * LANES : (f + 1) * LANES], end[:, :tail]], axis=1)
        every = lax.dot_general(
            choice, full.astype(BF16), (((0,), (0,)), ((), ())), preferred_element_type=F32
        )
        placed = jnp.where(field_of_row == f, every, placed)
    spreader = (iota((levels, depth), 1) // fields == iota((levels, depth), 0)).astype(F32).astype(BF16)
    own = iota(spread.shape, 1) % fields == iota(spread.shape, 0) % fields
    spread[...] = jnp.where(own, jnp.dot(placed.astype(BF16), spreader, preferred_element_type=F32), 0.0)
    result[...] = jnp.zeros(result.shape, F32)
    for s in range(own_slots):
        at = slice(s * fields, (s + 1) * fields)
        result[at, :levels] = jnp.dot(
            spread[at].astype(BF16), matrices[s].reshape(depth, levels), preferred_element_type=F32
        )
    backward = []
    for k in range(PAIR):
        rows = chosen[pl.ds(k, owners, stride=PAIR), :][:, : own_slots * fields]
        field_of_lane = iota(rows.shape, 1) % fields
        backward += [jnp.where(field_of_lane == f, rows, 0.0) for f in range(fields)]
    rows = split_dot(jnp.concatenate(backward, axis=0).astype(BF16), result[...])
    blocks = [rows[r * owners : (r + 1) * owners] for r in range(PAIR * fields)]
    tails = tail_lanes(blocks[0], 0)
    for r in range(1, PAIR * fields):
        tails = tails + tail_lanes(blocks[r], tail * r)
    answer[...] = jnp.concatenate([block[:, :LANES] for block in blocks] + [tails], axis=1).reshape(answer.shape)


def physics_first(received, matrices, answer, chosen_out, spread, result):
    own_slots, levels, fields, _ = matrices.shape
    owners = received.shape[0]
    code_lane = fields * levels
    codes = received[...].reshape(owners * PAIR, received.shape[2]).astype(F32)[:, code_lane : code_lane + 1]
    wanted = (lax.broadcasted_iota(jnp.int32, chosen_out.shape, 1) // fields + 1).astype(F32)
    chosen_out[...] = (codes == wanted).astype(F32)
    products(chosen_out, received, matrices, answer, spread, result)


def physics_second(received, matrices, chosen, answer, spread, result):
    products(chosen, received, matrices, answer, spread, result)


def add_first(plan, returned, late, field, *rest, levels):
    for f in range(field.shape[0]):
        unpack_field(late, field, f)
    add_increments(plan, returned, field, field, *rest, levels=levels)


def add_increments(plan, returned, base, field, lon_even, lon_odd, lat_even, lat_odd, inbox, *, levels):
    fields, halves, columns_all, lanes = field.shape
    owners = returned.shape[0]
    per_owner = inbox.shape[1] // owners
    tail = levels - LANES
    lines = returned[...].reshape(owners, returned.shape[2])
    tails = lines[:, per_owner * LANES :]
    for r in range(per_owner):
        inbox[0, r * owners : (r + 1) * owners] = lines[:, r * LANES : (r + 1) * LANES]
        inbox[1, r * owners : (r + 1) * owners] = pltpu.roll(tails, LANES - tail * r, 1) if r else tails

    def body(entries):
        found = []
        for column, row in entries:
            for f in range(fields):
                for h in range(halves):
                    here = (f, h, pl.ds(column, 1), slice(None))
                    found.append((here, base[here] + inbox[h, pl.ds(row + f * owners, 1), :]))
        for here, value in found:
            field[here] = value

    entry_groups(plan, body)
    span_lon = lat_even.shape[1]
    span_lat = columns_all // span_lon
    lon_up, lat_up = upward()
    places = edge_places(columns_all, span_lon)
    lon_low, lon_high, lat_low, lat_high = [edge_blocks(field, place, tail) for place in places]
    for up, even, odd, lows, highs in (
        (lon_up, lon_even, lon_odd, lon_low, lon_high),
        (lat_up, lat_even, lat_odd, lat_low, lat_high),
    ):
        for block, (low, high) in enumerate(zip(lows, highs)):
            even[block, : low.shape[0]] = jnp.where(up, high, low).astype(even.dtype)
            odd[block, : low.shape[0]] = jnp.where(up, low, high).astype(odd.dtype)


def edge_places(columns_all, span_lon):
    span_lat = columns_all // span_lon
    return (
        slice(0, span_lat),
        slice(columns_all - span_lat, columns_all),
        pl.ds(0, span_lon, stride=span_lat),
        pl.ds(span_lat - 1, span_lon, stride=span_lat),
    )


def edge_blocks(field, place, tail):
    fields = field.shape[0]
    return [field[f, 0, place, :] for f in range(fields)] + [
        side_by_side([field[f, 1, place, :] for f in range(fields)], tail)
    ]


def upward():
    return lax.axis_index("gx") % 2 == 0, lax.axis_index("gy") % 2 == 0


def inner_stencil(field, coef, extra, out):
    fields, halves, columns_all, lanes = field.shape
    span_lat, span_lon = coef.shape[1:]
    row = lax.broadcasted_iota(jnp.int32, (span_lat, 1), 0)
    for p in range(span_lon):
        weight = [coef[k, :, p : p + 1] for k in range(4)]
        weight[2] = jnp.where(row == 0, 0.0, weight[2])
        weight[3] = jnp.where(row == span_lat - 1, 0.0, weight[3])
        weight = [jnp.broadcast_to(w, (span_lat, lanes)) for w in weight]
        at = slice(p * span_lat, (p + 1) * span_lat)
        for f in range(fields):
            for h in range(halves):
                here = field[f, h, at]
                total = here + weight[2] * pltpu.roll(here, 1, 0) + weight[3] * pltpu.roll(here, span_lat - 1, 0)
                if p > 0:
                    total = total + weight[0] * field[f, h, (p - 1) * span_lat : p * span_lat]
                if p < span_lon - 1:
                    total = total + weight[1] * field[f, h, (p + 1) * span_lat : (p + 2) * span_lat]
                if extra is None:
                    out[f, h, at] = total
                elif h == 0:
                    out[f, h, at] = total + extra[f, at, :lanes].astype(F32)
                else:
                    tail = extra.shape[2] - lanes
                    out[f, h, at, :tail] = total[:, :tail] + extra[f, at, lanes:].astype(F32)


def inner_first(field, coef, early, out):
    inner_stencil(field, coef, early, out)


def inner_last(field, coef, out):
    inner_stencil(field, coef, None, out)


def edge_weights(coef):
    span_lat, span_lon = coef.shape[1:]
    same = lax.broadcasted_iota(jnp.int32, (span_lon, span_lon), 0) == lax.broadcasted_iota(
        jnp.int32, (span_lon, span_lon), 1
    )

    def upright(line):
        return jnp.sum(jnp.where(same, jnp.broadcast_to(line, (span_lon, span_lon)), 0.0), axis=1, keepdims=True)

    return (
        coef[0, :, :1],
        coef[1, :, span_lon - 1 :],
        upright(coef[2, :1, :]),
        upright(coef[3, span_lat - 1 :, :]),
    )


def add_edges(f, weights, lon_even, lon_odd, lat_even, lat_odd, out, tail):
    fields, _, columns_all, lanes = out.shape
    span_lon = lat_even.shape[1]
    span_lat = columns_all // span_lon
    lon_up, lat_up = upward()
    for h, block in ((0, f), (1, fields)):
        edges = []
        for up, even, odd, count in ((lon_up, lon_even, lon_odd, span_lat), (lat_up, lat_even, lat_odd, span_lon)):
            first, second = even[block, :count].astype(F32), odd[block, :count].astype(F32)
            if h and f:
                first, second = [pltpu.roll(edge, lanes - tail * f, 1) for edge in (first, second)]
            edges += [jnp.where(up, second, first), jnp.where(up, first, second)]
        for place, weight, edge in zip(edge_places(columns_all, span_lon), weights, edges):
            at = (f, h, place, slice(None))
            out[at] = out[at] + weight * edge


def edges_first(plan, inner, coef, lon_odd, lat_odd, lon_even, lat_even, out, outbox, rows, *, levels):
    fields, halves, columns_all, lanes = out.shape
    owners = outbox.shape[0]
    tail = levels - lanes
    weights = edge_weights(coef)
    rows[...] = jnp.zeros(rows.shape, F32)
    for f in range(fields):
        add_edges(f, weights, lon_even, lon_odd, lat_even, lat_odd, out, tail)

    gather_columns(plan, out, rows, owners)
    pack_rows(rows, 0.0, tail, outbox)


def edges_last(inner, coef, lon_odd, lat_odd, lon_even, lat_even, out_hbm, both, out, sems):
    fields, halves, columns_all, lanes = inner.shape
    tail = out.shape[2] - lanes
    weights = edge_weights(coef)
    copies = []
    for f in range(fields):
        add_edges(f, weights, lon_even, lon_odd, lat_even, lat_odd, both, tail)
        out[f, :, :lanes] = both[f, 0]
        out[f, :, lanes:] = both[f, 1, :, :tail]
        copies.append(pltpu.make_async_copy(out.at[f], out_hbm.at[f], sems.at[f]))
        copies[f].start()
    for copy in copies:
        copy.wait()


def exchange(lines):
    return lax.all_to_all(lines, "gy", split_axis=0, concat_axis=0, tiled=True)


def swap(edge, axis, start, periodic):
    count = lax.axis_size(axis)
    pairs = [(i, i + 1) for i in range(start, count - 1, 2)]
    if start and periodic:
        pairs.append((count - 1, 0))
    return lax.ppermute(edge, axis, pairs + [(high, low) for low, high in pairs])


def halos(lon_even, lon_odd, lat_even, lat_odd):
    lon_odd = swap(lon_odd, "gx", 1, True)
    lat_odd = swap(lat_odd, "gy", 1, False)
    lon_even = swap(lon_even, "gx", 0, True)
    lat_even = swap(lat_even, "gy", 0, False)
    return lon_odd, lat_odd, lon_even, lat_even


def on_device(late, early, stencil_coef, jacobian, cloudy_cols, cloudy_count, owner_rank, owner_slot):
    fields, levels, span_lon, span_lat = late.shape
    groups = lax.axis_size("gy")
    own_slots = jacobian.shape[1]
    capacity = cloudy_cols.shape[2]
    columns_all = span_lon * span_lat
    late = late.transpose(0, 2, 3, 1).reshape(fields, columns_all, levels)
    early = early.transpose(0, 2, 3, 1).reshape(fields, columns_all, levels)
    coef = stencil_coef.transpose(0, 2, 1)
    matrices = jacobian[0].transpose(0, 2, 1, 3)
    shape = jax.ShapeDtypeStruct
    per_owner = PAIR * fields
    inbox_rows = groups * per_owner
    grid = (fields, columns_all, levels)
    halves = (fields, 2, columns_all, LANES)
    plan_shape = shape((2 * capacity + 1,), jnp.int32)

    outbox_shape = shape((groups, PAIR, (fields + 1) * LANES), BF16)
    outbox, plan = call(
        pack_first,
        [outbox_shape, plan_shape],
        [HBM] * 5,
        [VMEM, SMEM],
        [
            SMEM(cloudy_cols.shape, jnp.int32),
            SMEM(cloudy_count.shape, jnp.int32),
            SMEM(owner_rank.shape, jnp.int32),
            SMEM(owner_slot.shape, jnp.int32),
            VMEM(grid, BF16),
            VMEM(halves, F32),
            VMEM((2, inbox_rows, LANES), F32),
            VMEM((groups * PAIR, LANES), F32),
            SMEM((groups,), jnp.int32),
            pltpu.SemaphoreType.DMA((4 + fields,)),
        ],
        vmem=57,
    )(cloudy_cols, cloudy_count, owner_rank, owner_slot, late)
    chosen_shape = shape((groups * PAIR, own_slots * fields), F32)
    answer_shape = shape((groups, 1, (per_owner + 1) * LANES), F32)
    spaces = [
        VMEM((own_slots * fields, levels * fields), F32),
        VMEM((own_slots * fields, 2 * LANES), F32),
    ]
    answer, chosen = call(physics_first, [answer_shape, chosen_shape], [VMEM] * 2, [VMEM] * 2, spaces)(
        exchange(outbox), matrices
    )
    returned = exchange(answer)

    def add(kernel, returned, base, aliases, edge_type):
        return call(
            functools.partial(kernel, levels=levels),
            [shape(halves, F32)] + [shape((fields + 1, span_lon, LANES), edge_type)] * 4,
            [SMEM] + [VMEM] * 2,
            [VMEM] * 5,
            [VMEM((2, inbox_rows, LANES), F32)],
            aliases,
        )(plan, returned, base)

    field, *edges = add(add_first, returned, late, {}, F32)
    neighbours = halos(*edges)
    (inner,) = call(inner_first, [shape(halves, F32)], [VMEM] * 3, [VMEM], touched=6000000)(field, coef, early)
    adjoint, outbox = call(
        functools.partial(edges_first, levels=levels),
        [shape(halves, F32), outbox_shape],
        [SMEM] + [VMEM] * 6,
        [VMEM] * 2,
        [VMEM((2, inbox_rows, LANES), F32)],
        {1: 0},
    )(plan, inner, coef, *neighbours)
    (answer,) = call(physics_second, [answer_shape], [VMEM] * 3, [VMEM], spaces)(
        exchange(outbox), matrices, chosen
    )
    field, *edges = add(add_increments, exchange(answer), adjoint, {2: 0}, BF16)
    neighbours = halos(*edges)
    (inner,) = call(inner_last, [shape(halves, F32)], [VMEM] * 2, [VMEM], touched=6000000)(field, coef)
    final, _ = call(
        edges_last,
        [shape(grid, F32), shape(halves, F32)],
        [VMEM] * 6,
        [HBM, VMEM],
        [VMEM(grid, F32), pltpu.SemaphoreType.DMA((fields,))],
        {0: 1},
    )(inner, coef, *neighbours)
    return final.reshape(fields, span_lon, span_lat, levels).transpose(0, 3, 1, 2)


def solution(mesh):
    return jax.shard_map(
        on_device,
        mesh=mesh,
        in_specs=(
            P(None, None, "gx", "gy"),
            P(None, None, "gx", "gy"),
            P(None, "gx", "gy"),
            P("gx", "gy", None, None, None),
            P("gx", "gy", None),
            P("gx", "gy"),
            P("gx", "gy", None),
            P("gx", "gy", None),
        ),
        out_specs=P(None, None, "gx", "gy"),
        check_vma=False,
    )
```

```python
import functools

import jax
import jax.numpy as jnp
from jax import lax
from jax.experimental import pallas as pl
from jax.experimental.pallas import tpu as pltpu
from jax.sharding import PartitionSpec as P

BF16 = jnp.bfloat16
F32 = jnp.float32
VMEM = pltpu.VMEM
SMEM = pltpu.SMEM
HBM = pltpu.HBM
PAIR = 2
LANES = 128
GROUP = 4


def call(kernel, out_shape, in_spaces, out_spaces, scratch=(), aliases=None, flops=1000, touched=1000000, vmem=40):
    return pl.pallas_call(
        kernel,
        out_shape=out_shape,
        in_specs=[pl.BlockSpec(memory_space=space) for space in in_spaces],
        out_specs=[pl.BlockSpec(memory_space=space) for space in out_spaces],
        scratch_shapes=scratch,
        input_output_aliases=aliases or {},
        compiler_params=pltpu.CompilerParams(vmem_limit_bytes=vmem * 1024 * 1024),
        cost_estimate=pl.CostEstimate(flops=flops, bytes_accessed=touched, transcendentals=0),
    )


def entry_groups(plan, body):
    capacity = (plan.shape[0] - 1) // 2

    def step(g, carry):
        first = g * GROUP
        body([(plan[1 + first + i], plan[1 + capacity + first + i]) for i in range(GROUP)])
        return carry

    lax.fori_loop(0, (plan[0] + (GROUP - 1)) // GROUP, step, 0)


def shifted_tail(packed, f, at):
    end = packed[f, at, LANES:].astype(F32)
    end = jnp.concatenate([end, jnp.zeros((end.shape[0], LANES - end.shape[1]), F32)], axis=1)
    return pltpu.roll(end, (packed.shape[2] - LANES) * f, 1) if f else end


def unpack_field(packed, planes, f):
    fields = packed.shape[0]
    planes[f] = packed[f, :, :LANES].astype(F32)
    end = shifted_tail(packed, f, slice(None))
    planes[fields] = planes[fields] + end if f else end


def tail_lanes(block, start):
    end = block[:, LANES:]
    return pltpu.roll(end, start, 1) if start else end


def pack_first(
    cols_hbm, count_hbm, owner_hbm, slot_hbm, late_hbm, outbox, plan, cols, count, owner, slot, late, field, rows, codes, used, sems
):
    fields, _, levels = late.shape
    capacity = cols.shape[2]
    owners = used.shape[0]
    tail = levels - LANES
    small = [(cols_hbm, cols), (count_hbm, count), (owner_hbm, owner), (slot_hbm, slot)]
    copies = [pltpu.make_async_copy(source, target, sems.at[i]) for i, (source, target) in enumerate(small)]
    copies += [pltpu.make_async_copy(late_hbm.at[f], late.at[f], sems.at[len(small) + f]) for f in range(fields)]
    for copy in copies:
        copy.start()
    for o in range(owners):
        used[o] = 0
    rows[...] = jnp.zeros(rows.shape, F32)
    codes[...] = jnp.zeros(codes.shape, F32)
    for copy in copies[: len(small)]:
        copy.wait()
    live = count[0, 0]
    plan[0] = live

    def route(e, carry):
        o = owner[0, 0, e]
        rank = used[o]
        used[o] = rank + 1
        plan[1 + e] = cols[0, 0, e]
        plan[1 + capacity + e] = o * PAIR + rank
        codes[pl.ds(o * PAIR + rank, 1), :] = jnp.full((1, LANES), slot[0, 0, e] + 1, jnp.int32).astype(F32)
        return carry

    lax.fori_loop(0, live, route, 0)
    whole = (live // GROUP) * GROUP

    def repeat(e, carry):
        for part in (1, 1 + capacity):
            plan[part + e] = plan[part + whole]
        return carry

    lax.fori_loop(live, ((live + (GROUP - 1)) // GROUP) * GROUP, repeat, 0)
    for f in range(fields):
        copies[len(small) + f].wait()
        unpack_field(late, field, f)
    gather_columns(plan, field, rows)
    pack_rows(rows, codes[...], tail * fields, outbox)


def gather_columns(plan, planes, rows):
    def body(entries):
        found = [(h, at, planes[h, pl.ds(column, 1), :]) for column, at in entries for h in range(planes.shape[0])]
        for h, at, value in found:
            rows[h, pl.ds(at, 1), :] = value

    entry_groups(plan, body)


def pack_rows(rows, codes, code_lane, outbox):
    fields = rows.shape[0] - 1
    lane = lax.broadcasted_iota(jnp.int32, rows.shape[1:], 1)
    tails = jnp.where(lane < code_lane, rows[fields], 0.0)
    if codes is not None:
        tails = jnp.where(lane == code_lane, codes, tails)
    packed = jnp.concatenate([rows[f] for f in range(fields)] + [tails], axis=1)
    outbox[...] = packed.astype(BF16).reshape(outbox.shape)


def split_dot(chosen, value):
    high = value.astype(BF16)
    rest = value - high.astype(F32)
    middle = rest.astype(BF16)
    low = (rest - middle.astype(F32)).astype(BF16)
    dot = functools.partial(jnp.dot, preferred_element_type=F32)
    return dot(chosen, high) + dot(chosen, middle) + dot(chosen, low)


def products(chosen, received, matrices, answer, spread, result):
    own_slots, levels, fields, _ = matrices.shape
    owners = received.shape[0]
    depth = levels * fields
    tail = levels - LANES
    iota = functools.partial(lax.broadcasted_iota, jnp.int32)
    values = received[...].reshape(owners * PAIR, received.shape[2]).astype(F32)
    choice = chosen[...].astype(BF16)
    field_of_row = iota((own_slots * fields, levels), 0) % fields
    placed = jnp.zeros((own_slots * fields, levels), F32)
    tails = values[:, fields * LANES :]
    for f in range(fields):
        end = pltpu.roll(tails, LANES - tail * f, 1) if f else tails
        full = jnp.concatenate([values[:, f * LANES : (f + 1) * LANES], end[:, :tail]], axis=1)
        every = lax.dot_general(
            choice, full.astype(BF16), (((0,), (0,)), ((), ())), preferred_element_type=F32
        )
        placed = jnp.where(field_of_row == f, every, placed)
    spreader = (iota((levels, depth), 1) // fields == iota((levels, depth), 0)).astype(F32).astype(BF16)
    own = iota(spread.shape, 1) % fields == iota(spread.shape, 0) % fields
    spread[...] = jnp.where(own, jnp.dot(placed.astype(BF16), spreader, preferred_element_type=F32), 0.0)
    result[...] = jnp.zeros(result.shape, F32)
    for s in range(own_slots):
        at = slice(s * fields, (s + 1) * fields)
        result[at, :levels] = jnp.dot(
            spread[at].astype(BF16), matrices[s].reshape(depth, levels), preferred_element_type=F32
        )
    backward = []
    for k in range(PAIR):
        rows = chosen[pl.ds(k, owners, stride=PAIR), :][:, : own_slots * fields]
        field_of_lane = iota(rows.shape, 1) % fields
        backward += [jnp.where(field_of_lane == f, rows, 0.0) for f in range(fields)]
    rows = split_dot(jnp.concatenate(backward, axis=0).astype(BF16), result[...])
    blocks = [rows[r * owners : (r + 1) * owners] for r in range(PAIR * fields)]
    tails = tail_lanes(blocks[0], 0)
    for r in range(1, PAIR * fields):
        tails = tails + tail_lanes(blocks[r], tail * r)
    answer[...] = jnp.concatenate([block[:, :LANES] for block in blocks] + [tails], axis=1).reshape(answer.shape)


def physics_first(received, matrices, answer, chosen_out, spread, result):
    own_slots, levels, fields, _ = matrices.shape
    owners = received.shape[0]
    code_lane = fields * levels
    codes = received[...].reshape(owners * PAIR, received.shape[2]).astype(F32)[:, code_lane : code_lane + 1]
    wanted = (lax.broadcasted_iota(jnp.int32, chosen_out.shape, 1) // fields + 1).astype(F32)
    chosen_out[...] = (codes == wanted).astype(F32)
    products(chosen_out, received, matrices, answer, spread, result)


def physics_second(received, matrices, chosen, answer, spread, result):
    products(chosen, received, matrices, answer, spread, result)


def add_first(plan, returned, late, field, *rest, tail):
    for f in range(late.shape[0]):
        unpack_field(late, field, f)
    add_increments(plan, returned, field, field, *rest, tail=tail)


def add_increments(plan, returned, base, field, lon_even, lon_odd, lat_even, lat_odd, inbox, *, tail):
    planes, columns_all, lanes = field.shape
    fields = planes - 1
    owners = returned.shape[0]
    lines = returned[...].reshape(owners, returned.shape[2])
    tails = lines[:, PAIR * fields * lanes :]
    for k in range(PAIR):
        at = pl.ds(k, owners, stride=PAIR)
        for f in range(fields):
            r = k * fields + f
            inbox[f, at, :] = lines[:, r * lanes : (r + 1) * lanes]
        inbox[fields, at, :] = pltpu.roll(tails, lanes - tail * fields * k, 1) if k else tails

    def body(entries):
        found = []
        for column, at in entries:
            for h in range(planes):
                here = (h, pl.ds(column, 1), slice(None))
                found.append((here, base[here] + inbox[h, pl.ds(at, 1), :]))
        for here, value in found:
            field[here] = value

    entry_groups(plan, body)
    span_lon = lat_even.shape[1]
    lon_up, lat_up = upward()
    lon_low, lon_high, lat_low, lat_high = edge_places(columns_all, span_lon)
    for up, even, odd, low_place, high_place in (
        (lon_up, lon_even, lon_odd, lon_low, lon_high),
        (lat_up, lat_even, lat_odd, lat_low, lat_high),
    ):
        for h in range(planes):
            low, high = field[h, low_place, :], field[h, high_place, :]
            even[h, : low.shape[0]] = jnp.where(up, high, low).astype(even.dtype)
            odd[h, : low.shape[0]] = jnp.where(up, low, high).astype(odd.dtype)


def edge_places(columns_all, span_lon):
    span_lat = columns_all // span_lon
    return (
        slice(0, span_lat),
        slice(columns_all - span_lat, columns_all),
        pl.ds(0, span_lon, stride=span_lat),
        pl.ds(span_lat - 1, span_lon, stride=span_lat),
    )


def upward():
    return lax.axis_index("gx") % 2 == 0, lax.axis_index("gy") % 2 == 0


def inner_stencil(field, coef, extra, out):
    planes, columns_all, lanes = field.shape
    fields = planes - 1
    span_lat, span_lon = coef.shape[1:]
    row = lax.broadcasted_iota(jnp.int32, (span_lat, 1), 0)
    for p in range(span_lon):
        weight = [coef[k, :, p : p + 1] for k in range(4)]
        weight[2] = jnp.where(row == 0, 0.0, weight[2])
        weight[3] = jnp.where(row == span_lat - 1, 0.0, weight[3])
        weight = [jnp.broadcast_to(w, (span_lat, lanes)) for w in weight]
        at = slice(p * span_lat, (p + 1) * span_lat)
        for h in range(planes):
            here = field[h, at]
            total = here + weight[2] * pltpu.roll(here, 1, 0) + weight[3] * pltpu.roll(here, span_lat - 1, 0)
            if p > 0:
                total = total + weight[0] * field[h, (p - 1) * span_lat : p * span_lat]
            if p < span_lon - 1:
                total = total + weight[1] * field[h, (p + 1) * span_lat : (p + 2) * span_lat]
            if extra is not None and h < fields:
                total = total + extra[h, at, :lanes].astype(F32)
            elif extra is not None:
                for f in range(fields):
                    total = total + shifted_tail(extra, f, at)
            out[h, at] = total


def inner_first(field, coef, early, out):
    inner_stencil(field, coef, early, out)


def inner_last(field, coef, out):
    inner_stencil(field, coef, None, out)


def edge_weights(coef):
    span_lat, span_lon = coef.shape[1:]
    same = lax.broadcasted_iota(jnp.int32, (span_lon, span_lon), 0) == lax.broadcasted_iota(
        jnp.int32, (span_lon, span_lon), 1
    )

    def upright(line):
        return jnp.sum(jnp.where(same, jnp.broadcast_to(line, (span_lon, span_lon)), 0.0), axis=1, keepdims=True)

    return (
        coef[0, :, :1],
        coef[1, :, span_lon - 1 :],
        upright(coef[2, :1, :]),
        upright(coef[3, span_lat - 1 :, :]),
    )


def add_edges(h, weights, lon_even, lon_odd, lat_even, lat_odd, out):
    columns_all = out.shape[1]
    span_lon = lat_even.shape[1]
    span_lat = columns_all // span_lon
    lon_up, lat_up = upward()
    edges = []
    for up, even, odd, count in ((lon_up, lon_even, lon_odd, span_lat), (lat_up, lat_even, lat_odd, span_lon)):
        first, second = even[h, :count].astype(F32), odd[h, :count].astype(F32)
        edges += [jnp.where(up, second, first), jnp.where(up, first, second)]
    for place, weight, edge in zip(edge_places(columns_all, span_lon), weights, edges):
        at = (h, place, slice(None))
        out[at] = out[at] + weight * edge


def edges_first(plan, inner, coef, lon_odd, lat_odd, lon_even, lat_even, out, outbox, rows, *, tail):
    weights = edge_weights(coef)
    rows[...] = jnp.zeros(rows.shape, F32)
    for h in range(out.shape[0]):
        add_edges(h, weights, lon_even, lon_odd, lat_even, lat_odd, out)
    gather_columns(plan, out, rows)
    pack_rows(rows, None, tail * (out.shape[0] - 1), outbox)


def edges_last(inner, coef, lon_odd, lat_odd, lon_even, lat_even, out_hbm, planes, out, sems):
    fields, _, levels = out.shape
    tail = levels - LANES
    weights = edge_weights(coef)
    add_edges(fields, weights, lon_even, lon_odd, lat_even, lat_odd, planes)
    copies = []
    for f in range(fields):
        add_edges(f, weights, lon_even, lon_odd, lat_even, lat_odd, planes)
        out[f, :, :LANES] = planes[f]
        ends = planes[fields]
        out[f, :, LANES:] = (pltpu.roll(ends, LANES - tail * f, 1) if f else ends)[:, :tail]
        copies.append(pltpu.make_async_copy(out.at[f], out_hbm.at[f], sems.at[f]))
        copies[f].start()
    for copy in copies:
        copy.wait()


def exchange(lines):
    return lax.all_to_all(lines, "gy", split_axis=0, concat_axis=0, tiled=True)


def swap(edge, axis, start, periodic):
    count = lax.axis_size(axis)
    pairs = [(i, i + 1) for i in range(start, count - 1, 2)]
    if start and periodic:
        pairs.append((count - 1, 0))
    return lax.ppermute(edge, axis, pairs + [(high, low) for low, high in pairs])


def halos(lon_even, lon_odd, lat_even, lat_odd):
    lon_odd = swap(lon_odd, "gx", 1, True)
    lat_odd = swap(lat_odd, "gy", 1, False)
    lon_even = swap(lon_even, "gx", 0, True)
    lat_even = swap(lat_even, "gy", 0, False)
    return lon_odd, lat_odd, lon_even, lat_even


def on_device(late, early, stencil_coef, jacobian, cloudy_cols, cloudy_count, owner_rank, owner_slot):
    fields, levels, span_lon, span_lat = late.shape
    groups = lax.axis_size("gy")
    own_slots = jacobian.shape[1]
    capacity = cloudy_cols.shape[2]
    columns_all = span_lon * span_lat
    late = late.transpose(0, 2, 3, 1).reshape(fields, columns_all, levels)
    early = early.transpose(0, 2, 3, 1).reshape(fields, columns_all, levels)
    coef = stencil_coef.transpose(0, 2, 1)
    matrices = jacobian[0].transpose(0, 2, 1, 3)
    shape = jax.ShapeDtypeStruct
    per_owner = PAIR * fields
    grid = (fields, columns_all, levels)
    tail = levels - LANES
    planes = (fields + 1, columns_all, LANES)
    rows_shape = (fields + 1, groups * PAIR, LANES)
    plan_shape = shape((2 * capacity + 1,), jnp.int32)

    outbox_shape = shape((groups, PAIR, (fields + 1) * LANES), BF16)
    outbox, plan = call(
        pack_first,
        [outbox_shape, plan_shape],
        [HBM] * 5,
        [VMEM, SMEM],
        [
            SMEM(cloudy_cols.shape, jnp.int32),
            SMEM(cloudy_count.shape, jnp.int32),
            SMEM(owner_rank.shape, jnp.int32),
            SMEM(owner_slot.shape, jnp.int32),
            VMEM(grid, BF16),
            VMEM(planes, F32),
            VMEM(rows_shape, F32),
            VMEM((groups * PAIR, LANES), F32),
            SMEM((groups,), jnp.int32),
            pltpu.SemaphoreType.DMA((4 + fields,)),
        ],
        vmem=57,
    )(cloudy_cols, cloudy_count, owner_rank, owner_slot, late)
    chosen_shape = shape((groups * PAIR, own_slots * fields), F32)
    answer_shape = shape((groups, 1, (per_owner + 1) * LANES), F32)
    spaces = [
        VMEM((own_slots * fields, levels * fields), F32),
        VMEM((own_slots * fields, 2 * LANES), F32),
    ]
    answer, chosen = call(physics_first, [answer_shape, chosen_shape], [VMEM] * 2, [VMEM] * 2, spaces)(
        exchange(outbox), matrices
    )
    returned = exchange(answer)

    def add(kernel, returned, base, aliases, edge_type):
        return call(
            functools.partial(kernel, tail=tail),
            [shape(planes, F32)] + [shape((fields + 1, span_lon, LANES), edge_type)] * 4,
            [SMEM] + [VMEM] * 2,
            [VMEM] * 5,
            [VMEM(rows_shape, F32)],
            aliases,
        )(plan, returned, base)

    field, *edges = add(add_first, returned, late, {}, F32)
    neighbours = halos(*edges)
    (inner,) = call(inner_first, [shape(planes, F32)], [VMEM] * 3, [VMEM], touched=6000000)(field, coef, early)
    adjoint, outbox = call(
        functools.partial(edges_first, tail=tail),
        [shape(planes, F32), outbox_shape],
        [SMEM] + [VMEM] * 6,
        [VMEM] * 2,
        [VMEM(rows_shape, F32)],
        {1: 0},
    )(plan, inner, coef, *neighbours)
    (answer,) = call(physics_second, [answer_shape], [VMEM] * 3, [VMEM], spaces)(
        exchange(outbox), matrices, chosen
    )
    field, *edges = add(add_increments, exchange(answer), adjoint, {2: 0}, BF16)
    neighbours = halos(*edges)
    (inner,) = call(inner_last, [shape(planes, F32)], [VMEM] * 2, [VMEM], touched=6000000)(field, coef)
    final, _ = call(
        edges_last,
        [shape(grid, F32), shape(planes, F32)],
        [VMEM] * 6,
        [HBM, VMEM],
        [VMEM(grid, F32), pltpu.SemaphoreType.DMA((fields,))],
        {0: 1},
    )(inner, coef, *neighbours)
    return final.reshape(fields, span_lon, span_lat, levels).transpose(0, 3, 1, 2)


def solution(mesh):
    return jax.shard_map(
        on_device,
        mesh=mesh,
        in_specs=(
            P(None, None, "gx", "gy"),
            P(None, None, "gx", "gy"),
            P(None, "gx", "gy"),
            P("gx", "gy", None, None, None),
            P("gx", "gy", None),
            P("gx", "gy"),
            P("gx", "gy", None),
            P("gx", "gy", None),
        ),
        out_specs=P(None, None, "gx", "gy"),
        check_vma=False,
    )
```

```python
import functools

import jax
import jax.numpy as jnp
from jax import lax
from jax.experimental import pallas as pl
from jax.experimental.pallas import tpu as pltpu
from jax.sharding import PartitionSpec as P

BF16 = jnp.bfloat16
F32 = jnp.float32
VMEM = pltpu.VMEM
SMEM = pltpu.SMEM
HBM = pltpu.HBM
PAIR = 2
LANES = 128
GROUP = 4
KEEP = 11
CHUNK = 5


def call(kernel, out_shape, in_spaces, out_spaces, scratch=(), aliases=None, flops=1000, touched=1000000, vmem=40):
    return pl.pallas_call(
        kernel,
        out_shape=out_shape,
        in_specs=[pl.BlockSpec(memory_space=space) for space in in_spaces],
        out_specs=[pl.BlockSpec(memory_space=space) for space in out_spaces],
        scratch_shapes=scratch,
        input_output_aliases=aliases or {},
        compiler_params=pltpu.CompilerParams(vmem_limit_bytes=vmem * 1024 * 1024),
        cost_estimate=pl.CostEstimate(flops=flops, bytes_accessed=touched, transcendentals=0),
    )


def entry_groups(plan, body):
    capacity = (plan.shape[0] - 1) // 2

    def step(g, carry):
        first = g * GROUP
        body([(plan[1 + first + i], plan[1 + capacity + first + i]) for i in range(GROUP)])
        return carry

    lax.fori_loop(0, (plan[0] + (GROUP - 1)) // GROUP, step, 0)


def shifted_tail(packed, f, at):
    end = packed[f, at, LANES:].astype(F32)
    end = jnp.concatenate([end, jnp.zeros((end.shape[0], LANES - end.shape[1]), F32)], axis=1)
    return pltpu.roll(end, (packed.shape[2] - LANES) * f, 1) if f else end


def unpack_field(packed, planes, f):
    fields = packed.shape[0]
    planes[f] = packed[f, :, :LANES].astype(F32)
    end = shifted_tail(packed, f, slice(None))
    planes[fields] = planes[fields] + end if f else end


def tail_lanes(block, start):
    end = block[:, LANES:]
    return pltpu.roll(end, start, 1) if start else end


def pack_first(
    cols_hbm, count_hbm, owner_hbm, slot_hbm, late_hbm, outbox, plan, cols, count, owner, slot, late, field, rows, codes, used, sems
):
    fields, _, levels = late.shape
    capacity = cols.shape[2]
    owners = used.shape[0]
    tail = levels - LANES
    small = [(cols_hbm, cols), (count_hbm, count), (owner_hbm, owner), (slot_hbm, slot)]
    copies = [pltpu.make_async_copy(source, target, sems.at[i]) for i, (source, target) in enumerate(small)]
    copies += [pltpu.make_async_copy(late_hbm.at[f], late.at[f], sems.at[len(small) + f]) for f in range(fields)]
    for copy in copies:
        copy.start()
    for o in range(owners):
        used[o] = 0
    rows[...] = jnp.zeros(rows.shape, F32)
    codes[...] = jnp.zeros(codes.shape, F32)
    for copy in copies[: len(small)]:
        copy.wait()
    live = count[0, 0]
    plan[0] = live

    def route(e, carry):
        o = owner[0, 0, e]
        rank = used[o]
        used[o] = rank + 1
        plan[1 + e] = cols[0, 0, e]
        plan[1 + capacity + e] = o * PAIR + rank
        codes[pl.ds(o * PAIR + rank, 1), :] = jnp.full((1, LANES), slot[0, 0, e] + 1, jnp.int32).astype(F32)
        return carry

    lax.fori_loop(0, live, route, 0)
    whole = (live // GROUP) * GROUP

    def repeat(e, carry):
        for part in (1, 1 + capacity):
            plan[part + e] = plan[part + whole]
        return carry

    lax.fori_loop(live, ((live + (GROUP - 1)) // GROUP) * GROUP, repeat, 0)
    for f in range(fields):
        copies[len(small) + f].wait()
        unpack_field(late, field, f)
    gather_columns(plan, field, rows)
    pack_rows(rows, codes[...], tail * fields, outbox)


def gather_columns(plan, planes, rows):
    def body(entries):
        found = [(h, at, planes[h, pl.ds(column, 1), :]) for column, at in entries for h in range(planes.shape[0])]
        for h, at, value in found:
            rows[h, pl.ds(at, 1), :] = value

    entry_groups(plan, body)


def pack_rows(rows, codes, code_lane, outbox):
    fields = rows.shape[0] - 1
    lane = lax.broadcasted_iota(jnp.int32, rows.shape[1:], 1)
    tails = jnp.where(lane < code_lane, rows[fields], 0.0)
    if codes is not None:
        tails = jnp.where(lane == code_lane, codes, tails)
    packed = jnp.concatenate([rows[f] for f in range(fields)] + [tails], axis=1)
    outbox[...] = packed.astype(BF16).reshape(outbox.shape)


def split_dot(chosen, value):
    high = value.astype(BF16)
    rest = value - high.astype(F32)
    middle = rest.astype(BF16)
    low = (rest - middle.astype(F32)).astype(BF16)
    dot = functools.partial(jnp.dot, preferred_element_type=F32)
    return dot(chosen, high) + dot(chosen, middle) + dot(chosen, low)


def bring(matrices_hbm, kept, sem):
    copy = pltpu.make_async_copy(matrices_hbm.at[: kept.shape[0]], kept, sem)
    copy.start()
    copy.wait()


def products(chosen, received, matrices, arrivals, answer, spread, result):
    own_slots = len(matrices)
    levels, fields, _ = matrices[0].shape
    owners = received.shape[0]
    depth = levels * fields
    tail = levels - LANES
    iota = functools.partial(lax.broadcasted_iota, jnp.int32)
    values = received[...].reshape(owners * PAIR, received.shape[2]).astype(F32)
    choice = chosen[...].astype(BF16)
    field_of_row = iota((own_slots * fields, levels), 0) % fields
    placed = jnp.zeros((own_slots * fields, levels), F32)
    tails = values[:, fields * LANES :]
    for f in range(fields):
        end = pltpu.roll(tails, LANES - tail * f, 1) if f else tails
        full = jnp.concatenate([values[:, f * LANES : (f + 1) * LANES], end[:, :tail]], axis=1)
        every = lax.dot_general(
            choice, full.astype(BF16), (((0,), (0,)), ((), ())), preferred_element_type=F32
        )
        placed = jnp.where(field_of_row == f, every, placed)
    spreader = (iota((levels, depth), 1) // fields == iota((levels, depth), 0)).astype(F32).astype(BF16)
    own = iota(spread.shape, 1) % fields == iota(spread.shape, 0) % fields
    spread[...] = jnp.where(own, jnp.dot(placed.astype(BF16), spreader, preferred_element_type=F32), 0.0)
    result[...] = jnp.zeros(result.shape, F32)
    for s in range(own_slots):
        at = slice(s * fields, (s + 1) * fields)
        if s in arrivals:
            arrivals[s].wait()
        result[at, :levels] = jnp.dot(
            spread[at].astype(BF16), matrices[s][...].reshape(depth, levels), preferred_element_type=F32
        )
    backward = []
    for k in range(PAIR):
        rows = chosen[pl.ds(k, owners, stride=PAIR), :][:, : own_slots * fields]
        field_of_lane = iota(rows.shape, 1) % fields
        backward += [jnp.where(field_of_lane == f, rows, 0.0) for f in range(fields)]
    rows = split_dot(jnp.concatenate(backward, axis=0).astype(BF16), result[...])
    blocks = [rows[r * owners : (r + 1) * owners] for r in range(PAIR * fields)]
    tails = tail_lanes(blocks[0], 0)
    for r in range(1, PAIR * fields):
        tails = tails + tail_lanes(blocks[r], tail * r)
    answer[...] = jnp.concatenate([block[:, :LANES] for block in blocks] + [tails], axis=1).reshape(answer.shape)


def physics_first(received, kept, matrices_hbm, answer, chosen_out, spread, result, rest, sems):
    own_slots, levels, fields, _ = matrices_hbm.shape
    keep = kept.shape[0]
    arrivals = {}
    for i, s in enumerate(range(keep, own_slots, CHUNK)):
        count = min(CHUNK, own_slots - s)
        arrivals[s] = pltpu.make_async_copy(
            matrices_hbm.at[s : s + count], rest.at[s - keep : s - keep + count], sems.at[i]
        )
        arrivals[s].start()
    owners = received.shape[0]
    code_lane = fields * levels
    codes = received[...].reshape(owners * PAIR, received.shape[2]).astype(F32)[:, code_lane : code_lane + 1]
    wanted = (lax.broadcasted_iota(jnp.int32, chosen_out.shape, 1) // fields + 1).astype(F32)
    chosen_out[...] = (codes == wanted).astype(F32)
    matrices = [kept.at[s] for s in range(keep)] + [rest.at[s] for s in range(own_slots - keep)]
    products(chosen_out, received, matrices, arrivals, answer, spread, result)


def physics_second(received, matrices, chosen, answer, spread, result):
    each = [matrices.at[s] for s in range(matrices.shape[0])]
    products(chosen, received, each, {}, answer, spread, result)


def add_first(plan, returned, late, field, *rest, tail):
    for f in range(late.shape[0]):
        unpack_field(late, field, f)
    add_increments(plan, returned, field, field, *rest, tail=tail)


def add_increments(plan, returned, base, field, lon_even, lon_odd, lat_even, lat_odd, inbox, *, tail):
    planes, columns_all, lanes = field.shape
    fields = planes - 1
    owners = returned.shape[0]
    lines = returned[...].reshape(owners, returned.shape[2])
    tails = lines[:, PAIR * fields * lanes :]
    for k in range(PAIR):
        at = pl.ds(k, owners, stride=PAIR)
        for f in range(fields):
            r = k * fields + f
            inbox[f, at, :] = lines[:, r * lanes : (r + 1) * lanes]
        inbox[fields, at, :] = pltpu.roll(tails, lanes - tail * fields * k, 1) if k else tails

    def body(entries):
        found = []
        for column, at in entries:
            for h in range(planes):
                here = (h, pl.ds(column, 1), slice(None))
                found.append((here, base[here] + inbox[h, pl.ds(at, 1), :]))
        for here, value in found:
            field[here] = value

    entry_groups(plan, body)
    span_lon = lat_even.shape[1]
    lon_up, lat_up = upward()
    lon_low, lon_high, lat_low, lat_high = edge_places(columns_all, span_lon)
    for up, even, odd, low_place, high_place in (
        (lon_up, lon_even, lon_odd, lon_low, lon_high),
        (lat_up, lat_even, lat_odd, lat_low, lat_high),
    ):
        for h in range(planes):
            low, high = field[h, low_place, :], field[h, high_place, :]
            even[h, : low.shape[0]] = jnp.where(up, high, low).astype(even.dtype)
            odd[h, : low.shape[0]] = jnp.where(up, low, high).astype(odd.dtype)


def edge_places(columns_all, span_lon):
    span_lat = columns_all // span_lon
    return (
        slice(0, span_lat),
        slice(columns_all - span_lat, columns_all),
        pl.ds(0, span_lon, stride=span_lat),
        pl.ds(span_lat - 1, span_lon, stride=span_lat),
    )


def upward():
    return lax.axis_index("gx") % 2 == 0, lax.axis_index("gy") % 2 == 0


def inner_stencil(field, coef, extra, out):
    planes, columns_all, lanes = field.shape
    fields = planes - 1
    span_lat, span_lon = coef.shape[1:]
    row = lax.broadcasted_iota(jnp.int32, (span_lat, 1), 0)
    for p in range(span_lon):
        weight = [coef[k, :, p : p + 1] for k in range(4)]
        weight[2] = jnp.where(row == 0, 0.0, weight[2])
        weight[3] = jnp.where(row == span_lat - 1, 0.0, weight[3])
        weight = [jnp.broadcast_to(w, (span_lat, lanes)) for w in weight]
        at = slice(p * span_lat, (p + 1) * span_lat)
        for h in range(planes):
            here = field[h, at]
            total = here + weight[2] * pltpu.roll(here, 1, 0) + weight[3] * pltpu.roll(here, span_lat - 1, 0)
            if p > 0:
                total = total + weight[0] * field[h, (p - 1) * span_lat : p * span_lat]
            if p < span_lon - 1:
                total = total + weight[1] * field[h, (p + 1) * span_lat : (p + 2) * span_lat]
            if extra is not None and h < fields:
                total = total + extra[h, at, :lanes].astype(F32)
            elif extra is not None:
                for f in range(fields):
                    total = total + shifted_tail(extra, f, at)
            out[h, at] = total


def inner_first(field, coef, early, out):
    inner_stencil(field, coef, early, out)


def inner_last(field, coef, out):
    inner_stencil(field, coef, None, out)


def edge_weights(coef):
    span_lat, span_lon = coef.shape[1:]
    same = lax.broadcasted_iota(jnp.int32, (span_lon, span_lon), 0) == lax.broadcasted_iota(
        jnp.int32, (span_lon, span_lon), 1
    )

    def upright(line):
        return jnp.sum(jnp.where(same, jnp.broadcast_to(line, (span_lon, span_lon)), 0.0), axis=1, keepdims=True)

    return (
        coef[0, :, :1],
        coef[1, :, span_lon - 1 :],
        upright(coef[2, :1, :]),
        upright(coef[3, span_lat - 1 :, :]),
    )


def add_edges(h, weights, lon_even, lon_odd, lat_even, lat_odd, out):
    columns_all = out.shape[1]
    span_lon = lat_even.shape[1]
    span_lat = columns_all // span_lon
    lon_up, lat_up = upward()
    edges = []
    for up, even, odd, count in ((lon_up, lon_even, lon_odd, span_lat), (lat_up, lat_even, lat_odd, span_lon)):
        first, second = even[h, :count].astype(F32), odd[h, :count].astype(F32)
        edges += [jnp.where(up, second, first), jnp.where(up, first, second)]
    for place, weight, edge in zip(edge_places(columns_all, span_lon), weights, edges):
        at = (h, place, slice(None))
        out[at] = out[at] + weight * edge


def edges_first(plan, inner, coef, lon_odd, lat_odd, lon_even, lat_even, out, outbox, rows, *, tail):
    weights = edge_weights(coef)
    rows[...] = jnp.zeros(rows.shape, F32)
    for h in range(out.shape[0]):
        add_edges(h, weights, lon_even, lon_odd, lat_even, lat_odd, out)
    gather_columns(plan, out, rows)
    pack_rows(rows, None, tail * (out.shape[0] - 1), outbox)


def edges_last(inner, coef, lon_odd, lat_odd, lon_even, lat_even, out_hbm, planes, out, sems):
    fields, _, levels = out.shape
    tail = levels - LANES
    weights = edge_weights(coef)
    add_edges(fields, weights, lon_even, lon_odd, lat_even, lat_odd, planes)
    copies = []
    for f in range(fields):
        add_edges(f, weights, lon_even, lon_odd, lat_even, lat_odd, planes)
        out[f, :, :LANES] = planes[f]
        ends = planes[fields]
        out[f, :, LANES:] = (pltpu.roll(ends, LANES - tail * f, 1) if f else ends)[:, :tail]
        copies.append(pltpu.make_async_copy(out.at[f], out_hbm.at[f], sems.at[f]))
        copies[f].start()
    for copy in copies:
        copy.wait()


def exchange(lines):
    return lax.all_to_all(lines, "gy", split_axis=0, concat_axis=0, tiled=True)


def swap(edge, axis, start, periodic):
    count = lax.axis_size(axis)
    pairs = [(i, i + 1) for i in range(start, count - 1, 2)]
    if start and periodic:
        pairs.append((count - 1, 0))
    return lax.ppermute(edge, axis, pairs + [(high, low) for low, high in pairs])


def halos(lon_even, lon_odd, lat_even, lat_odd):
    lon_odd = swap(lon_odd, "gx", 1, True)
    lat_odd = swap(lat_odd, "gy", 1, False)
    lon_even = swap(lon_even, "gx", 0, True)
    lat_even = swap(lat_even, "gy", 0, False)
    return lon_odd, lat_odd, lon_even, lat_even


def on_device(late, early, stencil_coef, jacobian, cloudy_cols, cloudy_count, owner_rank, owner_slot):
    fields, levels, span_lon, span_lat = late.shape
    groups = lax.axis_size("gy")
    own_slots = jacobian.shape[1]
    capacity = cloudy_cols.shape[2]
    columns_all = span_lon * span_lat
    late = late.transpose(0, 2, 3, 1).reshape(fields, columns_all, levels)
    early = early.transpose(0, 2, 3, 1).reshape(fields, columns_all, levels)
    coef = stencil_coef.transpose(0, 2, 1)
    matrices = jacobian[0].transpose(0, 2, 1, 3)
    shape = jax.ShapeDtypeStruct
    per_owner = PAIR * fields
    grid = (fields, columns_all, levels)
    tail = levels - LANES
    planes = (fields + 1, columns_all, LANES)
    rows_shape = (fields + 1, groups * PAIR, LANES)
    plan_shape = shape((2 * capacity + 1,), jnp.int32)

    outbox_shape = shape((groups, PAIR, (fields + 1) * LANES), BF16)
    outbox, plan = call(
        pack_first,
        [outbox_shape, plan_shape],
        [HBM] * 5,
        [VMEM, SMEM],
        [
            SMEM(cloudy_cols.shape, jnp.int32),
            SMEM(cloudy_count.shape, jnp.int32),
            SMEM(owner_rank.shape, jnp.int32),
            SMEM(owner_slot.shape, jnp.int32),
            VMEM(grid, BF16),
            VMEM(planes, F32),
            VMEM(rows_shape, F32),
            VMEM((groups * PAIR, LANES), F32),
            SMEM((groups,), jnp.int32),
            pltpu.SemaphoreType.DMA((4 + fields,)),
        ],
        vmem=57,
    )(cloudy_cols, cloudy_count, owner_rank, owner_slot, late)
    chosen_shape = shape((groups * PAIR, own_slots * fields), F32)
    answer_shape = shape((groups, 1, (per_owner + 1) * LANES), F32)
    spaces = [
        VMEM((own_slots * fields, levels * fields), F32),
        VMEM((own_slots * fields, 2 * LANES), F32),
    ]
    (kept,) = call(
        bring,
        [shape((KEEP,) + matrices.shape[1:], BF16)],
        [HBM],
        [VMEM],
        [pltpu.SemaphoreType.DMA(())],
        touched=4000000,
        vmem=50,
    )(matrices)
    left = own_slots - KEEP
    answer, chosen = call(
        physics_first,
        [answer_shape, chosen_shape],
        [VMEM, VMEM, HBM],
        [VMEM] * 2,
        spaces + [VMEM((left,) + matrices.shape[1:], BF16), pltpu.SemaphoreType.DMA((-(-left // CHUNK),))],
        vmem=50,
    )(exchange(outbox), kept, matrices)
    returned = exchange(answer)

    def add(kernel, returned, base, aliases, edge_type):
        return call(
            functools.partial(kernel, tail=tail),
            [shape(planes, F32)] + [shape((fields + 1, span_lon, LANES), edge_type)] * 4,
            [SMEM] + [VMEM] * 2,
            [VMEM] * 5,
            [VMEM(rows_shape, F32)],
            aliases,
        )(plan, returned, base)

    field, *edges = add(add_first, returned, late, {}, F32)
    neighbours = halos(*edges)
    (inner,) = call(inner_first, [shape(planes, F32)], [VMEM] * 3, [VMEM], touched=6000000)(field, coef, early)
    adjoint, outbox = call(
        functools.partial(edges_first, tail=tail),
        [shape(planes, F32), outbox_shape],
        [SMEM] + [VMEM] * 6,
        [VMEM] * 2,
        [VMEM(rows_shape, F32)],
        {1: 0},
    )(plan, inner, coef, *neighbours)
    (answer,) = call(physics_second, [answer_shape], [VMEM] * 3, [VMEM], spaces)(
        exchange(outbox), matrices, chosen
    )
    field, *edges = add(add_increments, exchange(answer), adjoint, {2: 0}, BF16)
    neighbours = halos(*edges)
    (inner,) = call(inner_last, [shape(planes, F32)], [VMEM] * 2, [VMEM], touched=6000000)(field, coef)
    final, _ = call(
        edges_last,
        [shape(grid, F32), shape(planes, F32)],
        [VMEM] * 6,
        [HBM, VMEM],
        [VMEM(grid, F32), pltpu.SemaphoreType.DMA((fields,))],
        {0: 1},
    )(inner, coef, *neighbours)
    return final.reshape(fields, span_lon, span_lat, levels).transpose(0, 3, 1, 2)


def solution(mesh):
    return jax.shard_map(
        on_device,
        mesh=mesh,
        in_specs=(
            P(None, None, "gx", "gy"),
            P(None, None, "gx", "gy"),
            P(None, "gx", "gy"),
            P("gx", "gy", None, None, None),
            P("gx", "gy", None),
            P("gx", "gy"),
            P("gx", "gy", None),
            P("gx", "gy", None),
        ),
        out_specs=P(None, None, "gx", "gy"),
        check_vma=False,
    )
```

```python
import functools

import jax
import jax.numpy as jnp
from jax import lax
from jax.experimental import pallas as pl
from jax.experimental.pallas import tpu as pltpu
from jax.sharding import PartitionSpec as P

BF16 = jnp.bfloat16
F32 = jnp.float32
VMEM = pltpu.VMEM
SMEM = pltpu.SMEM
HBM = pltpu.HBM
PAIR = 2
LANES = 128
GROUP = 4
KEEP = 11
CHUNK = 5


def call(kernel, out_shape, in_spaces, out_spaces, scratch=(), aliases=None, flops=1000, touched=1000000, vmem=40):
    return pl.pallas_call(
        kernel,
        out_shape=out_shape,
        in_specs=[pl.BlockSpec(memory_space=space) for space in in_spaces],
        out_specs=[pl.BlockSpec(memory_space=space) for space in out_spaces],
        scratch_shapes=scratch,
        input_output_aliases=aliases or {},
        compiler_params=pltpu.CompilerParams(vmem_limit_bytes=vmem * 1024 * 1024),
        cost_estimate=pl.CostEstimate(flops=flops, bytes_accessed=touched, transcendentals=0),
    )


def entry_groups(plan, body):
    capacity = (plan.shape[0] - 1) // 2

    def step(g, carry):
        first = g * GROUP
        body([(plan[1 + first + i], plan[1 + capacity + first + i]) for i in range(GROUP)])
        return carry

    lax.fori_loop(0, (plan[0] + (GROUP - 1)) // GROUP, step, 0)


def shifted_tail(packed, f, at):
    end = packed[f, at, LANES:].astype(F32)
    end = jnp.concatenate([end, jnp.zeros((end.shape[0], LANES - end.shape[1]), F32)], axis=1)
    return pltpu.roll(end, (packed.shape[2] - LANES) * f, 1) if f else end


def unpack_field(packed, planes, f):
    fields = packed.shape[0]
    planes[f] = packed[f, :, :LANES].astype(F32)
    end = shifted_tail(packed, f, slice(None))
    planes[fields] = planes[fields] + end if f else end


def tail_lanes(block, start):
    end = block[:, LANES:]
    return pltpu.roll(end, start, 1) if start else end


def pack_first(
    cols_hbm, count_hbm, owner_hbm, slot_hbm, late_hbm, outbox, plan, cols, count, owner, slot, late, field, rows, codes, used, sems
):
    fields, _, levels = late.shape
    capacity = cols.shape[2]
    owners = used.shape[0]
    tail = levels - LANES
    small = [(cols_hbm, cols), (count_hbm, count), (owner_hbm, owner), (slot_hbm, slot)]
    copies = [pltpu.make_async_copy(source, target, sems.at[i]) for i, (source, target) in enumerate(small)]
    copies += [pltpu.make_async_copy(late_hbm.at[f], late.at[f], sems.at[len(small) + f]) for f in range(fields)]
    for copy in copies:
        copy.start()
    for o in range(owners):
        used[o] = 0
    rows[...] = jnp.zeros(rows.shape, F32)
    codes[...] = jnp.zeros(codes.shape, F32)
    for copy in copies[: len(small)]:
        copy.wait()
    live = count[0, 0]
    plan[0] = live

    def route(e, carry):
        o = owner[0, 0, e]
        rank = used[o]
        used[o] = rank + 1
        plan[1 + e] = cols[0, 0, e]
        plan[1 + capacity + e] = o * PAIR + rank
        codes[pl.ds(o * PAIR + rank, 1), :] = jnp.full((1, LANES), slot[0, 0, e] + 1, jnp.int32).astype(F32)
        return carry

    lax.fori_loop(0, live, route, 0)
    whole = (live // GROUP) * GROUP

    def repeat(e, carry):
        for part in (1, 1 + capacity):
            plan[part + e] = plan[part + whole]
        return carry

    lax.fori_loop(live, ((live + (GROUP - 1)) // GROUP) * GROUP, repeat, 0)
    for f in range(fields):
        copies[len(small) + f].wait()
        unpack_field(late, field, f)
    gather_columns(plan, field, rows)
    pack_rows(rows, codes[...], tail * fields, outbox)


def gather_columns(plan, planes, rows):
    def body(entries):
        found = [(h, at, planes[h, pl.ds(column, 1), :]) for column, at in entries for h in range(planes.shape[0])]
        for h, at, value in found:
            rows[h, pl.ds(at, 1), :] = value

    entry_groups(plan, body)


def pack_rows(rows, codes, code_lane, outbox):
    fields = rows.shape[0] - 1
    lane = lax.broadcasted_iota(jnp.int32, rows.shape[1:], 1)
    tails = jnp.where(lane < code_lane, rows[fields], 0.0)
    if codes is not None:
        tails = jnp.where(lane == code_lane, codes, tails)
    packed = jnp.concatenate([rows[f] for f in range(fields)] + [tails], axis=1)
    outbox[...] = packed.astype(BF16).reshape(outbox.shape)


def split_dot(chosen, value):
    high = value.astype(BF16)
    rest = value - high.astype(F32)
    middle = rest.astype(BF16)
    low = (rest - middle.astype(F32)).astype(BF16)
    dot = functools.partial(jnp.dot, preferred_element_type=F32)
    return dot(chosen, high) + dot(chosen, middle) + dot(chosen, low)


def bring(matrices_hbm, kept, sem):
    copy = pltpu.make_async_copy(matrices_hbm.at[: kept.shape[0]], kept, sem)
    copy.start()
    copy.wait()


def products(chosen, received, matrices, arrivals, answer, spread, result):
    own_slots = len(matrices)
    levels, fields, _ = matrices[0].shape
    owners = received.shape[0]
    depth = levels * fields
    tail = levels - LANES
    iota = functools.partial(lax.broadcasted_iota, jnp.int32)
    values = received[...].reshape(owners * PAIR, received.shape[2]).astype(F32)
    choice = chosen[...].astype(BF16)
    field_of_row = iota((own_slots * fields, levels), 0) % fields
    placed = jnp.zeros((own_slots * fields, levels), F32)
    tails = values[:, fields * LANES :]
    for f in range(fields):
        end = pltpu.roll(tails, LANES - tail * f, 1) if f else tails
        full = jnp.concatenate([values[:, f * LANES : (f + 1) * LANES], end[:, :tail]], axis=1)
        every = lax.dot_general(
            choice, full.astype(BF16), (((0,), (0,)), ((), ())), preferred_element_type=F32
        )
        placed = jnp.where(field_of_row == f, every, placed)
    spreader = (iota((levels, depth), 1) // fields == iota((levels, depth), 0)).astype(F32).astype(BF16)
    own = iota(spread.shape, 1) % fields == iota(spread.shape, 0) % fields
    spread[...] = jnp.where(own, jnp.dot(placed.astype(BF16), spreader, preferred_element_type=F32), 0.0)
    result[...] = jnp.zeros(result.shape, F32)
    for s in range(own_slots):
        at = slice(s * fields, (s + 1) * fields)
        if s in arrivals:
            arrivals[s].wait()
        result[at, :levels] = jnp.dot(
            spread[at].astype(BF16), matrices[s][...].reshape(depth, levels), preferred_element_type=F32
        )
    backward = []
    for k in range(PAIR):
        rows = chosen[pl.ds(k, owners, stride=PAIR), :][:, : own_slots * fields]
        field_of_lane = iota(rows.shape, 1) % fields
        backward += [jnp.where(field_of_lane == f, rows, 0.0) for f in range(fields)]
    rows = split_dot(jnp.concatenate(backward, axis=0).astype(BF16), result[...])
    blocks = [rows[r * owners : (r + 1) * owners] for r in range(PAIR * fields)]
    tails = tail_lanes(blocks[0], 0)
    for r in range(1, PAIR * fields):
        tails = tails + tail_lanes(blocks[r], tail * r)
    answer[...] = jnp.concatenate([block[:, :LANES] for block in blocks] + [tails], axis=1).reshape(answer.shape)


def fetch_rest(kept, matrices_hbm, rest, sems):
    own_slots, keep = matrices_hbm.shape[0], kept.shape[0]
    arrivals = {}
    for i, s in enumerate(range(keep, own_slots, CHUNK)):
        count = min(CHUNK, own_slots - s)
        arrivals[s] = pltpu.make_async_copy(
            matrices_hbm.at[s : s + count], rest.at[s - keep : s - keep + count], sems.at[i]
        )
        arrivals[s].start()
    return [kept.at[s] for s in range(keep)] + [rest.at[s] for s in range(own_slots - keep)], arrivals


def physics_first(received, kept, matrices_hbm, answer, chosen_out, spread, result, rest, sems):
    matrices, arrivals = fetch_rest(kept, matrices_hbm, rest, sems)
    levels, fields = matrices_hbm.shape[1:3]
    owners = received.shape[0]
    code_lane = fields * levels
    codes = received[...].reshape(owners * PAIR, received.shape[2]).astype(F32)[:, code_lane : code_lane + 1]
    wanted = (lax.broadcasted_iota(jnp.int32, chosen_out.shape, 1) // fields + 1).astype(F32)
    chosen_out[...] = (codes == wanted).astype(F32)
    products(chosen_out, received, matrices, arrivals, answer, spread, result)


def physics_second(received, kept, matrices_hbm, chosen, answer, spread, result, rest, sems):
    matrices, arrivals = fetch_rest(kept, matrices_hbm, rest, sems)
    products(chosen, received, matrices, arrivals, answer, spread, result)


def add_first(plan, returned, late, field, *rest, tail):
    for f in range(late.shape[0]):
        unpack_field(late, field, f)
    add_increments(plan, returned, field, field, *rest, tail=tail)


def add_increments(plan, returned, base, field, lon_even, lon_odd, lat_even, lat_odd, inbox, *, tail):
    planes, columns_all, lanes = field.shape
    fields = planes - 1
    owners = returned.shape[0]
    lines = returned[...].reshape(owners, returned.shape[2])
    tails = lines[:, PAIR * fields * lanes :]
    for k in range(PAIR):
        at = pl.ds(k, owners, stride=PAIR)
        for f in range(fields):
            r = k * fields + f
            inbox[f, at, :] = lines[:, r * lanes : (r + 1) * lanes]
        inbox[fields, at, :] = pltpu.roll(tails, lanes - tail * fields * k, 1) if k else tails

    def body(entries):
        found = []
        for column, at in entries:
            for h in range(planes):
                here = (h, pl.ds(column, 1), slice(None))
                found.append((here, base[here] + inbox[h, pl.ds(at, 1), :]))
        for here, value in found:
            field[here] = value

    entry_groups(plan, body)
    span_lon = lat_even.shape[1]
    lon_up, lat_up = upward()
    lon_low, lon_high, lat_low, lat_high = edge_places(columns_all, span_lon)
    for up, even, odd, low_place, high_place in (
        (lon_up, lon_even, lon_odd, lon_low, lon_high),
        (lat_up, lat_even, lat_odd, lat_low, lat_high),
    ):
        for h in range(planes):
            low, high = field[h, low_place, :], field[h, high_place, :]
            even[h, : low.shape[0]] = jnp.where(up, high, low).astype(even.dtype)
            odd[h, : low.shape[0]] = jnp.where(up, low, high).astype(odd.dtype)


def edge_places(columns_all, span_lon):
    span_lat = columns_all // span_lon
    return (
        slice(0, span_lat),
        slice(columns_all - span_lat, columns_all),
        pl.ds(0, span_lon, stride=span_lat),
        pl.ds(span_lat - 1, span_lon, stride=span_lat),
    )


def upward():
    return lax.axis_index("gx") % 2 == 0, lax.axis_index("gy") % 2 == 0


def inner_stencil(field, coef, extra, out):
    planes, columns_all, lanes = field.shape
    fields = planes - 1
    span_lat, span_lon = coef.shape[1:]
    row = lax.broadcasted_iota(jnp.int32, (span_lat, 1), 0)
    for p in range(span_lon):
        weight = [coef[k, :, p : p + 1] for k in range(4)]
        weight[2] = jnp.where(row == 0, 0.0, weight[2])
        weight[3] = jnp.where(row == span_lat - 1, 0.0, weight[3])
        weight = [jnp.broadcast_to(w, (span_lat, lanes)) for w in weight]
        at = slice(p * span_lat, (p + 1) * span_lat)
        for h in range(planes):
            here = field[h, at]
            total = here + weight[2] * pltpu.roll(here, 1, 0) + weight[3] * pltpu.roll(here, span_lat - 1, 0)
            if p > 0:
                total = total + weight[0] * field[h, (p - 1) * span_lat : p * span_lat]
            if p < span_lon - 1:
                total = total + weight[1] * field[h, (p + 1) * span_lat : (p + 2) * span_lat]
            if extra is not None and h < fields:
                total = total + extra[h, at, :lanes].astype(F32)
            elif extra is not None:
                for f in range(fields):
                    total = total + shifted_tail(extra, f, at)
            out[h, at] = total


def inner_first(field, coef, early, out):
    inner_stencil(field, coef, early, out)


def inner_last(field, coef, out):
    inner_stencil(field, coef, None, out)


def edge_weights(coef):
    span_lat, span_lon = coef.shape[1:]
    same = lax.broadcasted_iota(jnp.int32, (span_lon, span_lon), 0) == lax.broadcasted_iota(
        jnp.int32, (span_lon, span_lon), 1
    )

    def upright(line):
        return jnp.sum(jnp.where(same, jnp.broadcast_to(line, (span_lon, span_lon)), 0.0), axis=1, keepdims=True)

    return (
        coef[0, :, :1],
        coef[1, :, span_lon - 1 :],
        upright(coef[2, :1, :]),
        upright(coef[3, span_lat - 1 :, :]),
    )


def add_edges(h, weights, lon_even, lon_odd, lat_even, lat_odd, out):
    columns_all = out.shape[1]
    span_lon = lat_even.shape[1]
    span_lat = columns_all // span_lon
    lon_up, lat_up = upward()
    edges = []
    for up, even, odd, count in ((lon_up, lon_even, lon_odd, span_lat), (lat_up, lat_even, lat_odd, span_lon)):
        first, second = even[h, :count].astype(F32), odd[h, :count].astype(F32)
        edges += [jnp.where(up, second, first), jnp.where(up, first, second)]
    for place, weight, edge in zip(edge_places(columns_all, span_lon), weights, edges):
        at = (h, place, slice(None))
        out[at] = out[at] + weight * edge


def edges_first(plan, inner, coef, lon_odd, lat_odd, lon_even, lat_even, out, outbox, rows, *, tail):
    weights = edge_weights(coef)
    rows[...] = jnp.zeros(rows.shape, F32)
    for h in range(out.shape[0]):
        add_edges(h, weights, lon_even, lon_odd, lat_even, lat_odd, out)
    gather_columns(plan, out, rows)
    pack_rows(rows, None, tail * (out.shape[0] - 1), outbox)


def edges_last(inner, coef, lon_odd, lat_odd, lon_even, lat_even, out_hbm, planes, out, sems):
    fields, _, levels = out.shape
    tail = levels - LANES
    weights = edge_weights(coef)
    add_edges(fields, weights, lon_even, lon_odd, lat_even, lat_odd, planes)
    copies = []
    for f in range(fields):
        add_edges(f, weights, lon_even, lon_odd, lat_even, lat_odd, planes)
        out[f, :, :LANES] = planes[f]
        ends = planes[fields]
        out[f, :, LANES:] = (pltpu.roll(ends, LANES - tail * f, 1) if f else ends)[:, :tail]
        copies.append(pltpu.make_async_copy(out.at[f], out_hbm.at[f], sems.at[f]))
        copies[f].start()
    for copy in copies:
        copy.wait()


def exchange(lines):
    return lax.all_to_all(lines, "gy", split_axis=0, concat_axis=0, tiled=True)


def swap(edge, axis, start, periodic):
    count = lax.axis_size(axis)
    pairs = [(i, i + 1) for i in range(start, count - 1, 2)]
    if start and periodic:
        pairs.append((count - 1, 0))
    return lax.ppermute(edge, axis, pairs + [(high, low) for low, high in pairs])


def halos(lon_even, lon_odd, lat_even, lat_odd):
    lon_odd = swap(lon_odd, "gx", 1, True)
    lat_odd = swap(lat_odd, "gy", 1, False)
    lon_even = swap(lon_even, "gx", 0, True)
    lat_even = swap(lat_even, "gy", 0, False)
    return lon_odd, lat_odd, lon_even, lat_even


def on_device(late, early, stencil_coef, jacobian, cloudy_cols, cloudy_count, owner_rank, owner_slot):
    fields, levels, span_lon, span_lat = late.shape
    groups = lax.axis_size("gy")
    own_slots = jacobian.shape[1]
    capacity = cloudy_cols.shape[2]
    columns_all = span_lon * span_lat
    late = late.transpose(0, 2, 3, 1).reshape(fields, columns_all, levels)
    early = early.transpose(0, 2, 3, 1).reshape(fields, columns_all, levels)
    coef = stencil_coef.transpose(0, 2, 1)
    matrices = jacobian[0].transpose(0, 2, 1, 3)
    shape = jax.ShapeDtypeStruct
    per_owner = PAIR * fields
    grid = (fields, columns_all, levels)
    tail = levels - LANES
    planes = (fields + 1, columns_all, LANES)
    rows_shape = (fields + 1, groups * PAIR, LANES)
    plan_shape = shape((2 * capacity + 1,), jnp.int32)

    outbox_shape = shape((groups, PAIR, (fields + 1) * LANES), BF16)
    outbox, plan = call(
        pack_first,
        [outbox_shape, plan_shape],
        [HBM] * 5,
        [VMEM, SMEM],
        [
            SMEM(cloudy_cols.shape, jnp.int32),
            SMEM(cloudy_count.shape, jnp.int32),
            SMEM(owner_rank.shape, jnp.int32),
            SMEM(owner_slot.shape, jnp.int32),
            VMEM(grid, BF16),
            VMEM(planes, F32),
            VMEM(rows_shape, F32),
            VMEM((groups * PAIR, LANES), F32),
            SMEM((groups,), jnp.int32),
            pltpu.SemaphoreType.DMA((4 + fields,)),
        ],
        vmem=57,
    )(cloudy_cols, cloudy_count, owner_rank, owner_slot, late)
    chosen_shape = shape((groups * PAIR, own_slots * fields), F32)
    answer_shape = shape((groups, 1, (per_owner + 1) * LANES), F32)
    left = own_slots - KEEP
    spaces = [
        VMEM((own_slots * fields, levels * fields), F32),
        VMEM((own_slots * fields, 2 * LANES), F32),
        VMEM((left,) + matrices.shape[1:], BF16),
        pltpu.SemaphoreType.DMA((-(-left // CHUNK),)),
    ]
    (kept,) = call(
        bring,
        [shape((KEEP,) + matrices.shape[1:], BF16)],
        [HBM],
        [VMEM],
        [pltpu.SemaphoreType.DMA(())],
        touched=4000000,
        vmem=50,
    )(matrices)
    answer, chosen = call(
        physics_first,
        [answer_shape, chosen_shape],
        [VMEM, VMEM, HBM],
        [VMEM] * 2,
        spaces,
        vmem=50,
    )(exchange(outbox), kept, matrices)
    returned = exchange(answer)

    def add(kernel, returned, base, aliases, edge_type):
        return call(
            functools.partial(kernel, tail=tail),
            [shape(planes, F32)] + [shape((fields + 1, span_lon, LANES), edge_type)] * 4,
            [SMEM] + [VMEM] * 2,
            [VMEM] * 5,
            [VMEM(rows_shape, F32)],
            aliases,
        )(plan, returned, base)

    field, *edges = add(add_first, returned, late, {}, F32)
    neighbours = halos(*edges)
    (inner,) = call(inner_first, [shape(planes, F32)], [VMEM] * 3, [VMEM], touched=6000000)(field, coef, early)
    adjoint, outbox = call(
        functools.partial(edges_first, tail=tail),
        [shape(planes, F32), outbox_shape],
        [SMEM] + [VMEM] * 6,
        [VMEM] * 2,
        [VMEM(rows_shape, F32)],
        {1: 0},
    )(plan, inner, coef, *neighbours)
    (answer,) = call(physics_second, [answer_shape], [VMEM, VMEM, HBM, VMEM], [VMEM], spaces, vmem=50)(
        exchange(outbox), kept, matrices, chosen
    )
    field, *edges = add(add_increments, exchange(answer), adjoint, {2: 0}, BF16)
    neighbours = halos(*edges)
    (inner,) = call(inner_last, [shape(planes, F32)], [VMEM] * 2, [VMEM], touched=6000000)(field, coef)
    final, _ = call(
        edges_last,
        [shape(grid, F32), shape(planes, F32)],
        [VMEM] * 6,
        [HBM, VMEM],
        [VMEM(grid, F32), pltpu.SemaphoreType.DMA((fields,))],
        {0: 1},
    )(inner, coef, *neighbours)
    return final.reshape(fields, span_lon, span_lat, levels).transpose(0, 3, 1, 2)


def solution(mesh):
    return jax.shard_map(
        on_device,
        mesh=mesh,
        in_specs=(
            P(None, None, "gx", "gy"),
            P(None, None, "gx", "gy"),
            P(None, "gx", "gy"),
            P("gx", "gy", None, None, None),
            P("gx", "gy", None),
            P("gx", "gy"),
            P("gx", "gy", None),
            P("gx", "gy", None),
        ),
        out_specs=P(None, None, "gx", "gy"),
        check_vma=False,
    )
```

```python
import functools

import jax
import jax.numpy as jnp
from jax import lax
from jax.experimental import pallas as pl
from jax.experimental.pallas import tpu as pltpu
from jax.sharding import PartitionSpec as P

BF16 = jnp.bfloat16
F32 = jnp.float32
VMEM = pltpu.VMEM
SMEM = pltpu.SMEM
HBM = pltpu.HBM
PAIR = 2
LANES = 128
GROUP = 4
KEEP = 12
CHUNK = 1


def call(kernel, out_shape, in_spaces, out_spaces, scratch=(), aliases=None, flops=1000, touched=1000000, vmem=40):
    return pl.pallas_call(
        kernel,
        out_shape=out_shape,
        in_specs=[pl.BlockSpec(memory_space=space) for space in in_spaces],
        out_specs=[pl.BlockSpec(memory_space=space) for space in out_spaces],
        scratch_shapes=scratch,
        input_output_aliases=aliases or {},
        compiler_params=pltpu.CompilerParams(vmem_limit_bytes=vmem * 1024 * 1024),
        cost_estimate=pl.CostEstimate(flops=flops, bytes_accessed=touched, transcendentals=0),
    )


def entry_groups(plan, body):
    capacity = (plan.shape[0] - 1) // 2

    def step(g, carry):
        first = g * GROUP
        body([(plan[1 + first + i], plan[1 + capacity + first + i]) for i in range(GROUP)])
        return carry

    lax.fori_loop(0, (plan[0] + (GROUP - 1)) // GROUP, step, 0)


def shifted_tail(packed, f, at):
    end = packed[f, at, LANES:].astype(F32)
    end = jnp.concatenate([end, jnp.zeros((end.shape[0], LANES - end.shape[1]), F32)], axis=1)
    return pltpu.roll(end, (packed.shape[2] - LANES) * f, 1) if f else end


def unpack_field(packed, planes, f):
    fields = packed.shape[0]
    planes[f] = packed[f, :, :LANES].astype(F32)
    end = shifted_tail(packed, f, slice(None))
    planes[fields] = planes[fields] + end if f else end


def tail_lanes(block, start):
    end = block[:, LANES:]
    return pltpu.roll(end, start, 1) if start else end


def pack_first(
    cols_hbm, count_hbm, owner_hbm, slot_hbm, late_hbm, outbox, plan, cols, count, owner, slot, late, field, rows, codes, used, sems
):
    fields, _, levels = late.shape
    capacity = cols.shape[2]
    owners = used.shape[0]
    tail = levels - LANES
    small = [(cols_hbm, cols), (count_hbm, count), (owner_hbm, owner), (slot_hbm, slot)]
    copies = [pltpu.make_async_copy(source, target, sems.at[i]) for i, (source, target) in enumerate(small)]
    copies += [pltpu.make_async_copy(late_hbm.at[f], late.at[f], sems.at[len(small) + f]) for f in range(fields)]
    for copy in copies:
        copy.start()
    for o in range(owners):
        used[o] = 0
    rows[...] = jnp.zeros(rows.shape, F32)
    codes[...] = jnp.zeros(codes.shape, F32)
    for copy in copies[: len(small)]:
        copy.wait()
    live = count[0, 0]
    plan[0] = live

    def route(e, carry):
        o = owner[0, 0, e]
        rank = used[o]
        used[o] = rank + 1
        plan[1 + e] = cols[0, 0, e]
        plan[1 + capacity + e] = o * PAIR + rank
        codes[pl.ds(o * PAIR + rank, 1), :] = jnp.full((1, LANES), slot[0, 0, e] + 1, jnp.int32).astype(F32)
        return carry

    lax.fori_loop(0, live, route, 0)
    whole = (live // GROUP) * GROUP

    def repeat(e, carry):
        for part in (1, 1 + capacity):
            plan[part + e] = plan[part + whole]
        return carry

    lax.fori_loop(live, ((live + (GROUP - 1)) // GROUP) * GROUP, repeat, 0)
    for f in range(fields):
        copies[len(small) + f].wait()
        unpack_field(late, field, f)
    gather_columns(plan, field, rows)
    pack_rows(rows, codes[...], tail * fields, outbox)


def gather_columns(plan, planes, rows):
    def body(entries):
        found = [(h, at, planes[h, pl.ds(column, 1), :]) for column, at in entries for h in range(planes.shape[0])]
        for h, at, value in found:
            rows[h, pl.ds(at, 1), :] = value

    entry_groups(plan, body)


def pack_rows(rows, codes, code_lane, outbox):
    fields = rows.shape[0] - 1
    lane = lax.broadcasted_iota(jnp.int32, rows.shape[1:], 1)
    tails = jnp.where(lane < code_lane, rows[fields], 0.0)
    if codes is not None:
        tails = jnp.where(lane == code_lane, codes, tails)
    packed = jnp.concatenate([rows[f] for f in range(fields)] + [tails], axis=1)
    outbox[...] = packed.astype(BF16).reshape(outbox.shape)


def split_dot(chosen, value):
    high = value.astype(BF16)
    rest = value - high.astype(F32)
    middle = rest.astype(BF16)
    low = (rest - middle.astype(F32)).astype(BF16)
    dot = functools.partial(jnp.dot, preferred_element_type=F32)
    return dot(chosen, high) + dot(chosen, middle) + dot(chosen, low)


def bring(matrices_hbm, kept, sem):
    copy = pltpu.make_async_copy(matrices_hbm.at[: kept.shape[0]], kept, sem)
    copy.start()
    copy.wait()


def products(chosen, received, matrices, arrivals, answer, spread, result):
    own_slots = len(matrices)
    levels, fields, _ = matrices[0].shape
    owners = received.shape[0]
    depth = levels * fields
    tail = levels - LANES
    iota = functools.partial(lax.broadcasted_iota, jnp.int32)
    values = received[...].reshape(owners * PAIR, received.shape[2]).astype(F32)
    choice = chosen[...].astype(BF16)
    field_of_row = iota((own_slots * fields, levels), 0) % fields
    placed = jnp.zeros((own_slots * fields, levels), F32)
    tails = values[:, fields * LANES :]
    for f in range(fields):
        end = pltpu.roll(tails, LANES - tail * f, 1) if f else tails
        full = jnp.concatenate([values[:, f * LANES : (f + 1) * LANES], end[:, :tail]], axis=1)
        every = lax.dot_general(
            choice, full.astype(BF16), (((0,), (0,)), ((), ())), preferred_element_type=F32
        )
        placed = jnp.where(field_of_row == f, every, placed)
    spreader = (iota((levels, depth), 1) // fields == iota((levels, depth), 0)).astype(F32).astype(BF16)
    own = iota(spread.shape, 1) % fields == iota(spread.shape, 0) % fields
    spread[...] = jnp.where(own, jnp.dot(placed.astype(BF16), spreader, preferred_element_type=F32), 0.0)
    result[...] = jnp.zeros(result.shape, F32)
    for s in range(own_slots):
        at = slice(s * fields, (s + 1) * fields)
        if s in arrivals:
            arrivals[s].wait()
        result[at, :levels] = jnp.dot(
            spread[at].astype(BF16), matrices[s][...].reshape(depth, levels), preferred_element_type=F32
        )
    backward = []
    for k in range(PAIR):
        rows = chosen[pl.ds(k, owners, stride=PAIR), :][:, : own_slots * fields]
        field_of_lane = iota(rows.shape, 1) % fields
        backward += [jnp.where(field_of_lane == f, rows, 0.0) for f in range(fields)]
    rows = split_dot(jnp.concatenate(backward, axis=0).astype(BF16), result[...])
    blocks = [rows[r * owners : (r + 1) * owners] for r in range(PAIR * fields)]
    tails = tail_lanes(blocks[0], 0)
    for r in range(1, PAIR * fields):
        tails = tails + tail_lanes(blocks[r], tail * r)
    answer[...] = jnp.concatenate([block[:, :LANES] for block in blocks] + [tails], axis=1).reshape(answer.shape)


def fetch_rest(kept, matrices_hbm, rest, sems):
    own_slots, keep = matrices_hbm.shape[0], kept.shape[0]
    arrivals = {}
    for i, s in enumerate(range(keep, own_slots, CHUNK)):
        count = min(CHUNK, own_slots - s)
        arrivals[s] = pltpu.make_async_copy(
            matrices_hbm.at[s : s + count], rest.at[s - keep : s - keep + count], sems.at[i]
        )
        arrivals[s].start()
    return [kept.at[s] for s in range(keep)] + [rest.at[s] for s in range(own_slots - keep)], arrivals


def physics_first(received, kept, matrices_hbm, answer, chosen_out, spread, result, rest, sems):
    matrices, arrivals = fetch_rest(kept, matrices_hbm, rest, sems)
    levels, fields = matrices_hbm.shape[1:3]
    owners = received.shape[0]
    code_lane = fields * levels
    codes = received[...].reshape(owners * PAIR, received.shape[2]).astype(F32)[:, code_lane : code_lane + 1]
    wanted = (lax.broadcasted_iota(jnp.int32, chosen_out.shape, 1) // fields + 1).astype(F32)
    chosen_out[...] = (codes == wanted).astype(F32)
    products(chosen_out, received, matrices, arrivals, answer, spread, result)


def physics_second(received, kept, matrices_hbm, chosen, answer, spread, result, rest, sems):
    matrices, arrivals = fetch_rest(kept, matrices_hbm, rest, sems)
    products(chosen, received, matrices, arrivals, answer, spread, result)


def add_first(plan, returned, late, field, *rest, tail):
    for f in range(late.shape[0]):
        unpack_field(late, field, f)
    add_increments(plan, returned, field, field, *rest, tail=tail)


def add_increments(plan, returned, base, field, lon_even, lon_odd, lat_even, lat_odd, inbox, *, tail):
    planes, columns_all, lanes = field.shape
    fields = planes - 1
    owners = returned.shape[0]
    lines = returned[...].reshape(owners, returned.shape[2])
    tails = lines[:, PAIR * fields * lanes :]
    for k in range(PAIR):
        at = pl.ds(k, owners, stride=PAIR)
        for f in range(fields):
            r = k * fields + f
            inbox[f, at, :] = lines[:, r * lanes : (r + 1) * lanes]
        inbox[fields, at, :] = pltpu.roll(tails, lanes - tail * fields * k, 1) if k else tails

    def body(entries):
        found = []
        for column, at in entries:
            for h in range(planes):
                here = (h, pl.ds(column, 1), slice(None))
                found.append((here, base[here] + inbox[h, pl.ds(at, 1), :]))
        for here, value in found:
            field[here] = value

    entry_groups(plan, body)
    span_lon = lat_even.shape[1]
    lon_up, lat_up = upward()
    lon_low, lon_high, lat_low, lat_high = edge_places(columns_all, span_lon)
    for up, even, odd, low_place, high_place in (
        (lon_up, lon_even, lon_odd, lon_low, lon_high),
        (lat_up, lat_even, lat_odd, lat_low, lat_high),
    ):
        for h in range(planes):
            low, high = field[h, low_place, :], field[h, high_place, :]
            even[h, : low.shape[0]] = jnp.where(up, high, low).astype(even.dtype)
            odd[h, : low.shape[0]] = jnp.where(up, low, high).astype(odd.dtype)


def edge_places(columns_all, span_lon):
    span_lat = columns_all // span_lon
    return (
        slice(0, span_lat),
        slice(columns_all - span_lat, columns_all),
        pl.ds(0, span_lon, stride=span_lat),
        pl.ds(span_lat - 1, span_lon, stride=span_lat),
    )


def upward():
    return lax.axis_index("gx") % 2 == 0, lax.axis_index("gy") % 2 == 0


def inner_stencil(field, coef, extra, out):
    planes, columns_all, lanes = field.shape
    fields = planes - 1
    span_lat, span_lon = coef.shape[1:]
    row = lax.broadcasted_iota(jnp.int32, (span_lat, 1), 0)
    for p in range(span_lon):
        weight = [coef[k, :, p : p + 1] for k in range(4)]
        weight[2] = jnp.where(row == 0, 0.0, weight[2])
        weight[3] = jnp.where(row == span_lat - 1, 0.0, weight[3])
        weight = [jnp.broadcast_to(w, (span_lat, lanes)) for w in weight]
        at = slice(p * span_lat, (p + 1) * span_lat)
        for h in range(planes):
            here = field[h, at]
            total = here + weight[2] * pltpu.roll(here, 1, 0) + weight[3] * pltpu.roll(here, span_lat - 1, 0)
            if p > 0:
                total = total + weight[0] * field[h, (p - 1) * span_lat : p * span_lat]
            if p < span_lon - 1:
                total = total + weight[1] * field[h, (p + 1) * span_lat : (p + 2) * span_lat]
            if extra is not None and h < fields:
                total = total + extra[h, at, :lanes].astype(F32)
            elif extra is not None:
                for f in range(fields):
                    total = total + shifted_tail(extra, f, at)
            out[h, at] = total


def inner_first(field, coef, early, out):
    inner_stencil(field, coef, early, out)


def inner_last(field, coef, out):
    inner_stencil(field, coef, None, out)


def edge_weights(coef):
    span_lat, span_lon = coef.shape[1:]
    same = lax.broadcasted_iota(jnp.int32, (span_lon, span_lon), 0) == lax.broadcasted_iota(
        jnp.int32, (span_lon, span_lon), 1
    )

    def upright(line):
        return jnp.sum(jnp.where(same, jnp.broadcast_to(line, (span_lon, span_lon)), 0.0), axis=1, keepdims=True)

    return (
        coef[0, :, :1],
        coef[1, :, span_lon - 1 :],
        upright(coef[2, :1, :]),
        upright(coef[3, span_lat - 1 :, :]),
    )


def add_edges(h, weights, lon_even, lon_odd, lat_even, lat_odd, out):
    columns_all = out.shape[1]
    span_lon = lat_even.shape[1]
    span_lat = columns_all // span_lon
    lon_up, lat_up = upward()
    edges = []
    for up, even, odd, count in ((lon_up, lon_even, lon_odd, span_lat), (lat_up, lat_even, lat_odd, span_lon)):
        first, second = even[h, :count].astype(F32), odd[h, :count].astype(F32)
        edges += [jnp.where(up, second, first), jnp.where(up, first, second)]
    for place, weight, edge in zip(edge_places(columns_all, span_lon), weights, edges):
        at = (h, place, slice(None))
        out[at] = out[at] + weight * edge


def edges_first(plan, inner, coef, lon_odd, lat_odd, lon_even, lat_even, out, outbox, rows, *, tail):
    weights = edge_weights(coef)
    rows[...] = jnp.zeros(rows.shape, F32)
    for h in range(out.shape[0]):
        add_edges(h, weights, lon_even, lon_odd, lat_even, lat_odd, out)
    gather_columns(plan, out, rows)
    pack_rows(rows, None, tail * (out.shape[0] - 1), outbox)


def edges_last(inner, coef, lon_odd, lat_odd, lon_even, lat_even, out_hbm, planes, out, sems):
    fields, _, levels = out.shape
    tail = levels - LANES
    weights = edge_weights(coef)
    add_edges(fields, weights, lon_even, lon_odd, lat_even, lat_odd, planes)
    copies = []
    for f in range(fields):
        add_edges(f, weights, lon_even, lon_odd, lat_even, lat_odd, planes)
        out[f, :, :LANES] = planes[f]
        ends = planes[fields]
        out[f, :, LANES:] = (pltpu.roll(ends, LANES - tail * f, 1) if f else ends)[:, :tail]
        copies.append(pltpu.make_async_copy(out.at[f], out_hbm.at[f], sems.at[f]))
        copies[f].start()
    for copy in copies:
        copy.wait()


def exchange(lines):
    return lax.all_to_all(lines, "gy", split_axis=0, concat_axis=0, tiled=True)


def swap(edge, axis, start, periodic):
    count = lax.axis_size(axis)
    pairs = [(i, i + 1) for i in range(start, count - 1, 2)]
    if start and periodic:
        pairs.append((count - 1, 0))
    return lax.ppermute(edge, axis, pairs + [(high, low) for low, high in pairs])


def halos(lon_even, lon_odd, lat_even, lat_odd):
    lon_odd = swap(lon_odd, "gx", 1, True)
    lat_odd = swap(lat_odd, "gy", 1, False)
    lon_even = swap(lon_even, "gx", 0, True)
    lat_even = swap(lat_even, "gy", 0, False)
    return lon_odd, lat_odd, lon_even, lat_even


def on_device(late, early, stencil_coef, jacobian, cloudy_cols, cloudy_count, owner_rank, owner_slot):
    fields, levels, span_lon, span_lat = late.shape
    groups = lax.axis_size("gy")
    own_slots = jacobian.shape[1]
    capacity = cloudy_cols.shape[2]
    columns_all = span_lon * span_lat
    late = late.transpose(0, 2, 3, 1).reshape(fields, columns_all, levels)
    early = early.transpose(0, 2, 3, 1).reshape(fields, columns_all, levels)
    coef = stencil_coef.transpose(0, 2, 1)
    matrices = jacobian[0].transpose(0, 2, 1, 3)
    shape = jax.ShapeDtypeStruct
    per_owner = PAIR * fields
    grid = (fields, columns_all, levels)
    tail = levels - LANES
    planes = (fields + 1, columns_all, LANES)
    rows_shape = (fields + 1, groups * PAIR, LANES)
    plan_shape = shape((2 * capacity + 1,), jnp.int32)

    outbox_shape = shape((groups, PAIR, (fields + 1) * LANES), BF16)
    outbox, plan = call(
        pack_first,
        [outbox_shape, plan_shape],
        [HBM] * 5,
        [VMEM, SMEM],
        [
            SMEM(cloudy_cols.shape, jnp.int32),
            SMEM(cloudy_count.shape, jnp.int32),
            SMEM(owner_rank.shape, jnp.int32),
            SMEM(owner_slot.shape, jnp.int32),
            VMEM(grid, BF16),
            VMEM(planes, F32),
            VMEM(rows_shape, F32),
            VMEM((groups * PAIR, LANES), F32),
            SMEM((groups,), jnp.int32),
            pltpu.SemaphoreType.DMA((4 + fields,)),
        ],
        vmem=57,
    )(cloudy_cols, cloudy_count, owner_rank, owner_slot, late)
    chosen_shape = shape((groups * PAIR, own_slots * fields), F32)
    answer_shape = shape((groups, 1, (per_owner + 1) * LANES), F32)
    left = own_slots - KEEP
    spaces = [
        VMEM((own_slots * fields, levels * fields), F32),
        VMEM((own_slots * fields, 2 * LANES), F32),
        VMEM((left,) + matrices.shape[1:], BF16),
        pltpu.SemaphoreType.DMA((-(-left // CHUNK),)),
    ]
    (kept,) = call(
        bring,
        [shape((KEEP,) + matrices.shape[1:], BF16)],
        [HBM],
        [VMEM],
        [pltpu.SemaphoreType.DMA(())],
        touched=4000000,
        vmem=50,
    )(matrices)
    answer, chosen = call(
        physics_first,
        [answer_shape, chosen_shape],
        [VMEM, VMEM, HBM],
        [VMEM] * 2,
        spaces,
        vmem=50,
    )(exchange(outbox), kept, matrices)
    returned = exchange(answer)

    def add(kernel, returned, base, aliases, edge_type):
        return call(
            functools.partial(kernel, tail=tail),
            [shape(planes, F32)] + [shape((fields + 1, span_lon, LANES), edge_type)] * 4,
            [SMEM] + [VMEM] * 2,
            [VMEM] * 5,
            [VMEM(rows_shape, F32)],
            aliases,
        )(plan, returned, base)

    field, *edges = add(add_first, returned, late, {}, F32)
    neighbours = halos(*edges)
    (inner,) = call(inner_first, [shape(planes, F32)], [VMEM] * 3, [VMEM], touched=6000000)(field, coef, early)
    adjoint, outbox = call(
        functools.partial(edges_first, tail=tail),
        [shape(planes, F32), outbox_shape],
        [SMEM] + [VMEM] * 6,
        [VMEM] * 2,
        [VMEM(rows_shape, F32)],
        {1: 0},
    )(plan, inner, coef, *neighbours)
    (answer,) = call(physics_second, [answer_shape], [VMEM, VMEM, HBM, VMEM], [VMEM], spaces, vmem=50)(
        exchange(outbox), kept, matrices, chosen
    )
    field, *edges = add(add_increments, exchange(answer), adjoint, {2: 0}, BF16)
    neighbours = halos(*edges)
    (inner,) = call(inner_last, [shape(planes, F32)], [VMEM] * 2, [VMEM], touched=6000000)(field, coef)
    final, _ = call(
        edges_last,
        [shape(grid, F32), shape(planes, F32)],
        [VMEM] * 6,
        [HBM, VMEM],
        [VMEM(grid, F32), pltpu.SemaphoreType.DMA((fields,))],
        {0: 1},
    )(inner, coef, *neighbours)
    return final.reshape(fields, span_lon, span_lat, levels).transpose(0, 3, 1, 2)


def solution(mesh):
    return jax.shard_map(
        on_device,
        mesh=mesh,
        in_specs=(
            P(None, None, "gx", "gy"),
            P(None, None, "gx", "gy"),
            P(None, "gx", "gy"),
            P("gx", "gy", None, None, None),
            P("gx", "gy", None),
            P("gx", "gy"),
            P("gx", "gy", None),
            P("gx", "gy", None),
        ),
        out_specs=P(None, None, "gx", "gy"),
        check_vma=False,
    )
```

```python
import functools

import jax
import jax.numpy as jnp
from jax import lax
from jax.experimental import pallas as pl
from jax.experimental.pallas import tpu as pltpu
from jax.sharding import PartitionSpec as P

BF16 = jnp.bfloat16
F32 = jnp.float32
VMEM = pltpu.VMEM
SMEM = pltpu.SMEM
HBM = pltpu.HBM
PAIR = 2
LANES = 128
GROUP = 8
KEEP = 11
CHUNK = 5


def call(kernel, out_shape, in_spaces, out_spaces, scratch=(), aliases=None, flops=1000, touched=1000000, vmem=40):
    return pl.pallas_call(
        kernel,
        out_shape=out_shape,
        in_specs=[pl.BlockSpec(memory_space=space) for space in in_spaces],
        out_specs=[pl.BlockSpec(memory_space=space) for space in out_spaces],
        scratch_shapes=scratch,
        input_output_aliases=aliases or {},
        compiler_params=pltpu.CompilerParams(vmem_limit_bytes=vmem * 1024 * 1024),
        cost_estimate=pl.CostEstimate(flops=flops, bytes_accessed=touched, transcendentals=0),
    )


def entry_groups(plan, body):
    capacity = (plan.shape[0] - 1) // 2

    def step(g, carry):
        first = g * GROUP
        body([(plan[1 + first + i], plan[1 + capacity + first + i]) for i in range(GROUP)])
        return carry

    lax.fori_loop(0, (plan[0] + (GROUP - 1)) // GROUP, step, 0)


def shifted_tail(packed, f, at):
    end = packed[f, at, LANES:].astype(F32)
    end = jnp.concatenate([end, jnp.zeros((end.shape[0], LANES - end.shape[1]), F32)], axis=1)
    return pltpu.roll(end, (packed.shape[2] - LANES) * f, 1) if f else end


def unpack_field(packed, planes, f):
    fields = packed.shape[0]
    planes[f] = packed[f, :, :LANES].astype(F32)
    end = shifted_tail(packed, f, slice(None))
    planes[fields] = planes[fields] + end if f else end


def tail_lanes(block, start):
    end = block[:, LANES:]
    return pltpu.roll(end, start, 1) if start else end


def pack_first(
    cols_hbm, count_hbm, owner_hbm, slot_hbm, late_hbm, outbox, plan, cols, count, owner, slot, late, field, rows, codes, used, sems
):
    fields, _, levels = late.shape
    capacity = cols.shape[2]
    owners = used.shape[0]
    tail = levels - LANES
    small = [(cols_hbm, cols), (count_hbm, count), (owner_hbm, owner), (slot_hbm, slot)]
    copies = [pltpu.make_async_copy(source, target, sems.at[i]) for i, (source, target) in enumerate(small)]
    copies += [pltpu.make_async_copy(late_hbm.at[f], late.at[f], sems.at[len(small) + f]) for f in range(fields)]
    for copy in copies:
        copy.start()
    for o in range(owners):
        used[o] = 0
    rows[...] = jnp.zeros(rows.shape, F32)
    codes[...] = jnp.zeros(codes.shape, F32)
    for copy in copies[: len(small)]:
        copy.wait()
    live = count[0, 0]
    plan[0] = live

    def route(e, carry):
        o = owner[0, 0, e]
        rank = used[o]
        used[o] = rank + 1
        plan[1 + e] = cols[0, 0, e]
        plan[1 + capacity + e] = o * PAIR + rank
        codes[pl.ds(o * PAIR + rank, 1), :] = jnp.full((1, LANES), slot[0, 0, e] + 1, jnp.int32).astype(F32)
        return carry

    lax.fori_loop(0, live, route, 0)
    whole = (live // GROUP) * GROUP

    def repeat(e, carry):
        for part in (1, 1 + capacity):
            plan[part + e] = plan[part + whole]
        return carry

    lax.fori_loop(live, ((live + (GROUP - 1)) // GROUP) * GROUP, repeat, 0)
    for f in range(fields):
        copies[len(small) + f].wait()
        unpack_field(late, field, f)
    gather_columns(plan, field, rows)
    pack_rows(rows, codes[...], tail * fields, outbox)


def gather_columns(plan, planes, rows):
    def body(entries):
        found = [(h, at, planes[h, pl.ds(column, 1), :]) for column, at in entries for h in range(planes.shape[0])]
        for h, at, value in found:
            rows[h, pl.ds(at, 1), :] = value

    entry_groups(plan, body)


def pack_rows(rows, codes, code_lane, outbox):
    fields = rows.shape[0] - 1
    lane = lax.broadcasted_iota(jnp.int32, rows.shape[1:], 1)
    tails = jnp.where(lane < code_lane, rows[fields], 0.0)
    if codes is not None:
        tails = jnp.where(lane == code_lane, codes, tails)
    packed = jnp.concatenate([rows[f] for f in range(fields)] + [tails], axis=1)
    outbox[...] = packed.astype(BF16).reshape(outbox.shape)


def split_dot(chosen, value):
    high = value.astype(BF16)
    rest = value - high.astype(F32)
    middle = rest.astype(BF16)
    low = (rest - middle.astype(F32)).astype(BF16)
    dot = functools.partial(jnp.dot, preferred_element_type=F32)
    return dot(chosen, high) + dot(chosen, middle) + dot(chosen, low)


def bring(matrices_hbm, kept, sem):
    copy = pltpu.make_async_copy(matrices_hbm.at[: kept.shape[0]], kept, sem)
    copy.start()
    copy.wait()


def products(chosen, received, matrices, arrivals, answer, spread, result):
    own_slots = len(matrices)
    levels, fields, _ = matrices[0].shape
    owners = received.shape[0]
    depth = levels * fields
    tail = levels - LANES
    iota = functools.partial(lax.broadcasted_iota, jnp.int32)
    values = received[...].reshape(owners * PAIR, received.shape[2]).astype(F32)
    choice = chosen[...].astype(BF16)
    field_of_row = iota((own_slots * fields, levels), 0) % fields
    placed = jnp.zeros((own_slots * fields, levels), F32)
    tails = values[:, fields * LANES :]
    for f in range(fields):
        end = pltpu.roll(tails, LANES - tail * f, 1) if f else tails
        full = jnp.concatenate([values[:, f * LANES : (f + 1) * LANES], end[:, :tail]], axis=1)
        every = lax.dot_general(
            choice, full.astype(BF16), (((0,), (0,)), ((), ())), preferred_element_type=F32
        )
        placed = jnp.where(field_of_row == f, every, placed)
    spreader = (iota((levels, depth), 1) // fields == iota((levels, depth), 0)).astype(F32).astype(BF16)
    own = iota(spread.shape, 1) % fields == iota(spread.shape, 0) % fields
    spread[...] = jnp.where(own, jnp.dot(placed.astype(BF16), spreader, preferred_element_type=F32), 0.0)
    result[...] = jnp.zeros(result.shape, F32)
    for s in range(own_slots):
        at = slice(s * fields, (s + 1) * fields)
        if s in arrivals:
            arrivals[s].wait()
        result[at, :levels] = jnp.dot(
            spread[at].astype(BF16), matrices[s][...].reshape(depth, levels), preferred_element_type=F32
        )
    backward = []
    for k in range(PAIR):
        rows = chosen[pl.ds(k, owners, stride=PAIR), :][:, : own_slots * fields]
        field_of_lane = iota(rows.shape, 1) % fields
        backward += [jnp.where(field_of_lane == f, rows, 0.0) for f in range(fields)]
    rows = split_dot(jnp.concatenate(backward, axis=0).astype(BF16), result[...])
    blocks = [rows[r * owners : (r + 1) * owners] for r in range(PAIR * fields)]
    tails = tail_lanes(blocks[0], 0)
    for r in range(1, PAIR * fields):
        tails = tails + tail_lanes(blocks[r], tail * r)
    answer[...] = jnp.concatenate([block[:, :LANES] for block in blocks] + [tails], axis=1).reshape(answer.shape)


def fetch_rest(kept, matrices_hbm, rest, sems):
    own_slots, keep = matrices_hbm.shape[0], kept.shape[0]
    arrivals = {}
    for i, s in enumerate(range(keep, own_slots, CHUNK)):
        count = min(CHUNK, own_slots - s)
        arrivals[s] = pltpu.make_async_copy(
            matrices_hbm.at[s : s + count], rest.at[s - keep : s - keep + count], sems.at[i]
        )
        arrivals[s].start()
    return [kept.at[s] for s in range(keep)] + [rest.at[s] for s in range(own_slots - keep)], arrivals


def physics_first(received, kept, matrices_hbm, answer, chosen_out, spread, result, rest, sems):
    matrices, arrivals = fetch_rest(kept, matrices_hbm, rest, sems)
    levels, fields = matrices_hbm.shape[1:3]
    owners = received.shape[0]
    code_lane = fields * levels
    codes = received[...].reshape(owners * PAIR, received.shape[2]).astype(F32)[:, code_lane : code_lane + 1]
    wanted = (lax.broadcasted_iota(jnp.int32, chosen_out.shape, 1) // fields + 1).astype(F32)
    chosen_out[...] = (codes == wanted).astype(F32)
    products(chosen_out, received, matrices, arrivals, answer, spread, result)


def physics_second(received, kept, matrices_hbm, chosen, answer, spread, result, rest, sems):
    matrices, arrivals = fetch_rest(kept, matrices_hbm, rest, sems)
    products(chosen, received, matrices, arrivals, answer, spread, result)


def add_first(plan, returned, late, field, *rest, tail):
    for f in range(late.shape[0]):
        unpack_field(late, field, f)
    add_increments(plan, returned, field, field, *rest, tail=tail)


def add_increments(plan, returned, base, field, lon_even, lon_odd, lat_even, lat_odd, inbox, *, tail):
    planes, columns_all, lanes = field.shape
    fields = planes - 1
    owners = returned.shape[0]
    lines = returned[...].reshape(owners, returned.shape[2])
    tails = lines[:, PAIR * fields * lanes :]
    for k in range(PAIR):
        at = pl.ds(k, owners, stride=PAIR)
        for f in range(fields):
            r = k * fields + f
            inbox[f, at, :] = lines[:, r * lanes : (r + 1) * lanes]
        inbox[fields, at, :] = pltpu.roll(tails, lanes - tail * fields * k, 1) if k else tails

    def body(entries):
        found = []
        for column, at in entries:
            for h in range(planes):
                here = (h, pl.ds(column, 1), slice(None))
                found.append((here, base[here] + inbox[h, pl.ds(at, 1), :]))
        for here, value in found:
            field[here] = value

    entry_groups(plan, body)
    span_lon = lat_even.shape[1]
    lon_up, lat_up = upward()
    lon_low, lon_high, lat_low, lat_high = edge_places(columns_all, span_lon)
    for up, even, odd, low_place, high_place in (
        (lon_up, lon_even, lon_odd, lon_low, lon_high),
        (lat_up, lat_even, lat_odd, lat_low, lat_high),
    ):
        for h in range(planes):
            low, high = field[h, low_place, :], field[h, high_place, :]
            even[h, : low.shape[0]] = jnp.where(up, high, low).astype(even.dtype)
            odd[h, : low.shape[0]] = jnp.where(up, low, high).astype(odd.dtype)


def edge_places(columns_all, span_lon):
    span_lat = columns_all // span_lon
    return (
        slice(0, span_lat),
        slice(columns_all - span_lat, columns_all),
        pl.ds(0, span_lon, stride=span_lat),
        pl.ds(span_lat - 1, span_lon, stride=span_lat),
    )


def upward():
    return lax.axis_index("gx") % 2 == 0, lax.axis_index("gy") % 2 == 0


def inner_stencil(field, coef, extra, out):
    planes, columns_all, lanes = field.shape
    fields = planes - 1
    span_lat, span_lon = coef.shape[1:]
    row = lax.broadcasted_iota(jnp.int32, (span_lat, 1), 0)
    for p in range(span_lon):
        weight = [coef[k, :, p : p + 1] for k in range(4)]
        weight[2] = jnp.where(row == 0, 0.0, weight[2])
        weight[3] = jnp.where(row == span_lat - 1, 0.0, weight[3])
        weight = [jnp.broadcast_to(w, (span_lat, lanes)) for w in weight]
        at = slice(p * span_lat, (p + 1) * span_lat)
        for h in range(planes):
            here = field[h, at]
            total = here + weight[2] * pltpu.roll(here, 1, 0) + weight[3] * pltpu.roll(here, span_lat - 1, 0)
            if p > 0:
                total = total + weight[0] * field[h, (p - 1) * span_lat : p * span_lat]
            if p < span_lon - 1:
                total = total + weight[1] * field[h, (p + 1) * span_lat : (p + 2) * span_lat]
            if extra is not None and h < fields:
                total = total + extra[h, at, :lanes].astype(F32)
            elif extra is not None:
                for f in range(fields):
                    total = total + shifted_tail(extra, f, at)
            out[h, at] = total


def inner_first(field, coef, early, out):
    inner_stencil(field, coef, early, out)


def inner_last(field, coef, out):
    inner_stencil(field, coef, None, out)


def edge_weights(coef):
    span_lat, span_lon = coef.shape[1:]
    same = lax.broadcasted_iota(jnp.int32, (span_lon, span_lon), 0) == lax.broadcasted_iota(
        jnp.int32, (span_lon, span_lon), 1
    )

    def upright(line):
        return jnp.sum(jnp.where(same, jnp.broadcast_to(line, (span_lon, span_lon)), 0.0), axis=1, keepdims=True)

    return (
        coef[0, :, :1],
        coef[1, :, span_lon - 1 :],
        upright(coef[2, :1, :]),
        upright(coef[3, span_lat - 1 :, :]),
    )


def add_edges(h, weights, lon_even, lon_odd, lat_even, lat_odd, out):
    columns_all = out.shape[1]
    span_lon = lat_even.shape[1]
    span_lat = columns_all // span_lon
    lon_up, lat_up = upward()
    edges = []
    for up, even, odd, count in ((lon_up, lon_even, lon_odd, span_lat), (lat_up, lat_even, lat_odd, span_lon)):
        first, second = even[h, :count].astype(F32), odd[h, :count].astype(F32)
        edges += [jnp.where(up, second, first), jnp.where(up, first, second)]
    for place, weight, edge in zip(edge_places(columns_all, span_lon), weights, edges):
        at = (h, place, slice(None))
        out[at] = out[at] + weight * edge


def edges_first(plan, inner, coef, lon_odd, lat_odd, lon_even, lat_even, out, outbox, rows, *, tail):
    weights = edge_weights(coef)
    rows[...] = jnp.zeros(rows.shape, F32)
    for h in range(out.shape[0]):
        add_edges(h, weights, lon_even, lon_odd, lat_even, lat_odd, out)
    gather_columns(plan, out, rows)
    pack_rows(rows, None, tail * (out.shape[0] - 1), outbox)


def edges_last(inner, coef, lon_odd, lat_odd, lon_even, lat_even, out_hbm, planes, out, sems):
    fields, _, levels = out.shape
    tail = levels - LANES
    weights = edge_weights(coef)
    add_edges(fields, weights, lon_even, lon_odd, lat_even, lat_odd, planes)
    copies = []
    for f in range(fields):
        add_edges(f, weights, lon_even, lon_odd, lat_even, lat_odd, planes)
        out[f, :, :LANES] = planes[f]
        ends = planes[fields]
        out[f, :, LANES:] = (pltpu.roll(ends, LANES - tail * f, 1) if f else ends)[:, :tail]
        copies.append(pltpu.make_async_copy(out.at[f], out_hbm.at[f], sems.at[f]))
        copies[f].start()
    for copy in copies:
        copy.wait()


def exchange(lines):
    return lax.all_to_all(lines, "gy", split_axis=0, concat_axis=0, tiled=True)


def swap(edge, axis, start, periodic):
    count = lax.axis_size(axis)
    pairs = [(i, i + 1) for i in range(start, count - 1, 2)]
    if start and periodic:
        pairs.append((count - 1, 0))
    return lax.ppermute(edge, axis, pairs + [(high, low) for low, high in pairs])


def halos(lon_even, lon_odd, lat_even, lat_odd):
    lon_odd = swap(lon_odd, "gx", 1, True)
    lat_odd = swap(lat_odd, "gy", 1, False)
    lon_even = swap(lon_even, "gx", 0, True)
    lat_even = swap(lat_even, "gy", 0, False)
    return lon_odd, lat_odd, lon_even, lat_even


def on_device(late, early, stencil_coef, jacobian, cloudy_cols, cloudy_count, owner_rank, owner_slot):
    fields, levels, span_lon, span_lat = late.shape
    groups = lax.axis_size("gy")
    own_slots = jacobian.shape[1]
    capacity = cloudy_cols.shape[2]
    columns_all = span_lon * span_lat
    late = late.transpose(0, 2, 3, 1).reshape(fields, columns_all, levels)
    early = early.transpose(0, 2, 3, 1).reshape(fields, columns_all, levels)
    coef = stencil_coef.transpose(0, 2, 1)
    matrices = jacobian[0].transpose(0, 2, 1, 3)
    shape = jax.ShapeDtypeStruct
    per_owner = PAIR * fields
    grid = (fields, columns_all, levels)
    tail = levels - LANES
    planes = (fields + 1, columns_all, LANES)
    rows_shape = (fields + 1, groups * PAIR, LANES)
    plan_shape = shape((2 * capacity + 1,), jnp.int32)

    outbox_shape = shape((groups, PAIR, (fields + 1) * LANES), BF16)
    outbox, plan = call(
        pack_first,
        [outbox_shape, plan_shape],
        [HBM] * 5,
        [VMEM, SMEM],
        [
            SMEM(cloudy_cols.shape, jnp.int32),
            SMEM(cloudy_count.shape, jnp.int32),
            SMEM(owner_rank.shape, jnp.int32),
            SMEM(owner_slot.shape, jnp.int32),
            VMEM(grid, BF16),
            VMEM(planes, F32),
            VMEM(rows_shape, F32),
            VMEM((groups * PAIR, LANES), F32),
            SMEM((groups,), jnp.int32),
            pltpu.SemaphoreType.DMA((4 + fields,)),
        ],
        vmem=57,
    )(cloudy_cols, cloudy_count, owner_rank, owner_slot, late)
    chosen_shape = shape((groups * PAIR, own_slots * fields), F32)
    answer_shape = shape((groups, 1, (per_owner + 1) * LANES), F32)
    left = own_slots - KEEP
    spaces = [
        VMEM((own_slots * fields, levels * fields), F32),
        VMEM((own_slots * fields, 2 * LANES), F32),
        VMEM((left,) + matrices.shape[1:], BF16),
        pltpu.SemaphoreType.DMA((-(-left // CHUNK),)),
    ]
    (kept,) = call(
        bring,
        [shape((KEEP,) + matrices.shape[1:], BF16)],
        [HBM],
        [VMEM],
        [pltpu.SemaphoreType.DMA(())],
        touched=4000000,
        vmem=50,
    )(matrices)
    answer, chosen = call(
        physics_first,
        [answer_shape, chosen_shape],
        [VMEM, VMEM, HBM],
        [VMEM] * 2,
        spaces,
        vmem=50,
    )(exchange(outbox), kept, matrices)
    returned = exchange(answer)

    def add(kernel, returned, base, aliases, edge_type):
        return call(
            functools.partial(kernel, tail=tail),
            [shape(planes, F32)] + [shape((fields + 1, span_lon, LANES), edge_type)] * 4,
            [SMEM] + [VMEM] * 2,
            [VMEM] * 5,
            [VMEM(rows_shape, F32)],
            aliases,
        )(plan, returned, base)

    field, *edges = add(add_first, returned, late, {}, F32)
    neighbours = halos(*edges)
    (inner,) = call(inner_first, [shape(planes, F32)], [VMEM] * 3, [VMEM], touched=6000000)(field, coef, early)
    adjoint, outbox = call(
        functools.partial(edges_first, tail=tail),
        [shape(planes, F32), outbox_shape],
        [SMEM] + [VMEM] * 6,
        [VMEM] * 2,
        [VMEM(rows_shape, F32)],
        {1: 0},
    )(plan, inner, coef, *neighbours)
    (answer,) = call(physics_second, [answer_shape], [VMEM, VMEM, HBM, VMEM], [VMEM], spaces, vmem=50)(
        exchange(outbox), kept, matrices, chosen
    )
    field, *edges = add(add_increments, exchange(answer), adjoint, {2: 0}, BF16)
    neighbours = halos(*edges)
    (inner,) = call(inner_last, [shape(planes, F32)], [VMEM] * 2, [VMEM], touched=6000000)(field, coef)
    final, _ = call(
        edges_last,
        [shape(grid, F32), shape(planes, F32)],
        [VMEM] * 6,
        [HBM, VMEM],
        [VMEM(grid, F32), pltpu.SemaphoreType.DMA((fields,))],
        {0: 1},
    )(inner, coef, *neighbours)
    return final.reshape(fields, span_lon, span_lat, levels).transpose(0, 3, 1, 2)


def solution(mesh):
    return jax.shard_map(
        on_device,
        mesh=mesh,
        in_specs=(
            P(None, None, "gx", "gy"),
            P(None, None, "gx", "gy"),
            P(None, "gx", "gy"),
            P("gx", "gy", None, None, None),
            P("gx", "gy", None),
            P("gx", "gy"),
            P("gx", "gy", None),
            P("gx", "gy", None),
        ),
        out_specs=P(None, None, "gx", "gy"),
        check_vma=False,
    )
```
